512 devices in a mesh: tile: 128 (over y, z, core), seg: 4 (over x).
Axes of the slice: x: 4, y: 8, z: 8, core: 2. Of those that a mesh axis runs over, the one named last changes fastest.
Arguments:
- coords: float32 [3, 524288], P(None, ('tile', 'seg')), may hold values from 8 to 16
- weights: float32 [524288], P(('tile', 'seg')), may hold values from 0.5 to 4
- mode_vectors: bfloat16 [256, 3, 524288], P(None, None, ('tile', 'seg')), may hold values from -0.375 to 0.375
- amplitudes: float32 [256], replicated, may hold values from -4 to 4
- density_map: bfloat16 [128, 32768], P('tile'), may hold values from 0 to 2
- block_tiles: int32 [16384, 4], P(('tile', 'seg')), may hold values from 0 to 127, all different within a row; in each aligned block of 32 rows (0 to 31, 32 to 63, ...) at most 2 rows name the same one
- block_offsets: int32 [16384, 4, 3], P(('tile', 'seg')), may hold values from 0 to 16
Outputs:
- forces: float32 [3, 524288], P(None, ('tile', 'seg'))
- mode_grad: float32 [256], replicated
- correlation: float32 [], replicated
The draws below stay inside these ranges and needn't reach their ends.
Inputs may be any that keep to these rules, and one draw needn't show every extreme that they name: `block_tiles`: the 4 tiles of a row differ; among the 32 rows of one device no tile is named more than 2 times.
All inputs are finite; a program needn't handle non-finite values.
Results may differ from the reference program's by a relative error of at most 0.0044.
Values may be sent and summed in bfloat16 or wider, within the bound.
No kernel may reach another device: no remote copies, remote signals or barrier semaphores. Data moves between devices by JAX's collectives and lax.ppermute only.
A program may use at most 64 MiB of HBM per device.

```python
import math
import jax
import jax.numpy as jnp
import numpy as np
from jax import lax

EDGE = 32
MODES = 256
ATOM_BLOCK = 32
MARGIN = 4
BLK_DEV = 32
MOST = 2
TILES = 128
BLOCKS = 16384
ATOMS = 524288
VOXELS = 4194304


def touch_ends(result, key, low, top_value):
    extent = result.shape
    spot = [jax.random.randint(jax.random.fold_in(key, axis), (), 0, extent[axis]) for axis in range(len(extent))]
    result = result.at[tuple(spot)].set(low)
    longest = extent.index(max(extent))
    spot[longest] = (spot[longest] + 1) % extent[longest]
    return result.at[tuple(spot)].set(top_value)


def block_levels(rng, extent, split, low, top_value):
    def one(position, blocks):
        draws = jax.random.uniform(jax.random.fold_in(jax.random.fold_in(rng, 6), position), (blocks,), jnp.float32, low / len(split), top_value / len(split))
        return jnp.repeat(jnp.exp(draws), extent[position] // blocks).reshape((-1,) + (1,) * (len(extent) - position - 1))

    gain = one(*split[0])
    for cut in split[1:]:
        gain = gain * one(*cut)
    return gain


def deal_out(key, own, number, rows, count, top, limit, lean):
    ranking = jax.random.permutation(key, count)
    crowded, usual = portions_of(count, rows * top, limit, lean, True), portions_of(count, rows * top, limit, lean, False)
    places = jnp.arange(count)

    def named(lengths, turn):
        used = int((lengths > 0).sum())
        fixed = max(1, used // 4)
        moved = fixed + (places - fixed + turn * (used - fixed)) % max(1, count - fixed)
        return jnp.zeros((count,), jnp.int32).at[ranking[jnp.where(places < fixed, places, moved)]].set(jnp.asarray(lengths, jnp.int32))

    lengths = jnp.where(number % 4 == 0, named(crowded, number // 4), named(usual, number - number // 4 - 1))
    mixed = jax.random.permutation(jax.random.fold_in(own, 3), count)
    source_of, sink = mixed[0:count // 2 * 2:2], mixed[1:count // 2 * 2:2]
    slack = jnp.minimum(lengths[source_of] - 1, limit - lengths[sink]) // 2
    slack = jnp.where((source_of == ranking[0]) | (sink == ranking[0]) | (lengths[sink] == 0), 0, jnp.maximum(slack, 0))
    moved = jax.random.randint(jax.random.fold_in(own, 4), (count // 2,), 0, 1 << 20) % (slack + 1)
    lengths = lengths.at[source_of].add(-moved).at[sink].add(moved)
    labels = jnp.searchsorted(jnp.cumsum(lengths), jnp.arange(rows * top), side="right").astype(jnp.int32)
    grid = labels.reshape(top, rows).T
    grid = grid[jax.random.permutation(jax.random.fold_in(own, 1), rows)]
    turn = jax.random.randint(jax.random.fold_in(own, 2), (rows, 1), 0, top)
    return jnp.take_along_axis(grid, (jnp.arange(top)[None, :] + turn) % top, axis=1)


def portions_of(number_of, total, limit, lean, full):
    loads = [(1 << 20) // math.isqrt(grade ** lean) + 1 for grade in range(1, number_of + 1)]
    largest = limit if full else min(limit, max(-(-total // number_of), total * loads[0] // sum(loads)))
    least = 1 if total - largest >= number_of - 1 else 0
    holding, rest = [largest] + [least] * (number_of - 1), total - largest - least * (number_of - 1)
    while rest > 0:
        movable = [i for i in range(1, number_of) if holding[i] < largest] or [i for i in range(1, number_of) if holding[i] < limit]
        mass, left = sum([loads[i] for i in movable]), rest
        for i in movable:
            extra = min(limit - holding[i], max(1, left * loads[i] // mass), rest)
            holding[i] = holding[i] + extra
            rest = rest - extra
    return np.array(holding)


def centred(rng, shape, spread, most, split=(), kind=jnp.bfloat16):
    result = spread * jax.random.normal(rng, shape, jnp.float32)
    if split:
        result = result * block_levels(rng, shape, split, -0.22, 0.18)
    return jnp.clip(result, -most, most).astype(kind)


def setup_inputs(seed: int = 0) -> dict:
    key_list = jax.random.split(jax.random.key(seed), 8)
    coords = jnp.clip(8.0 + 8.0 * jax.random.uniform(key_list[0], (3, ATOMS), jnp.float32) ** block_levels(key_list[0], (3, ATOMS), ((1, 512),), -0.2, 0.2), 8.0, 16.0)
    weights = jnp.clip(jnp.exp(math.log(4.0) - 2.0794415 * jax.random.uniform(key_list[1], (ATOMS,), jnp.float32) ** block_levels(key_list[1], (ATOMS,), ((0, 512),), -0.2, 0.2)), 0.5, 4.0)
    mode_vectors = centred(key_list[2], (MODES, 3, ATOMS), MODES ** -0.5, 0.375, ((2, 512),))
    amplitudes = centred(key_list[3], (MODES,), 1.0, 4.0, (), jnp.float32)
    density_map = jnp.clip(2.0 * jax.random.uniform(key_list[4], (TILES, EDGE ** 3), jnp.float32) ** block_levels(key_list[4], (TILES, EDGE ** 3), ((0, 128),), -0.2, 0.2), 0.0, 2.0).astype(jnp.bfloat16)
    block_tiles_keys = jax.random.split(jax.random.fold_in(key_list[5], 1), BLOCKS // BLK_DEV)
    block_tiles_turns = jax.random.permutation(jax.random.fold_in(key_list[5], 3), BLOCKS // BLK_DEV)
    block_tiles = jax.vmap(lambda own, number: deal_out(jax.random.fold_in(key_list[5], 2), own, number, BLK_DEV, TILES, MARGIN, MOST, 2))(block_tiles_keys, block_tiles_turns).reshape((BLOCKS, MARGIN))
    block_offsets = touch_ends(jax.random.randint(key_list[6], (BLOCKS, MARGIN, 3), 0, EDGE // 2 + 1), jax.random.fold_in(key_list[6], 1), 0, (EDGE // 2 + 1) - 1).astype(jnp.int32)
    return dict(coords=coords, weights=weights, mode_vectors=mode_vectors, amplitudes=amplitudes, density_map=density_map, block_tiles=block_tiles, block_offsets=block_offsets)


inverse_var = 1.0 / 2.25

def factors(frame_pos, edge_len):
    centers = jnp.arange(edge_len, dtype=jnp.float32) + 0.5
    distance = centers[None, :, None] - frame_pos[:, None, :]
    profile = jnp.exp(-0.5 * inverse_var * distance * distance)
    slopes = inverse_var * distance * profile
    return (profile, slopes)

def splat_tile(frame_pos, masses, edge_len):
    profile, slopes = factors(frame_pos, edge_len)
    rounded = profile.astype(jnp.bfloat16)
    along_y = (masses[None, :] * profile[1]).astype(jnp.bfloat16)
    plane_kr = (rounded[2].astype(jnp.float32)[:, None, :] * rounded[0].astype(jnp.float32)[None, :, :]).astype(jnp.bfloat16)
    plane_kr = plane_kr.reshape(edge_len * edge_len, frame_pos.shape[1])
    return lax.dot_general(plane_kr, along_y, (((1,), (1,)), ((), ())), preferred_element_type=jnp.float32)

def backproject(frame_pos, masses, gradient, edge_len):
    profile, slopes = factors(frame_pos, edge_len)
    atom_count = frame_pos.shape[1]
    rounded = profile.astype(jnp.bfloat16)
    rounded_slopes = slopes.astype(jnp.bfloat16)
    y_factors = jnp.concatenate([(masses[None, :] * profile[1]).astype(jnp.bfloat16), (masses[None, :] * slopes[1]).astype(jnp.bfloat16)], axis=1)
    contracted = jnp.dot(gradient, y_factors, preferred_element_type=jnp.float32).astype(jnp.bfloat16)
    contracted = lax.optimization_barrier(contracted).astype(jnp.float32).reshape(edge_len, edge_len, 2 * atom_count)
    plain_sum = contracted[:, :, :atom_count]
    sloped = contracted[:, :, atom_count:]
    along_x = rounded[0].astype(jnp.float32)
    along_z = rounded[2].astype(jnp.float32)
    slope_x = rounded_slopes[0].astype(jnp.float32)
    slope_z = rounded_slopes[2].astype(jnp.float32)
    force_x = lax.optimization_barrier(jnp.sum(along_z * lax.optimization_barrier(jnp.sum(plain_sum * slope_x[None], axis=1)), axis=0))
    force_y = lax.optimization_barrier(jnp.sum(along_z * lax.optimization_barrier(jnp.sum(sloped * along_x[None], axis=1)), axis=0))
    force_z = lax.optimization_barrier(jnp.sum(slope_z * lax.optimization_barrier(jnp.sum(plain_sum * along_x[None], axis=1)), axis=0))
    return jnp.stack([force_x, force_y, force_z])

def gradient_of(density, target, totals, voxels):
    root = jnp.sqrt(totals[1] * totals[2])
    correlation = totals[0] / root
    return (voxels * (target / root - correlation * density / totals[1])).astype(jnp.bfloat16)

def reference(coords, weights, mode_vectors, amplitudes, density_map, block_tiles, block_offsets):
    flat_count = 3 * ATOMS
    modes_flat = mode_vectors.reshape(MODES, flat_count)
    displacement = jnp.dot(amplitudes.astype(jnp.bfloat16)[None, :], modes_flat, preferred_element_type=jnp.float32).reshape(3, ATOMS)
    positions = coords + displacement
    block_places = jnp.transpose(positions.reshape(3, BLOCKS, ATOM_BLOCK), (1, 0, 2))
    block_masses = weights.reshape(BLOCKS, ATOM_BLOCK)
    offsets = block_offsets.astype(jnp.float32)
    plane_rows = EDGE * EDGE
    zero_index = jnp.zeros((), jnp.int32)

    def add_block(density, block_item):
        block_place, masses, tile_ids, offset = block_item
        for column in range(MARGIN):
            frame_pos = block_place + offset[column][:, None]
            contribution = splat_tile(frame_pos, masses, EDGE)
            tile_index = tile_ids[column].astype(jnp.int32)
            current = lax.dynamic_slice(density, (tile_index, zero_index, zero_index), (1, plane_rows, EDGE))
            density = lax.dynamic_update_slice(density, current + contribution[None], (tile_index, zero_index, zero_index))
        return (density, None)
    density, _ = lax.scan(add_block, jnp.zeros((TILES, plane_rows, EDGE), jnp.float32), (block_places, block_masses, block_tiles, offsets))
    target = density_map.astype(jnp.float32).reshape(TILES, plane_rows, EDGE)
    totals = (jnp.sum(density * target), jnp.sum(density * density), jnp.sum(target * target))
    correlation = totals[0] / jnp.sqrt(totals[1] * totals[2])
    gradient = gradient_of(density, target, totals, VOXELS)

    def pull_block(block_item):
        block_place, masses, tile_ids, offset = block_item
        summed = jnp.zeros((3, ATOM_BLOCK), jnp.float32)
        for column in range(MARGIN):
            frame_pos = block_place + offset[column][:, None]
            tile_grad = lax.dynamic_index_in_dim(gradient, tile_ids[column].astype(jnp.int32), 0, keepdims=False)
            summed = summed + backproject(frame_pos, masses, tile_grad, EDGE)
        return summed
    pulled = lax.map(pull_block, (block_places, block_masses, block_tiles, offsets))
    forces = jnp.transpose(pulled, (1, 0, 2)).reshape(3, ATOMS)
    mode_grad = jnp.dot(modes_flat, forces.astype(jnp.bfloat16).reshape(flat_count), preferred_element_type=jnp.float32) / jnp.sqrt(jnp.float32(ATOMS))
    return (forces, mode_grad, correlation)
```

```python
import jax
import jax.numpy as jnp
from jax import lax
from jax.sharding import PartitionSpec as P

EDGE = 32
ATOM_BLOCK = 32


inverse_var = 1.0 / 2.25


def factors(frame_pos, edge_len):
    centers = jnp.arange(edge_len, dtype=jnp.float32) + 0.5
    distance = centers[None, :, None] - frame_pos[:, None, :]
    profile = jnp.exp(-0.5 * inverse_var * distance * distance)
    slopes = inverse_var * distance * profile
    return (profile, slopes)


def splat_tile(frame_pos, masses, edge_len):
    profile, slopes = factors(frame_pos, edge_len)
    rounded = profile.astype(jnp.bfloat16)
    along_y = (masses[None, :] * profile[1]).astype(jnp.bfloat16)
    plane_kr = (
        rounded[2].astype(jnp.float32)[:, None, :] * rounded[0].astype(jnp.float32)[None, :, :]
    ).astype(jnp.bfloat16)
    plane_kr = plane_kr.reshape(edge_len * edge_len, frame_pos.shape[1])
    return lax.dot_general(
        plane_kr, along_y, (((1,), (1,)), ((), ())), preferred_element_type=jnp.float32
    )


def backproject(frame_pos, masses, gradient, edge_len):
    profile, slopes = factors(frame_pos, edge_len)
    atom_count = frame_pos.shape[1]
    rounded = profile.astype(jnp.bfloat16)
    rounded_slopes = slopes.astype(jnp.bfloat16)
    y_factors = jnp.concatenate(
        [
            (masses[None, :] * profile[1]).astype(jnp.bfloat16),
            (masses[None, :] * slopes[1]).astype(jnp.bfloat16),
        ],
        axis=1,
    )
    contracted = jnp.dot(gradient, y_factors, preferred_element_type=jnp.float32).astype(
        jnp.bfloat16
    )
    contracted = (
        lax.optimization_barrier(contracted)
        .astype(jnp.float32)
        .reshape(edge_len, edge_len, 2 * atom_count)
    )
    plain_sum = contracted[:, :, :atom_count]
    sloped = contracted[:, :, atom_count:]
    along_x = rounded[0].astype(jnp.float32)
    along_z = rounded[2].astype(jnp.float32)
    slope_x = rounded_slopes[0].astype(jnp.float32)
    slope_z = rounded_slopes[2].astype(jnp.float32)
    force_x = jnp.sum(along_z * jnp.sum(plain_sum * slope_x[None], axis=1), axis=0)
    force_y = jnp.sum(along_z * jnp.sum(sloped * along_x[None], axis=1), axis=0)
    force_z = jnp.sum(slope_z * jnp.sum(plain_sum * along_x[None], axis=1), axis=0)
    return jnp.stack([force_x, force_y, force_z])


def gradient_of(density, target, totals, voxels):
    root = jnp.sqrt(totals[1] * totals[2])
    correlation = totals[0] / root
    return (voxels * (target / root - correlation * density / totals[1])).astype(jnp.bfloat16)


def swap_over(values, axis, mask):
    size = lax.axis_size(axis)
    return lax.ppermute(values, axis, [(i, i ^ mask) for i in range(size)])


def small_sum(values, axis):
    mask = 1
    while mask < lax.axis_size(axis):
        values = values + swap_over(values, axis, mask)
        mask *= 2
    return values


def ring_sum(values, axis):
    size = lax.axis_size(axis)
    step = [lax.ppermute(values, axis, [(i, (i + k) % size) for i in range(size)]) for k in (1, 2, 3)]
    return (values + step[1]) + (step[0] + step[2])


def on_device(coords, weights, mode_vectors, amplitudes, density_map, block_tiles, block_offsets):
    edge_len = EDGE
    atoms_per = ATOM_BLOCK
    a_dev = coords.shape[1]
    block_count = block_tiles.shape[0]
    per_block = block_tiles.shape[1]
    entry_count = block_count * per_block
    n_tile = lax.axis_size("tile")
    n_seg = lax.axis_size("seg")
    modes_flat = mode_vectors.reshape(mode_vectors.shape[0], 3 * a_dev)
    displacement = jnp.dot(
        amplitudes.astype(jnp.bfloat16)[None, :], modes_flat, preferred_element_type=jnp.float32
    ).reshape(3, a_dev)
    bundle = jnp.concatenate([coords + displacement, weights[None, :]], axis=0)
    tile_ids = block_tiles.reshape(entry_count)
    offsets_f = block_offsets.reshape(entry_count, 3).astype(jnp.float32)
    ordinal = jnp.arange(entry_count, dtype=jnp.int32)
    earlier = (ordinal[None, :] < ordinal[:, None]) & (tile_ids[None, :] == tile_ids[:, None])
    slot_of = 2 * tile_ids + jnp.sum(earlier.astype(jnp.int32), axis=1)
    chosen = (jnp.arange(2 * n_tile, dtype=jnp.int32)[:, None] == slot_of[None, :]).astype(
        jnp.float32
    )
    by_block = jnp.transpose(bundle.reshape(4, block_count, atoms_per), (1, 0, 2))
    shift = jnp.concatenate([offsets_f, jnp.zeros((entry_count, 1), jnp.float32)], axis=1)
    rows = jnp.repeat(by_block, per_block, axis=0) + shift[:, :, None]
    send = jnp.dot(chosen, rows.reshape(entry_count, 4 * atoms_per), precision=lax.Precision.HIGHEST)
    got = lax.all_to_all(
        send.reshape(n_tile, 2, 4 * atoms_per), "tile", split_axis=0, concat_axis=0, tiled=True
    )
    slot_count = 2 * n_tile
    group_slots = 32
    groups = slot_count // group_slots
    grouped = jnp.transpose(
        got.reshape(groups, group_slots, 4, atoms_per), (0, 2, 1, 3)
    ).reshape(groups, 4, group_slots * atoms_per)

    def add_group(density, group_rows):
        return (density + splat_tile(group_rows[:3], group_rows[3], edge_len), None)

    partial_density, _ = lax.scan(
        add_group, jnp.zeros((edge_len * edge_len, edge_len), jnp.float32), grouped
    )
    target = density_map.reshape(edge_len * edge_len // 4, edge_len * 4).astype(jnp.float32)
    voxels = float(n_tile * edge_len**3)
    density = ring_sum(partial_density.reshape(edge_len * edge_len // 4, edge_len * 4), "seg")
    totals = small_sum(
        jnp.stack([jnp.sum(density * target), jnp.sum(density * density), jnp.sum(target * target)]),
        "tile",
    )
    gradient = gradient_of(density, target, totals, voxels).reshape(edge_len * edge_len, edge_len)
    correlation = totals[0] / jnp.sqrt(totals[1] * totals[2])

    def pull_group(group_rows):
        return backproject(group_rows[:3], group_rows[3], gradient, edge_len)

    pulled = lax.map(pull_group, grouped)
    pulled = jnp.transpose(
        pulled.reshape(groups, 3, group_slots, atoms_per), (0, 2, 1, 3)
    ).reshape(n_tile, 2, 3 * atoms_per)
    back = lax.all_to_all(pulled, "tile", split_axis=0, concat_axis=0, tiled=True)
    per_entry = jnp.dot(
        chosen.T, back.reshape(slot_count, 3 * atoms_per), precision=lax.Precision.HIGHEST
    )
    forces = jnp.sum(per_entry.reshape(block_count, per_block, 3, atoms_per), axis=1)
    forces = jnp.transpose(forces, (1, 0, 2)).reshape(3, a_dev)
    partial_modes = jnp.dot(
        modes_flat,
        forces.astype(jnp.bfloat16).reshape(3 * a_dev),
        preferred_element_type=jnp.float32,
    )
    total_atoms = a_dev * n_tile * n_seg
    partial_modes = ring_sum(partial_modes.reshape(2, 128), "seg")
    every = lax.all_to_all(
        jnp.broadcast_to(partial_modes[None], (n_tile, 2, 128)),
        "tile",
        split_axis=0,
        concat_axis=0,
        tiled=True,
    )
    mode_grad = jnp.sum(every, axis=0).reshape(-1) / jnp.sqrt(jnp.float32(total_atoms))
    return (forces, mode_grad, correlation)


def solution(mesh):
    return jax.shard_map(
        on_device,
        mesh=mesh,
        in_specs=(
            P(None, ("tile", "seg")),
            P(("tile", "seg")),
            P(None, None, ("tile", "seg")),
            P(),
            P("tile", None),
            P(("tile", "seg"), None),
            P(("tile", "seg"), None, None),
        ),
        out_specs=(P(None, ("tile", "seg")), P(), P()),
        check_vma=False,
    )
```

```python
import jax
import jax.numpy as jnp
from jax import lax
from jax.experimental import pallas as pl
from jax.experimental.pallas import tpu as pltpu
from jax.sharding import Mesh
from jax.sharding import PartitionSpec as P

EDGE = 32
ATOM_BLOCK = 32
PLANE = EDGE * EDGE
LANES = 128
CHUNK = 256

inverse_var = 1.0 / 2.25


def factors(places):
    centers = lax.broadcasted_iota(jnp.int32, (EDGE, places.shape[1]), 0).astype(jnp.float32) + 0.5
    distance = centers - places
    profile = jnp.exp(-0.5 * inverse_var * distance * distance)
    return profile, inverse_var * distance * profile


def unpack_rows(got_ref, place_ref):
    pairs = got_ref.shape[0] // 4
    left = lax.broadcasted_iota(jnp.int32, (pairs, LANES), 1) < LANES // 2
    for part in range(2):
        even = got_ref[pl.ds(part, pairs, stride=4), :]
        odd = got_ref[pl.ds(2 + part, pairs, stride=4), :]
        place_ref[2 * part] = jnp.where(left, even, pltpu.roll(odd, LANES // 2, 1))
        place_ref[2 * part + 1] = jnp.where(left, pltpu.roll(even, LANES // 2, 1), odd)


def chunk_row(place_ref, component, start):
    rows = CHUNK // LANES
    return jnp.concatenate([place_ref[component, pl.ds(start + i, 1), :] for i in range(rows)], axis=1)


def splat_kernel(got_ref, out_ref, place_ref, line_ref, plane_ref):
    unpack_rows(got_ref, place_ref)
    per = plane_ref.shape[0]
    rows = CHUNK // LANES
    out_ref[0] = jnp.zeros_like(out_ref[0])

    @pl.loop(0, place_ref.shape[1] // (rows * per))
    def _(step):
        for part in range(per):
            start = (step * per + part) * rows
            along_x = factors(chunk_row(place_ref, 0, start))[0].astype(jnp.bfloat16)
            along_y = factors(chunk_row(place_ref, 1, start))[0]
            along_z = factors(chunk_row(place_ref, 2, start))[0]
            masses = chunk_row(place_ref, 3, start)
            along_y = (masses * along_y).astype(jnp.bfloat16)
            line_ref[part] = along_z.astype(jnp.bfloat16).astype(jnp.float32)
            for z in range(EDGE):
                line = jnp.broadcast_to(line_ref[part, pl.ds(z, 1), :], (EDGE, CHUNK))
                plane_ref[part, pl.ds(z * EDGE, EDGE), :] = line.astype(jnp.bfloat16) * along_x
            out_ref[0] += lax.dot_general(
                along_y,
                plane_ref[part],
                (((1,), (1,)), ((), ())),
                preferred_element_type=jnp.float32,
            )

    for copy in range(1, out_ref.shape[0]):
        out_ref[copy] = out_ref[0]


def pull_kernel(got_ref, parts_ref, target_ref, out_ref, place_ref, line_ref, plane_ref, row_ref, sum_ref):
    unpack_rows(got_ref, place_ref)
    per = plane_ref.shape[0]
    rows = CHUNK // LANES
    target = target_ref[...]
    density = (parts_ref[0] + parts_ref[2]) + (parts_ref[1] + parts_ref[3])
    wide = target.astype(jnp.float32)
    high = density.astype(jnp.bfloat16)
    rest = density - high.astype(jnp.float32)
    middle = rest.astype(jnp.bfloat16)
    low = (rest - middle.astype(jnp.float32)).astype(jnp.bfloat16)
    row_ref[0:EDGE] = target
    row_ref[EDGE : 2 * EDGE] = high
    row_ref[2 * EDGE : 3 * EDGE] = middle
    row_ref[3 * EDGE : 4 * EDGE] = low

    @pl.loop(0, place_ref.shape[1] // (rows * per))
    def _(step):
        for part in range(per):
            start = (step * per + part) * rows
            profile_x, slope_x = factors(chunk_row(place_ref, 0, start))
            profile_y, slope_y = factors(chunk_row(place_ref, 1, start))
            profile_z, slope_z = factors(chunk_row(place_ref, 2, start))
            masses = chunk_row(place_ref, 3, start)
            profile_x = profile_x.astype(jnp.bfloat16)
            slope_x = slope_x.astype(jnp.bfloat16)
            along_y = (masses * profile_y).astype(jnp.bfloat16).astype(jnp.float32)
            slope_y = (masses * slope_y).astype(jnp.bfloat16).astype(jnp.float32)
            line_ref[part, 0] = profile_z.astype(jnp.bfloat16).astype(jnp.float32)
            line_ref[part, 1] = slope_z.astype(jnp.bfloat16).astype(jnp.float32)
            for z in range(EDGE):
                line = jnp.broadcast_to(line_ref[part, 0, pl.ds(z, 1), :], (EDGE, CHUNK))
                slope_line = jnp.broadcast_to(line_ref[part, 1, pl.ds(z, 1), :], (EDGE, CHUNK))
                line = line.astype(jnp.bfloat16)
                slope_line = slope_line.astype(jnp.bfloat16)
                place = pl.ds(z * EDGE, EDGE)
                plane_ref[part, place, pl.ds(0, CHUNK)] = line * slope_x
                plane_ref[part, place, pl.ds(CHUNK, CHUNK)] = line * profile_x
                plane_ref[part, place, pl.ds(2 * CHUNK, CHUNK)] = slope_line * profile_x
            for component, weight in enumerate((along_y, slope_y, along_y)):
                pulled = jnp.dot(
                    row_ref[...],
                    plane_ref[part, :, pl.ds(component * CHUNK, CHUNK)],
                    preferred_element_type=jnp.float32,
                )
                model = (pulled[EDGE : 2 * EDGE] + pulled[2 * EDGE : 3 * EDGE]) + pulled[3 * EDGE :]
                sums = (
                    jnp.sum(pulled[:EDGE] * weight, axis=0, keepdims=True),
                    jnp.sum(model * weight, axis=0, keepdims=True),
                )
                for kind in range(2):
                    for i in range(rows):
                        sum_ref[kind, component, pl.ds(start + i, 1), :] = sums[kind][
                            :, i * LANES : (i + 1) * LANES
                        ]

    pairs = place_ref.shape[1]
    left = lax.broadcasted_iota(jnp.int32, (pairs, LANES), 1) < LANES // 2
    for component in range(3):
        first, second = sum_ref[0, component], sum_ref[1, component]
        out_ref[pl.ds(component, pairs, stride=8), :] = jnp.where(
            left, first, pltpu.roll(second, LANES // 2, 1)
        )
        out_ref[pl.ds(4 + component, pairs, stride=8), :] = jnp.where(
            left, pltpu.roll(first, LANES // 2, 1), second
        )
    lane = lax.broadcasted_iota(jnp.int32, (2 * pairs, LANES), 1)
    totals = jnp.zeros((2 * pairs, LANES), jnp.float32)
    for place, product in enumerate((density * wide, density * density, wide * wide)):
        totals = jnp.where(lane == place, jnp.sum(product), totals)
    out_ref[pl.ds(3, 2 * pairs, stride=4), :] = totals


def splat(got, copies):
    pairs = got.shape[0] // 4
    return pl.pallas_call(
        splat_kernel,
        out_shape=jax.ShapeDtypeStruct((copies, EDGE, PLANE), jnp.float32),
        in_specs=[pl.BlockSpec(memory_space=pltpu.VMEM)],
        out_specs=pl.BlockSpec(memory_space=pltpu.VMEM),
        scratch_shapes=[
            pltpu.VMEM((4, pairs, LANES), jnp.float32),
            pltpu.VMEM((2, EDGE, CHUNK), jnp.float32),
            pltpu.VMEM((2, PLANE, CHUNK), jnp.bfloat16),
        ],
        compiler_params=pltpu.CompilerParams(vmem_limit_bytes=32 * 2**20),
        cost_estimate=pl.CostEstimate(flops=2**29, bytes_accessed=2**20, transcendentals=2**20),
        name="splat",
    )(got)


def pull(got, parts, target):
    pairs = got.shape[0] // 4
    return pl.pallas_call(
        pull_kernel,
        out_shape=jax.ShapeDtypeStruct((8 * pairs, LANES), jnp.float32),
        in_specs=[pl.BlockSpec(memory_space=pltpu.VMEM)] * 3,
        out_specs=pl.BlockSpec(memory_space=pltpu.VMEM),
        scratch_shapes=[
            pltpu.VMEM((4, pairs, LANES), jnp.float32),
            pltpu.VMEM((2, 2, EDGE, CHUNK), jnp.float32),
            pltpu.VMEM((2, PLANE, 3 * CHUNK), jnp.bfloat16),
            pltpu.VMEM((4 * EDGE, PLANE), jnp.bfloat16),
            pltpu.VMEM((2, 3, pairs, LANES), jnp.float32),
        ],
        compiler_params=pltpu.CompilerParams(vmem_limit_bytes=32 * 2**20),
        cost_estimate=pl.CostEstimate(flops=2**32, bytes_accessed=2**20, transcendentals=2**20),
        name="pull",
    )(got, parts, target)


TILE_AXES = ("y", "z", "core")


def exchange(values, axes):
    return lax.all_to_all(values, axes, split_axis=0, concat_axis=0, tiled=True)


def sum_over(values, axes):
    copies = jnp.broadcast_to(values[None], (lax.axis_size(axes),) + values.shape)
    return jnp.sum(exchange(copies, axes), axis=0)


def on_device(coords, weights, mode_vectors, amplitudes, density_map, block_tiles, block_offsets):
    atoms_per = ATOM_BLOCK
    a_dev = coords.shape[1]
    block_count, per_block = block_tiles.shape
    entry_count = block_count * per_block
    n_tile = lax.axis_size(TILE_AXES)
    n_seg = lax.axis_size("seg")
    modes_flat = mode_vectors.reshape(mode_vectors.shape[0], 3 * a_dev)
    displacement = jnp.dot(
        amplitudes.astype(jnp.bfloat16)[None, :], modes_flat, preferred_element_type=jnp.float32
    ).reshape(3, a_dev)
    bundle = jnp.concatenate([coords + displacement, weights[None, :]], axis=0)
    tile_ids = block_tiles.reshape(entry_count)
    offsets_f = block_offsets.reshape(entry_count, 3).astype(jnp.float32)
    ordinal = jnp.arange(entry_count, dtype=jnp.int32)
    earlier = (ordinal[None, :] < ordinal[:, None]) & (tile_ids[None, :] == tile_ids[:, None])
    rank = jnp.sum(earlier.astype(jnp.int32), axis=1)
    tiles = jnp.arange(n_tile, dtype=jnp.int32)
    chosen = (
        (tile_ids[None, None, :] == tiles[None, :, None])
        & (rank[None, None, :] == jnp.arange(2, dtype=jnp.int32)[:, None, None])
    ).astype(jnp.float32)
    by_block = jnp.transpose(bundle.reshape(4, block_count, atoms_per), (1, 0, 2))
    shift = jnp.concatenate([offsets_f, jnp.zeros((entry_count, 1), jnp.float32)], axis=1)
    rows = jnp.repeat(by_block, per_block, axis=0) + shift[:, :, None]
    send = jnp.einsum("rte,eca->tcra", chosen, rows, precision=lax.Precision.HIGHEST)
    got = exchange(send.reshape(n_tile, 2, LANES), TILE_AXES).reshape(2 * n_tile, LANES)

    target = jnp.transpose(density_map.reshape(PLANE, EDGE))
    parts = exchange(splat(got, n_seg), "seg")
    pulled = pull(got, parts, target)
    back = exchange(pulled.reshape(n_tile, 4, LANES), TILE_AXES)

    voxels = float(n_tile * EDGE**3)
    totals = jnp.sum(back[:, 3, :3], axis=0)
    root = jnp.sqrt(totals[1] * totals[2])
    correlation = totals[0] / root
    half = LANES // 2
    slot_forces = voxels * (
        back[:, :3, :half] / root - correlation * back[:, :3, half:] / totals[1]
    ).reshape(n_tile, 3, 2, atoms_per)
    to_block = jnp.sum(chosen.reshape(2, n_tile, block_count, per_block), axis=3)
    forces = jnp.einsum(
        "rtb,tcra->cba", to_block, slot_forces, precision=lax.Precision.HIGHEST
    ).reshape(3, a_dev)
    partial_modes = jnp.dot(
        modes_flat,
        forces.astype(jnp.bfloat16).reshape(3 * a_dev),
        preferred_element_type=jnp.float32,
    )
    total_atoms = a_dev * n_tile * n_seg
    mode_sum = sum_over(sum_over(partial_modes.reshape(2, LANES), ("z", "core")), ("y", "seg"))
    mode_grad = mode_sum.reshape(-1) / jnp.sqrt(jnp.float32(total_atoms))
    return (forces, mode_grad, correlation)


def solution(mesh):
    split = Mesh(mesh.devices.reshape(8, 8, 2, 4), TILE_AXES + ("seg",))
    every = TILE_AXES + ("seg",)
    return jax.shard_map(
        on_device,
        mesh=split,
        in_specs=(
            P(None, every),
            P(every),
            P(None, None, every),
            P(),
            P(TILE_AXES, None),
            P(every, None),
            P(every, None, None),
        ),
        out_specs=(P(None, every), P(), P()),
        check_vma=False,
    )
```

```python
import jax
import jax.numpy as jnp
from jax import lax
from jax.experimental import pallas as pl
from jax.experimental.pallas import tpu as pltpu
from jax.sharding import Mesh
from jax.sharding import PartitionSpec as P

EDGE = 32
ATOM_BLOCK = 32
PLANE = EDGE * EDGE
LANES = 128
CHUNK = 256

inverse_var = 1.0 / 2.25


def factors(places):
    centers = lax.broadcasted_iota(jnp.int32, (EDGE, places.shape[1]), 0).astype(jnp.float32) + 0.5
    distance = centers - places
    profile = jnp.exp(-0.5 * inverse_var * distance * distance)
    return profile, inverse_var * distance * profile


def exact_parts(values):
    high = values.astype(jnp.bfloat16)
    rest = values - high.astype(jnp.float32)
    middle = rest.astype(jnp.bfloat16)
    return high, middle, (rest - middle.astype(jnp.float32)).astype(jnp.bfloat16)


def against_rows(left, right):
    return lax.dot_general(
        left, right, (((1,), (1,)), ((), ())), preferred_element_type=jnp.float32
    )


def quarter_of(shape):
    return lax.broadcasted_iota(jnp.int32, shape, 1) // ATOM_BLOCK


def regroup(rows, target):
    quarter = quarter_of(rows[0].shape)
    result = jnp.zeros_like(rows[0])
    for i in range(4):
        moved = pltpu.roll(rows[i], ((i - target) % 4) * ATOM_BLOCK, 1) if i != target else rows[i]
        result = jnp.where(quarter == i, moved, result)
    return result


def pack_kernel(*refs):
    sources, (send_ref, pick_ref), (cell_ref, block_ref) = refs[:6], refs[6:8], refs[8:10]
    local, sems = refs[10:16], refs[16]
    copies = [
        pltpu.make_async_copy(source, place, sems.at[i])
        for i, (source, place) in enumerate(zip(sources, local))
    ]
    for copy in copies:
        copy.start()
    tiles_ref, offsets_ref, amps_ref, coords_ref, weights_ref, modes_ref = local
    n_tile = send_ref.shape[0] // 2
    blocks = block_ref.shape[0]
    cells = cell_ref.shape[1]
    for copy in copies[:2]:
        copy.wait()
    shape = (n_tile, blocks)
    tile_of_row = lax.broadcasted_iota(jnp.int32, shape, 0)
    row = lax.broadcasted_iota(jnp.int32, (blocks, blocks), 0)
    column = lax.broadcasted_iota(jnp.int32, (blocks, blocks), 1)
    before = jnp.where(row < column, 1.0, 0.0).astype(jnp.bfloat16)
    same = jnp.where(row == column, 1.0, 0.0).astype(jnp.bfloat16)
    ones = jnp.ones((blocks, blocks), jnp.bfloat16)
    seen = jnp.zeros(shape, jnp.float32)
    picks = [jnp.zeros(shape, jnp.float32) for _ in range(2)]
    shifts = [jnp.zeros((n_tile, LANES), jnp.float32) for _ in range(2)]
    for k in range(tiles_ref.shape[0]):
        named = jnp.where(tiles_ref[pl.ds(k, 1), :] == tile_of_row, 1.0, 0.0)
        flags = named.astype(jnp.bfloat16)
        rank = seen + jnp.dot(flags, before, preferred_element_type=jnp.float32)
        seen = seen + jnp.dot(flags, ones, preferred_element_type=jnp.float32)
        offsets = [
            jnp.broadcast_to(offsets_ref[c, pl.ds(k, 1), :].astype(jnp.float32), (ATOM_BLOCK, blocks))
            for c in range(3)
        ]
        offsets = jnp.concatenate(offsets + [jnp.zeros((ATOM_BLOCK, blocks), jnp.float32)], axis=0)
        for slot in range(2):
            mine = jnp.where(rank == float(slot), named, 0.0)
            picks[slot] = picks[slot] + mine
            shifts[slot] = shifts[slot] + against_rows(
                mine.astype(jnp.bfloat16), offsets.astype(jnp.bfloat16)
            )
    for copy in copies[2:]:
        copy.wait()
    amps = jnp.broadcast_to(amps_ref[...], (16, amps_ref.shape[1])).astype(jnp.bfloat16)
    for component in range(3):
        moved = jnp.dot(amps, modes_ref[component], preferred_element_type=jnp.float32)
        places = coords_ref[pl.ds(component, 1), :] + moved[0:1]
        for cell in range(cells):
            cell_ref[component, pl.ds(cell, 1), :] = places[:, cell * LANES : (cell + 1) * LANES]
    cell_ref[3] = weights_ref[...]
    for i in range(4):
        block_ref[pl.ds(i, cells, stride=4), :] = regroup([cell_ref[c] for c in range(4)], i)
    parts = exact_parts(block_ref[...])
    for slot in range(2):
        pick = picks[slot].astype(jnp.bfloat16)
        high, middle, low = [jnp.dot(pick, part, preferred_element_type=jnp.float32) for part in parts]
        send_ref[pl.ds(slot, n_tile, stride=2), :] = ((high + middle) + low) + shifts[slot]
        pick_ref[slot] = against_rows(same, pick).astype(jnp.bfloat16)


def finish_kernel(voxels, atoms, back_ref, pick_ref, modes_ref, forces_ref, spread_ref, score_ref, block_ref):
    n_tile = pick_ref.shape[2]
    lane = lax.broadcasted_iota(jnp.int32, (1, LANES), 1)
    totals = jnp.sum(back_ref[pl.ds(3, n_tile, stride=4), :], axis=0, keepdims=True)
    srm, srr, smm = [
        jnp.sum(jnp.where(lane == i, totals, 0.0), axis=1, keepdims=True) for i in range(3)
    ]
    root = jnp.sqrt(srr * smm)
    score = srm / root
    score_ref[...] = jnp.broadcast_to(score, score_ref.shape)
    map_scale = voxels / root
    model_scale = voxels * (score / srr)
    cells = forces_ref.shape[1] // LANES
    modes = jnp.zeros((1, modes_ref.shape[1]), jnp.float32)
    for component in range(3):
        pulled = back_ref[pl.ds(component, n_tile, stride=4), :]
        pulled = pulled * map_scale - pltpu.roll(pulled, LANES // 2, 1) * model_scale
        parts = exact_parts(pulled)
        first, second = [
            sum([jnp.dot(pick_ref[slot], part, preferred_element_type=jnp.float32) for part in parts[::-1]])
            for slot in range(2)
        ]
        block_ref[component] = first + pltpu.roll(second, LANES - ATOM_BLOCK, 1)
        rows = regroup([block_ref[component, pl.ds(i, cells, stride=4), :] for i in range(4)], 0)
        for cell in range(cells):
            forces_ref[pl.ds(component, 1), cell * LANES : (cell + 1) * LANES] = rows[cell : cell + 1]
        force = jnp.broadcast_to(forces_ref[pl.ds(component, 1), :], (16, forces_ref.shape[1]))
        modes = modes + against_rows(force.astype(jnp.bfloat16), modes_ref[component])[0:1]
    modes = modes / jnp.sqrt(jnp.float32(atoms))
    half = spread_ref.shape[0] // 2
    for part in range(2):
        spread_ref[pl.ds(part, half, stride=2), :] = jnp.broadcast_to(
            modes[:, part * LANES : (part + 1) * LANES], (half, LANES)
        )


def unpack_rows(got_ref, place_ref):
    groups = got_ref.shape[0] // 4
    rows = [got_ref[pl.ds(i, groups, stride=4), :] for i in range(4)]
    for component in range(4):
        place_ref[component] = regroup(rows, component)


def chunk_row(place_ref, component, chunk):
    rows = CHUNK // LANES
    return jnp.concatenate(
        [place_ref[component, pl.ds(chunk * rows + i, 1), :] for i in range(rows)], axis=1
    )


def pipeline(chunks, build, use):
    build(0, 0)

    @pl.loop(0, chunks // 2)
    def _(step):
        build(1, 2 * step + 1)
        use(0, 2 * step)
        build(0, jnp.minimum(2 * step + 2, chunks - 1))
        use(1, 2 * step + 1)


def splat_kernel(got_ref, out_ref, place_ref, line_ref, weight_ref, plane_ref):
    unpack_rows(got_ref, place_ref)
    out_ref[0] = jnp.zeros_like(out_ref[0])

    def build(slot, chunk):
        along_x = factors(chunk_row(place_ref, 0, chunk))[0].astype(jnp.bfloat16)
        along_y = factors(chunk_row(place_ref, 1, chunk))[0]
        along_z = factors(chunk_row(place_ref, 2, chunk))[0]
        weight_ref[slot] = (chunk_row(place_ref, 3, chunk) * along_y).astype(jnp.bfloat16)
        line_ref[slot] = along_z.astype(jnp.bfloat16).astype(jnp.float32)
        for z in range(EDGE):
            line = jnp.broadcast_to(line_ref[slot, pl.ds(z, 1), :], (EDGE, CHUNK))
            plane_ref[slot, pl.ds(z * EDGE, EDGE), :] = line.astype(jnp.bfloat16) * along_x

    def use(slot, chunk):
        out_ref[0] += against_rows(weight_ref[slot], plane_ref[slot])

    pipeline(place_ref.shape[1] * LANES // CHUNK, build, use)
    for copy in range(1, out_ref.shape[0]):
        out_ref[copy] = out_ref[0]


def pull_kernel(got_ref, parts_ref, target_ref, out_ref, place_ref, line_ref, weight_ref, plane_ref, row_ref, sum_ref):
    unpack_rows(got_ref, place_ref)
    target = target_ref[...]
    density = (parts_ref[0] + parts_ref[2]) + (parts_ref[1] + parts_ref[3])
    wide = target.astype(jnp.float32)
    high, middle, _ = exact_parts(density)
    row_ref[0:EDGE] = target
    row_ref[EDGE : 2 * EDGE] = high
    row_ref[2 * EDGE : 3 * EDGE] = middle

    def build(slot, chunk):
        profile_x, slope_x = factors(chunk_row(place_ref, 0, chunk))
        profile_y, slope_y = factors(chunk_row(place_ref, 1, chunk))
        profile_z, slope_z = factors(chunk_row(place_ref, 2, chunk))
        masses = chunk_row(place_ref, 3, chunk)
        profile_x = profile_x.astype(jnp.bfloat16)
        slope_x = slope_x.astype(jnp.bfloat16)
        weight_ref[slot, 0] = (masses * profile_y).astype(jnp.bfloat16).astype(jnp.float32)
        weight_ref[slot, 1] = (masses * slope_y).astype(jnp.bfloat16).astype(jnp.float32)
        line_ref[slot, 0] = profile_z.astype(jnp.bfloat16).astype(jnp.float32)
        line_ref[slot, 1] = slope_z.astype(jnp.bfloat16).astype(jnp.float32)
        for z in range(EDGE):
            line = jnp.broadcast_to(line_ref[slot, 0, pl.ds(z, 1), :], (EDGE, CHUNK))
            slope_line = jnp.broadcast_to(line_ref[slot, 1, pl.ds(z, 1), :], (EDGE, CHUNK))
            line = line.astype(jnp.bfloat16)
            slope_line = slope_line.astype(jnp.bfloat16)
            place = pl.ds(z * EDGE, EDGE)
            plane_ref[slot, place, pl.ds(0, CHUNK)] = line * slope_x
            plane_ref[slot, place, pl.ds(CHUNK, CHUNK)] = line * profile_x
            plane_ref[slot, place, pl.ds(2 * CHUNK, CHUNK)] = slope_line * profile_x

    def use(slot, chunk):
        rows = CHUNK // LANES
        for component, weight in enumerate((0, 1, 0)):
            pulled = jnp.dot(
                row_ref[...],
                plane_ref[slot, :, pl.ds(component * CHUNK, CHUNK)],
                preferred_element_type=jnp.float32,
            )
            weight = weight_ref[slot, weight]
            model = pulled[EDGE : 2 * EDGE] + pulled[2 * EDGE :]
            sums = (
                jnp.sum(pulled[:EDGE] * weight, axis=0, keepdims=True),
                jnp.sum(model * weight, axis=0, keepdims=True),
            )
            for kind in range(2):
                for i in range(rows):
                    sum_ref[kind, component, pl.ds(chunk * rows + i, 1), :] = sums[kind][
                        :, i * LANES : (i + 1) * LANES
                    ]

    pipeline(place_ref.shape[1] * LANES // CHUNK, build, use)
    pairs = place_ref.shape[1]
    left = lax.broadcasted_iota(jnp.int32, (pairs, LANES), 1) < LANES // 2
    for component in range(3):
        first, second = sum_ref[0, component], sum_ref[1, component]
        out_ref[pl.ds(component, pairs, stride=8), :] = jnp.where(
            left, first, pltpu.roll(second, LANES // 2, 1)
        )
        out_ref[pl.ds(4 + component, pairs, stride=8), :] = jnp.where(
            left, pltpu.roll(first, LANES // 2, 1), second
        )
    lane = lax.broadcasted_iota(jnp.int32, (2 * pairs, LANES), 1)
    totals = jnp.zeros((2 * pairs, LANES), jnp.float32)
    for place, product in enumerate((density * wide, density * density, wide * wide)):
        totals = jnp.where(lane == place, jnp.sum(product), totals)
    out_ref[pl.ds(3, 2 * pairs, stride=4), :] = totals


def call(kernel, name, out_shape, scratch, flops, *operands, source=pltpu.VMEM, limit=32):
    vmem = pl.BlockSpec(memory_space=pltpu.VMEM)
    return pl.pallas_call(
        kernel,
        out_shape=out_shape,
        in_specs=[pl.BlockSpec(memory_space=source)] * len(operands),
        out_specs=jax.tree.map(lambda _: vmem, out_shape),
        scratch_shapes=[pltpu.VMEM(*entry) if isinstance(entry, tuple) else entry for entry in scratch],
        compiler_params=pltpu.CompilerParams(vmem_limit_bytes=limit * 2**20),
        cost_estimate=pl.CostEstimate(flops=flops, bytes_accessed=2**20, transcendentals=2**20),
        name=name,
    )(*operands)


def pack(coords, weights, modes, amplitudes, tiles, offsets, n_tile):
    blocks = tiles.shape[1]
    operands = (tiles, offsets, amplitudes, coords, weights, modes)
    return call(
        pack_kernel,
        "pack",
        (
            jax.ShapeDtypeStruct((2 * n_tile, LANES), jnp.float32),
            jax.ShapeDtypeStruct((2, blocks, n_tile), jnp.bfloat16),
        ),
        [((4, weights.shape[0], LANES), jnp.float32), ((blocks, LANES), jnp.float32)]
        + [(operand.shape, operand.dtype) for operand in operands]
        + [pltpu.SemaphoreType.DMA((len(operands),))],
        2**26,
        *operands,
        source=pltpu.HBM,
        limit=60,
    )


def finish(back, picks, modes, voxels, atoms, copies):
    blocks = picks.shape[1]
    return call(
        lambda *refs: finish_kernel(voxels, atoms, *refs),
        "finish",
        (
            jax.ShapeDtypeStruct((3, modes.shape[2]), jnp.float32),
            jax.ShapeDtypeStruct((2 * copies, LANES), jnp.float32),
            jax.ShapeDtypeStruct((1, LANES), jnp.float32),
        ),
        [((3, blocks, LANES), jnp.float32)],
        2**26,
        back,
        picks,
        modes,
    )


def splat(got, copies):
    groups = got.shape[0] // 4
    return call(
        splat_kernel,
        "splat",
        jax.ShapeDtypeStruct((copies, EDGE, PLANE), jnp.float32),
        [
            ((4, groups, LANES), jnp.float32),
            ((2, EDGE, CHUNK), jnp.float32),
            ((2, EDGE, CHUNK), jnp.bfloat16),
            ((2, PLANE, CHUNK), jnp.bfloat16),
        ],
        2**29,
        got,
    )


def pull(got, parts, target):
    groups = got.shape[0] // 4
    return call(
        pull_kernel,
        "pull",
        jax.ShapeDtypeStruct((8 * groups, LANES), jnp.float32),
        [
            ((4, groups, LANES), jnp.float32),
            ((2, 2, EDGE, CHUNK), jnp.float32),
            ((2, 2, EDGE, CHUNK), jnp.float32),
            ((2, PLANE, 3 * CHUNK), jnp.bfloat16),
            ((3 * EDGE, PLANE), jnp.bfloat16),
            ((2, 3, groups, LANES), jnp.float32),
        ],
        2**32,
        got,
        parts,
        target,
    )


TILE_AXES = ("y", "z", "core")


def exchange(values, axes):
    return lax.all_to_all(values, axes, split_axis=0, concat_axis=0, tiled=True)


def on_device(coords, weights, mode_vectors, amplitudes, density_map, block_tiles, block_offsets):
    a_dev = coords.shape[1]
    n_tile = lax.axis_size(TILE_AXES)
    n_seg = lax.axis_size("seg")
    modes = jnp.transpose(mode_vectors, (1, 0, 2))
    send, picks = pack(
        coords,
        weights.reshape(a_dev // LANES, LANES),
        modes,
        amplitudes.reshape(1, -1),
        block_tiles.T,
        jnp.transpose(block_offsets, (2, 1, 0)),
        n_tile,
    )
    got = exchange(send.reshape(n_tile, 2, LANES), TILE_AXES).reshape(2 * n_tile, LANES)
    target = jnp.transpose(density_map.reshape(PLANE, EDGE))
    parts = exchange(splat(got, n_seg), "seg")
    pulled = pull(got, parts, target)
    back = exchange(pulled.reshape(n_tile, 4, LANES), TILE_AXES).reshape(4 * n_tile, LANES)
    near, far = ("z", "core"), ("y", "seg")
    forces, spread, score = finish(
        back, picks, modes, float(n_tile * EDGE**3), a_dev * n_tile * n_seg, lax.axis_size(near)
    )
    near_sum = jnp.sum(exchange(spread.reshape(-1, 2, LANES), near), axis=0)
    copies = jnp.broadcast_to(near_sum[None], (lax.axis_size(far), 2, LANES))
    mode_grad = jnp.sum(exchange(copies, far), axis=0).reshape(-1)
    return (forces, mode_grad, score[0, 0])


def solution(mesh):
    split = Mesh(mesh.devices.reshape(8, 8, 2, 4), TILE_AXES + ("seg",))
    every = TILE_AXES + ("seg",)
    return jax.shard_map(
        on_device,
        mesh=split,
        in_specs=(
            P(None, every),
            P(every),
            P(None, None, every),
            P(),
            P(TILE_AXES, None),
            P(every, None),
            P(every, None, None),
        ),
        out_specs=(P(None, every), P(), P()),
        check_vma=False,
    )
```

```python
import jax
import jax.numpy as jnp
from jax import lax
from jax.experimental import pallas as pl
from jax.experimental.pallas import tpu as pltpu
from jax.sharding import Mesh
from jax.sharding import PartitionSpec as P

EDGE = 32
ATOM_BLOCK = 32
PLANE = EDGE * EDGE
LANES = 128
SPLAT_CHUNK = 512
PULL_CHUNK = 256

inverse_var = 1.0 / 2.25


def factors(places):
    centers = lax.broadcasted_iota(jnp.int32, (EDGE, places.shape[1]), 0).astype(jnp.float32) + 0.5
    distance = centers - places
    profile = jnp.exp(-0.5 * inverse_var * distance * distance)
    return profile, inverse_var * distance * profile


def exact_parts(values):
    high = values.astype(jnp.bfloat16)
    rest = values - high.astype(jnp.float32)
    middle = rest.astype(jnp.bfloat16)
    return high, middle, (rest - middle.astype(jnp.float32)).astype(jnp.bfloat16)


def against_rows(left, right):
    return lax.dot_general(
        left, right, (((1,), (1,)), ((), ())), preferred_element_type=jnp.float32
    )


def quarter_of(shape):
    return lax.broadcasted_iota(jnp.int32, shape, 1) // ATOM_BLOCK


def regroup(rows, target):
    quarter = quarter_of(rows[0].shape)
    result = jnp.zeros_like(rows[0])
    for i in range(4):
        moved = pltpu.roll(rows[i], ((i - target) % 4) * ATOM_BLOCK, 1) if i != target else rows[i]
        result = jnp.where(quarter == i, moved, result)
    return result


def pack_kernel(*refs):
    sources, (send_ref, pick_ref), (cell_ref, block_ref) = refs[:6], refs[6:8], refs[8:10]
    local, sems = refs[10:16], refs[16]
    copies = [
        pltpu.make_async_copy(source, place, sems.at[i])
        for i, (source, place) in enumerate(zip(sources, local))
    ]
    for copy in copies:
        copy.start()
    tiles_ref, offsets_ref, amps_ref, coords_ref, weights_ref, modes_ref = local
    n_tile = send_ref.shape[0] // 2
    blocks = block_ref.shape[0]
    cells = cell_ref.shape[1]
    for copy in copies[:2]:
        copy.wait()
    shape = (n_tile, blocks)
    tile_of_row = lax.broadcasted_iota(jnp.int32, shape, 0)
    row = lax.broadcasted_iota(jnp.int32, (blocks, blocks), 0)
    column = lax.broadcasted_iota(jnp.int32, (blocks, blocks), 1)
    before = jnp.where(row < column, 1.0, 0.0).astype(jnp.bfloat16)
    same = jnp.where(row == column, 1.0, 0.0).astype(jnp.bfloat16)
    ones = jnp.ones((blocks, blocks), jnp.bfloat16)
    seen = jnp.zeros(shape, jnp.float32)
    picks = [jnp.zeros(shape, jnp.float32) for _ in range(2)]
    shifts = [jnp.zeros((n_tile, LANES), jnp.float32) for _ in range(2)]
    for k in range(tiles_ref.shape[0]):
        named = jnp.where(tiles_ref[pl.ds(k, 1), :] == tile_of_row, 1.0, 0.0)
        flags = named.astype(jnp.bfloat16)
        rank = seen + jnp.dot(flags, before, preferred_element_type=jnp.float32)
        seen = seen + jnp.dot(flags, ones, preferred_element_type=jnp.float32)
        offsets = [
            jnp.broadcast_to(offsets_ref[c, pl.ds(k, 1), :].astype(jnp.float32), (ATOM_BLOCK, blocks))
            for c in range(3)
        ]
        offsets = jnp.concatenate(offsets + [jnp.zeros((ATOM_BLOCK, blocks), jnp.float32)], axis=0)
        for slot in range(2):
            mine = jnp.where(rank == float(slot), named, 0.0)
            picks[slot] = picks[slot] + mine
            shifts[slot] = shifts[slot] + against_rows(
                mine.astype(jnp.bfloat16), offsets.astype(jnp.bfloat16)
            )
    for copy in copies[2:]:
        copy.wait()
    amps = jnp.broadcast_to(amps_ref[...], (16, amps_ref.shape[1])).astype(jnp.bfloat16)
    for component in range(3):
        moved = jnp.dot(amps, modes_ref[component], preferred_element_type=jnp.float32)
        places = coords_ref[pl.ds(component, 1), :] + moved[0:1]
        for cell in range(cells):
            cell_ref[component, pl.ds(cell, 1), :] = places[:, cell * LANES : (cell + 1) * LANES]
    cell_ref[3] = weights_ref[...]
    for i in range(4):
        block_ref[pl.ds(i, cells, stride=4), :] = regroup([cell_ref[c] for c in range(4)], i)
    parts = exact_parts(block_ref[...])
    for slot in range(2):
        pick = picks[slot].astype(jnp.bfloat16)
        high, middle, low = [jnp.dot(pick, part, preferred_element_type=jnp.float32) for part in parts]
        send_ref[pl.ds(slot, n_tile, stride=2), :] = ((high + middle) + low) + shifts[slot]
        pick_ref[slot] = against_rows(same, pick).astype(jnp.bfloat16)


def finish_kernel(voxels, atoms, back_ref, pick_ref, modes_ref, forces_ref, spread_ref, score_ref, block_ref):
    n_tile = pick_ref.shape[2]
    lane = lax.broadcasted_iota(jnp.int32, (1, LANES), 1)
    totals = jnp.sum(back_ref[pl.ds(3, n_tile, stride=4), :], axis=0, keepdims=True)
    srm, srr, smm = [
        jnp.sum(jnp.where(lane == i, totals, 0.0), axis=1, keepdims=True) for i in range(3)
    ]
    root = jnp.sqrt(srr * smm)
    score = srm / root
    score_ref[...] = jnp.broadcast_to(score, score_ref.shape)
    map_scale = voxels / root
    model_scale = voxels * (score / srr)
    cells = forces_ref.shape[1] // LANES
    modes = jnp.zeros((1, modes_ref.shape[1]), jnp.float32)
    for component in range(3):
        pulled = back_ref[pl.ds(component, n_tile, stride=4), :]
        pulled = pulled * map_scale - pltpu.roll(pulled, LANES // 2, 1) * model_scale
        parts = exact_parts(pulled)
        first, second = [
            sum([jnp.dot(pick_ref[slot], part, preferred_element_type=jnp.float32) for part in parts[::-1]])
            for slot in range(2)
        ]
        block_ref[component] = first + pltpu.roll(second, LANES - ATOM_BLOCK, 1)
        rows = regroup([block_ref[component, pl.ds(i, cells, stride=4), :] for i in range(4)], 0)
        for cell in range(cells):
            forces_ref[pl.ds(component, 1), cell * LANES : (cell + 1) * LANES] = rows[cell : cell + 1]
        force = jnp.broadcast_to(forces_ref[pl.ds(component, 1), :], (16, forces_ref.shape[1]))
        modes = modes + against_rows(force.astype(jnp.bfloat16), modes_ref[component])[0:1]
    modes = modes / jnp.sqrt(jnp.float32(atoms))
    half = spread_ref.shape[0] // 2
    for part in range(2):
        spread_ref[pl.ds(part, half, stride=2), :] = jnp.broadcast_to(
            modes[:, part * LANES : (part + 1) * LANES], (half, LANES)
        )


def unpack_rows(got_ref, place_ref):
    groups = got_ref.shape[0] // 4
    rows = [got_ref[pl.ds(i, groups, stride=4), :] for i in range(4)]
    for component in range(4):
        place_ref[component] = regroup(rows, component)


def chunk_row(place_ref, component, chunk, size):
    rows = size // LANES
    return jnp.concatenate(
        [place_ref[component, pl.ds(chunk * rows + i, 1), :] for i in range(rows)], axis=1
    )


def pipeline(chunks, build, use):
    build(0, 0)

    @pl.loop(0, chunks // 2)
    def _(step):
        build(1, 2 * step + 1)
        use(0, 2 * step)
        build(0, jnp.minimum(2 * step + 2, chunks - 1))
        use(1, 2 * step + 1)


def build_plane(place_ref, line_ref, plane_ref, slot, chunk, size):
    along_x = factors(chunk_row(place_ref, 0, chunk, size))[0].astype(jnp.bfloat16)
    along_z = factors(chunk_row(place_ref, 2, chunk, size))[0].astype(jnp.bfloat16)
    line_ref[slot] = along_z.astype(jnp.float32)
    for z in range(EDGE):
        line = jnp.broadcast_to(line_ref[slot, pl.ds(z, 1), :], (EDGE, size))
        plane_ref[slot, pl.ds(z * EDGE, EDGE), :] = line.astype(jnp.bfloat16) * along_x


def splat_kernel(got_ref, out_ref, place_ref, line_ref, weight_ref, plane_ref, sum_ref):
    size = plane_ref.shape[2]
    unpack_rows(got_ref, place_ref)
    sum_ref[...] = jnp.zeros_like(sum_ref)

    def build(slot, chunk):
        build_plane(place_ref, line_ref, plane_ref, slot, chunk, size)
        along_y = factors(chunk_row(place_ref, 1, chunk, size))[0]
        weight_ref[slot] = (chunk_row(place_ref, 3, chunk, size) * along_y).astype(jnp.bfloat16)

    def use(slot, chunk):
        sum_ref[...] += against_rows(plane_ref[slot], weight_ref[slot])

    pipeline(place_ref.shape[1] * LANES // size, build, use)
    total = sum_ref[...].T
    for copy in range(out_ref.shape[0]):
        out_ref[copy] = total


def pull_kernel(got_ref, parts_ref, target_ref, out_ref, place_ref, line_ref, weight_ref, plane_ref, row_ref, sum_ref):
    size = plane_ref.shape[2]
    unpack_rows(got_ref, place_ref)
    density = (parts_ref[0] + parts_ref[2]) + (parts_ref[1] + parts_ref[3])
    wide = target_ref[...].astype(jnp.float32)
    voxel = lax.broadcasted_iota(jnp.int32, (EDGE, PLANE), 1)
    middle = EDGE / 2
    center_x = (voxel % EDGE).astype(jnp.float32) + (0.5 - middle)
    center_z = (voxel // EDGE).astype(jnp.float32) + (0.5 - middle)
    row_ref[0:EDGE] = target_ref[...]
    places = [(wide * center_x, 1), (wide * center_z, 3), (density, 5), (density * center_x, 7), (density * center_z, 9)]
    for values, place in places:
        high, low, _ = exact_parts(values)
        row_ref[place * EDGE : (place + 1) * EDGE] = high
        row_ref[(place + 1) * EDGE : (place + 2) * EDGE] = low

    def build(slot, chunk):
        build_plane(place_ref, line_ref, plane_ref, slot, chunk, size)
        profile_y, slope_y = factors(chunk_row(place_ref, 1, chunk, size))
        masses = chunk_row(place_ref, 3, chunk, size)
        weight_ref[slot, 0] = (masses * profile_y).astype(jnp.bfloat16).astype(jnp.float32)
        weight_ref[slot, 1] = (masses * slope_y).astype(jnp.bfloat16).astype(jnp.float32)

    def use(slot, chunk):
        rows = size // LANES
        pulled = jnp.dot(row_ref[...], plane_ref[slot], preferred_element_type=jnp.float32)
        block = [pulled[i * EDGE : (i + 1) * EDGE] for i in range(11)]
        along_y, slope_y = weight_ref[slot, 0], weight_ref[slot, 1]
        place_x = chunk_row(place_ref, 0, chunk, size) - middle
        place_z = chunk_row(place_ref, 2, chunk, size) - middle
        kinds = (
            (block[0], block[1] + block[2], block[3] + block[4]),
            (block[5] + block[6], block[7] + block[8], block[9] + block[10]),
        )
        for kind, (plain, by_x, by_z) in enumerate(kinds):
            whole, force_y, moment_x, moment_z = [
                jnp.sum(values * weight, axis=0, keepdims=True)
                for values, weight in ((plain, along_y), (plain, slope_y), (by_x, along_y), (by_z, along_y))
            ]
            force_x = inverse_var * (moment_x - place_x * whole)
            force_z = inverse_var * (moment_z - place_z * whole)
            for component, force in enumerate((force_x, force_y, force_z)):
                for i in range(rows):
                    sum_ref[kind, component, pl.ds(chunk * rows + i, 1), :] = force[
                        :, i * LANES : (i + 1) * LANES
                    ]

    pipeline(place_ref.shape[1] * LANES // size, build, use)
    pairs = place_ref.shape[1]
    left = lax.broadcasted_iota(jnp.int32, (pairs, LANES), 1) < LANES // 2
    for component in range(3):
        first, second = sum_ref[0, component], sum_ref[1, component]
        out_ref[pl.ds(component, pairs, stride=8), :] = jnp.where(
            left, first, pltpu.roll(second, LANES // 2, 1)
        )
        out_ref[pl.ds(4 + component, pairs, stride=8), :] = jnp.where(
            left, pltpu.roll(first, LANES // 2, 1), second
        )
    lane = lax.broadcasted_iota(jnp.int32, (2 * pairs, LANES), 1)
    totals = jnp.zeros((2 * pairs, LANES), jnp.float32)
    for place, product in enumerate((density * wide, density * density, wide * wide)):
        totals = jnp.where(lane == place, jnp.sum(product), totals)
    out_ref[pl.ds(3, 2 * pairs, stride=4), :] = totals


def call(kernel, name, out_shape, scratch, flops, *operands, source=pltpu.VMEM, limit=32):
    vmem = pl.BlockSpec(memory_space=pltpu.VMEM)
    return pl.pallas_call(
        kernel,
        out_shape=out_shape,
        in_specs=[pl.BlockSpec(memory_space=source)] * len(operands),
        out_specs=jax.tree.map(lambda _: vmem, out_shape),
        scratch_shapes=[pltpu.VMEM(*entry) if isinstance(entry, tuple) else entry for entry in scratch],
        compiler_params=pltpu.CompilerParams(vmem_limit_bytes=limit * 2**20),
        cost_estimate=pl.CostEstimate(flops=flops, bytes_accessed=2**20, transcendentals=2**20),
        name=name,
    )(*operands)


def pack(coords, weights, modes, amplitudes, tiles, offsets, n_tile):
    blocks = tiles.shape[1]
    operands = (tiles, offsets, amplitudes, coords, weights, modes)
    return call(
        pack_kernel,
        "pack",
        (
            jax.ShapeDtypeStruct((2 * n_tile, LANES), jnp.float32),
            jax.ShapeDtypeStruct((2, blocks, n_tile), jnp.bfloat16),
        ),
        [((4, weights.shape[0], LANES), jnp.float32), ((blocks, LANES), jnp.float32)]
        + [(operand.shape, operand.dtype) for operand in operands]
        + [pltpu.SemaphoreType.DMA((len(operands),))],
        2**26,
        *operands,
        source=pltpu.HBM,
        limit=60,
    )


def finish(back, picks, modes, voxels, atoms, copies):
    blocks = picks.shape[1]
    return call(
        lambda *refs: finish_kernel(voxels, atoms, *refs),
        "finish",
        (
            jax.ShapeDtypeStruct((3, modes.shape[2]), jnp.float32),
            jax.ShapeDtypeStruct((2 * copies, LANES), jnp.float32),
            jax.ShapeDtypeStruct((1, LANES), jnp.float32),
        ),
        [((3, blocks, LANES), jnp.float32)],
        2**26,
        back,
        picks,
        modes,
    )


def splat(got, copies):
    groups = got.shape[0] // 4
    size = min(SPLAT_CHUNK, groups * LANES // 2)
    return call(
        splat_kernel,
        "splat",
        jax.ShapeDtypeStruct((copies, EDGE, PLANE), jnp.float32),
        [
            ((4, groups, LANES), jnp.float32),
            ((2, EDGE, size), jnp.float32),
            ((2, EDGE, size), jnp.bfloat16),
            ((2, PLANE, size), jnp.bfloat16),
            ((PLANE, EDGE), jnp.float32),
        ],
        2**29,
        got,
    )


def pull(got, parts, target):
    groups = got.shape[0] // 4
    size = min(PULL_CHUNK, groups * LANES // 2)
    return call(
        pull_kernel,
        "pull",
        jax.ShapeDtypeStruct((8 * groups, LANES), jnp.float32),
        [
            ((4, groups, LANES), jnp.float32),
            ((2, EDGE, size), jnp.float32),
            ((2, 2, EDGE, size), jnp.float32),
            ((2, PLANE, size), jnp.bfloat16),
            ((11 * EDGE, PLANE), jnp.bfloat16),
            ((2, 3, groups, LANES), jnp.float32),
        ],
        2**32,
        got,
        parts,
        target,
    )


TILE_AXES = ("y", "z", "core")


def exchange(values, axes):
    return lax.all_to_all(values, axes, split_axis=0, concat_axis=0, tiled=True)


def on_device(coords, weights, mode_vectors, amplitudes, density_map, block_tiles, block_offsets):
    a_dev = coords.shape[1]
    n_tile = lax.axis_size(TILE_AXES)
    n_seg = lax.axis_size("seg")
    modes = jnp.transpose(mode_vectors, (1, 0, 2))
    send, picks = pack(
        coords,
        weights.reshape(a_dev // LANES, LANES),
        modes,
        amplitudes.reshape(1, -1),
        block_tiles.T,
        jnp.transpose(block_offsets, (2, 1, 0)),
        n_tile,
    )
    got = exchange(send.reshape(n_tile, 2, LANES), TILE_AXES).reshape(2 * n_tile, LANES)
    target = jnp.transpose(density_map.reshape(PLANE, EDGE))
    parts = exchange(splat(got, n_seg), "seg")
    pulled = pull(got, parts, target)
    back = exchange(pulled.reshape(n_tile, 4, LANES), TILE_AXES).reshape(4 * n_tile, LANES)
    near, far = ("z", "core"), ("y", "seg")
    forces, spread, score = finish(
        back, picks, modes, float(n_tile * EDGE**3), a_dev * n_tile * n_seg, lax.axis_size(near)
    )
    near_sum = jnp.sum(exchange(spread.reshape(-1, 2, LANES), near), axis=0)
    copies = jnp.broadcast_to(near_sum[None], (lax.axis_size(far), 2, LANES))
    mode_grad = jnp.sum(exchange(copies, far), axis=0).reshape(-1)
    return (forces, mode_grad, score[0, 0])


def solution(mesh):
    split = Mesh(mesh.devices.reshape(8, 8, 2, 4), TILE_AXES + ("seg",))
    every = TILE_AXES + ("seg",)
    return jax.shard_map(
        on_device,
        mesh=split,
        in_specs=(
            P(None, every),
            P(every),
            P(None, None, every),
            P(),
            P(TILE_AXES, None),
            P(every, None),
            P(every, None, None),
        ),
        out_specs=(P(None, every), P(), P()),
        check_vma=False,
    )
```

```python
import jax
import jax.numpy as jnp
from jax import lax
from jax.experimental import pallas as pl
from jax.experimental.pallas import tpu as pltpu
from jax.sharding import Mesh
from jax.sharding import PartitionSpec as P

EDGE = 32
ATOM_BLOCK = 32
PLANE = EDGE * EDGE
LANES = 128
SPLAT_CHUNK = 512
PULL_CHUNK = 512
WIDTH = 256

inverse_var = 1.0 / 2.25


def factors(places):
    centers = lax.broadcasted_iota(jnp.int32, (EDGE, places.shape[1]), 0).astype(jnp.float32) + 0.5
    distance = centers - places
    profile = jnp.exp(-0.5 * inverse_var * distance * distance)
    return profile, inverse_var * distance * profile


def exact_parts(values):
    high = values.astype(jnp.bfloat16)
    rest = values - high.astype(jnp.float32)
    middle = rest.astype(jnp.bfloat16)
    return high, middle, (rest - middle.astype(jnp.float32)).astype(jnp.bfloat16)


def against_rows(left, right):
    return lax.dot_general(
        left, right, (((1,), (1,)), ((), ())), preferred_element_type=jnp.float32
    )


def quarter_of(shape):
    return lax.broadcasted_iota(jnp.int32, shape, 1) // ATOM_BLOCK


def regroup(rows, target):
    quarter = quarter_of(rows[0].shape)
    result = jnp.zeros_like(rows[0])
    for i in range(4):
        moved = pltpu.roll(rows[i], ((i - target) % 4) * ATOM_BLOCK, 1) if i != target else rows[i]
        result = jnp.where(quarter == i, moved, result)
    return result


def pack_kernel(*refs):
    sources, (send_ref, pick_ref), (cell_ref, block_ref) = refs[:6], refs[6:8], refs[8:10]
    local, sems = refs[10:16], refs[16]
    copies = [
        pltpu.make_async_copy(source, place, sems.at[i])
        for i, (source, place) in enumerate(zip(sources, local))
    ]
    for copy in copies:
        copy.start()
    tiles_ref, offsets_ref, amps_ref, coords_ref, weights_ref, modes_ref = local
    n_tile = send_ref.shape[0] // 2
    blocks = block_ref.shape[0]
    cells = cell_ref.shape[1]
    for copy in copies[:2]:
        copy.wait()
    shape = (n_tile, blocks)
    tile_of_row = lax.broadcasted_iota(jnp.int32, shape, 0)
    row = lax.broadcasted_iota(jnp.int32, (blocks, blocks), 0)
    column = lax.broadcasted_iota(jnp.int32, (blocks, blocks), 1)
    before = jnp.where(row < column, 1.0, 0.0).astype(jnp.bfloat16)
    same = jnp.where(row == column, 1.0, 0.0).astype(jnp.bfloat16)
    ones = jnp.ones((blocks, blocks), jnp.bfloat16)
    seen = jnp.zeros(shape, jnp.float32)
    picks = [jnp.zeros(shape, jnp.float32) for _ in range(2)]
    shifts = [jnp.zeros((n_tile, LANES), jnp.float32) for _ in range(2)]
    for k in range(tiles_ref.shape[0]):
        named = jnp.where(tiles_ref[pl.ds(k, 1), :] == tile_of_row, 1.0, 0.0)
        flags = named.astype(jnp.bfloat16)
        rank = seen + jnp.dot(flags, before, preferred_element_type=jnp.float32)
        seen = seen + jnp.dot(flags, ones, preferred_element_type=jnp.float32)
        offsets = [
            jnp.broadcast_to(offsets_ref[c, pl.ds(k, 1), :].astype(jnp.float32), (ATOM_BLOCK, blocks))
            for c in range(3)
        ]
        offsets = jnp.concatenate(offsets + [jnp.zeros((ATOM_BLOCK, blocks), jnp.float32)], axis=0)
        for slot in range(2):
            mine = jnp.where(rank == float(slot), named, 0.0)
            picks[slot] = picks[slot] + mine
            shifts[slot] = shifts[slot] + against_rows(
                mine.astype(jnp.bfloat16), offsets.astype(jnp.bfloat16)
            )
    for copy in copies[2:]:
        copy.wait()
    amps = jnp.broadcast_to(amps_ref[...], (16, amps_ref.shape[1])).astype(jnp.bfloat16)
    for component in range(3):
        moved = jnp.dot(amps, modes_ref[component], preferred_element_type=jnp.float32)
        places = coords_ref[pl.ds(component, 1), :] + moved[0:1]
        for cell in range(cells):
            cell_ref[component, pl.ds(cell, 1), :] = places[:, cell * LANES : (cell + 1) * LANES]
    cell_ref[3] = weights_ref[...]
    for i in range(4):
        block_ref[pl.ds(i, cells, stride=4), :] = regroup([cell_ref[c] for c in range(4)], i)
    parts = exact_parts(block_ref[...])
    for slot in range(2):
        pick = picks[slot].astype(jnp.bfloat16)
        high, middle, low = [jnp.dot(pick, part, preferred_element_type=jnp.float32) for part in parts]
        send_ref[pl.ds(slot, n_tile, stride=2), :] = ((high + middle) + low) + shifts[slot]
        pick_ref[slot] = against_rows(same, pick).astype(jnp.bfloat16)


def finish_kernel(voxels, atoms, back_ref, pick_ref, modes_ref, forces_ref, spread_ref, score_ref, block_ref):
    n_tile = pick_ref.shape[2]
    lane = lax.broadcasted_iota(jnp.int32, (1, LANES), 1)
    totals = jnp.sum(back_ref[pl.ds(3, n_tile, stride=4), :], axis=0, keepdims=True)
    srm, srr, smm = [
        jnp.sum(jnp.where(lane == i, totals, 0.0), axis=1, keepdims=True) for i in range(3)
    ]
    root = jnp.sqrt(srr * smm)
    score = srm / root
    score_ref[...] = jnp.broadcast_to(score, score_ref.shape)
    map_scale = voxels / root
    model_scale = voxels * (score / srr)
    cells = forces_ref.shape[1] // LANES
    modes = jnp.zeros((1, modes_ref.shape[1]), jnp.float32)
    for component in range(3):
        pulled = back_ref[pl.ds(component, n_tile, stride=4), :]
        pulled = pulled * map_scale - pltpu.roll(pulled, LANES // 2, 1) * model_scale
        parts = exact_parts(pulled)
        first, second = [
            sum([jnp.dot(pick_ref[slot], part, preferred_element_type=jnp.float32) for part in parts[::-1]])
            for slot in range(2)
        ]
        block_ref[component] = first + pltpu.roll(second, LANES - ATOM_BLOCK, 1)
        rows = regroup([block_ref[component, pl.ds(i, cells, stride=4), :] for i in range(4)], 0)
        for cell in range(cells):
            forces_ref[pl.ds(component, 1), cell * LANES : (cell + 1) * LANES] = rows[cell : cell + 1]
        force = jnp.broadcast_to(forces_ref[pl.ds(component, 1), :], (16, forces_ref.shape[1]))
        modes = modes + against_rows(force.astype(jnp.bfloat16), modes_ref[component])[0:1]
    modes = modes / jnp.sqrt(jnp.float32(atoms))
    half = spread_ref.shape[0] // 2
    for part in range(2):
        spread_ref[pl.ds(part, half, stride=2), :] = jnp.broadcast_to(
            modes[:, part * LANES : (part + 1) * LANES], (half, LANES)
        )


def unpack_rows(got_ref, place_ref):
    groups = got_ref.shape[0] // 4
    rows = [got_ref[pl.ds(i, groups, stride=4), :] for i in range(4)]
    for component in range(4):
        place_ref[component] = regroup(rows, component)


def chunk_row(place_ref, component, chunk, size):
    rows = size // LANES
    return jnp.concatenate(
        [place_ref[component, pl.ds(chunk * rows + i, 1), :] for i in range(rows)], axis=1
    )


def pipeline(chunks, build, use):
    build(0, 0)

    @pl.loop(0, chunks // 2)
    def _(step):
        build(1, 2 * step + 1)
        use(0, 2 * step)
        build(0, jnp.minimum(2 * step + 2, chunks - 1))
        use(1, 2 * step + 1)


def build_plane(place_ref, line_ref, plane_ref, slot, chunk, size):
    along_x = factors(chunk_row(place_ref, 0, chunk, size))[0].astype(jnp.bfloat16)
    along_z = factors(chunk_row(place_ref, 2, chunk, size))[0].astype(jnp.bfloat16)
    line_ref[slot] = along_z.astype(jnp.float32)
    for z in range(EDGE):
        line = jnp.broadcast_to(line_ref[slot, pl.ds(z, 1), :], (EDGE, size))
        plane_ref[slot, pl.ds(z * EDGE, EDGE), :] = line.astype(jnp.bfloat16) * along_x


def splat_kernel(got_ref, out_ref, place_ref, line_ref, weight_ref, plane_ref, sum_ref):
    size = plane_ref.shape[2]
    unpack_rows(got_ref, place_ref)
    sum_ref[...] = jnp.zeros_like(sum_ref)

    def build(slot, chunk):
        build_plane(place_ref, line_ref, plane_ref, slot, chunk, size)
        along_y = factors(chunk_row(place_ref, 1, chunk, size))[0]
        weight_ref[slot] = (chunk_row(place_ref, 3, chunk, size) * along_y).astype(jnp.bfloat16)

    def use(slot, chunk):
        for half in range(2):
            rows = pl.ds(half * PLANE // 2, PLANE // 2)
            sum_ref[rows, :] += against_rows(plane_ref[slot, rows, :], weight_ref[slot])

    pipeline(place_ref.shape[1] * LANES // size, build, use)
    total = sum_ref[...].T
    for copy in range(out_ref.shape[0]):
        out_ref[copy] = total


def pull_kernel(got_ref, parts_ref, target_ref, out_ref, place_ref, line_ref, weight_ref, plane_ref, row_ref, sum_ref):
    size = plane_ref.shape[2]
    unpack_rows(got_ref, place_ref)
    density = (parts_ref[0] + parts_ref[2]) + (parts_ref[1] + parts_ref[3])
    wide = target_ref[...].astype(jnp.float32)
    voxel = lax.broadcasted_iota(jnp.int32, (EDGE, PLANE), 1)
    middle = EDGE / 2
    center_x = (voxel % EDGE).astype(jnp.float32) + (0.5 - middle)
    center_z = (voxel // EDGE).astype(jnp.float32) + (0.5 - middle)
    row_ref[0:EDGE] = target_ref[...]
    places = [(wide * center_x, 1), (wide * center_z, 3), (density, 5), (density * center_x, 7), (density * center_z, 9)]
    for values, place in places:
        high, low, _ = exact_parts(values)
        row_ref[place * EDGE : (place + 1) * EDGE] = high
        row_ref[(place + 1) * EDGE : (place + 2) * EDGE] = low

    def build(slot, chunk):
        build_plane(place_ref, line_ref, plane_ref, slot, chunk, size)
        profile_y, slope_y = factors(chunk_row(place_ref, 1, chunk, size))
        masses = chunk_row(place_ref, 3, chunk, size)
        weight_ref[slot, 0] = (masses * profile_y).astype(jnp.bfloat16).astype(jnp.float32)
        weight_ref[slot, 1] = (masses * slope_y).astype(jnp.bfloat16).astype(jnp.float32)

    def use(slot, chunk):
        width = min(WIDTH, size)
        for part in range(size // width):
            use_part(slot, chunk * (size // width) + part, pl.ds(part * width, width), width)

    def use_part(slot, chunk, atoms, size):
        rows = size // LANES
        pulled = jnp.dot(row_ref[...], plane_ref[slot, :, atoms], preferred_element_type=jnp.float32)
        block = [pulled[i * EDGE : (i + 1) * EDGE] for i in range(11)]
        along_y, slope_y = weight_ref[slot, 0, :, atoms], weight_ref[slot, 1, :, atoms]
        place_x = chunk_row(place_ref, 0, chunk, size) - middle
        place_z = chunk_row(place_ref, 2, chunk, size) - middle
        kinds = (
            (block[0], block[1] + block[2], block[3] + block[4]),
            (block[5] + block[6], block[7] + block[8], block[9] + block[10]),
        )
        for kind, (plain, by_x, by_z) in enumerate(kinds):
            whole, force_y, moment_x, moment_z = [
                jnp.sum(values * weight, axis=0, keepdims=True)
                for values, weight in ((plain, along_y), (plain, slope_y), (by_x, along_y), (by_z, along_y))
            ]
            force_x = inverse_var * (moment_x - place_x * whole)
            force_z = inverse_var * (moment_z - place_z * whole)
            for component, force in enumerate((force_x, force_y, force_z)):
                for i in range(rows):
                    sum_ref[kind, component, pl.ds(chunk * rows + i, 1), :] = force[
                        :, i * LANES : (i + 1) * LANES
                    ]

    pipeline(place_ref.shape[1] * LANES // size, build, use)
    pairs = place_ref.shape[1]
    left = lax.broadcasted_iota(jnp.int32, (pairs, LANES), 1) < LANES // 2
    for component in range(3):
        first, second = sum_ref[0, component], sum_ref[1, component]
        out_ref[pl.ds(component, pairs, stride=8), :] = jnp.where(
            left, first, pltpu.roll(second, LANES // 2, 1)
        )
        out_ref[pl.ds(4 + component, pairs, stride=8), :] = jnp.where(
            left, pltpu.roll(first, LANES // 2, 1), second
        )
    lane = lax.broadcasted_iota(jnp.int32, (2 * pairs, LANES), 1)
    totals = jnp.zeros((2 * pairs, LANES), jnp.float32)
    for place, product in enumerate((density * wide, density * density, wide * wide)):
        totals = jnp.where(lane == place, jnp.sum(product), totals)
    out_ref[pl.ds(3, 2 * pairs, stride=4), :] = totals


def call(kernel, name, out_shape, scratch, flops, *operands, source=pltpu.VMEM, limit=32):
    vmem = pl.BlockSpec(memory_space=pltpu.VMEM)
    return pl.pallas_call(
        kernel,
        out_shape=out_shape,
        in_specs=[pl.BlockSpec(memory_space=source)] * len(operands),
        out_specs=jax.tree.map(lambda _: vmem, out_shape),
        scratch_shapes=[pltpu.VMEM(*entry) if isinstance(entry, tuple) else entry for entry in scratch],
        compiler_params=pltpu.CompilerParams(vmem_limit_bytes=limit * 2**20),
        cost_estimate=pl.CostEstimate(flops=flops, bytes_accessed=2**20, transcendentals=2**20),
        name=name,
    )(*operands)


def pack(coords, weights, modes, amplitudes, tiles, offsets, n_tile):
    blocks = tiles.shape[1]
    operands = (tiles, offsets, amplitudes, coords, weights, modes)
    return call(
        pack_kernel,
        "pack",
        (
            jax.ShapeDtypeStruct((2 * n_tile, LANES), jnp.float32),
            jax.ShapeDtypeStruct((2, blocks, n_tile), jnp.bfloat16),
        ),
        [((4, weights.shape[0], LANES), jnp.float32), ((blocks, LANES), jnp.float32)]
        + [(operand.shape, operand.dtype) for operand in operands]
        + [pltpu.SemaphoreType.DMA((len(operands),))],
        2**26,
        *operands,
        source=pltpu.HBM,
        limit=60,
    )


def finish(back, picks, modes, voxels, atoms, copies):
    blocks = picks.shape[1]
    return call(
        lambda *refs: finish_kernel(voxels, atoms, *refs),
        "finish",
        (
            jax.ShapeDtypeStruct((3, modes.shape[2]), jnp.float32),
            jax.ShapeDtypeStruct((2 * copies, LANES), jnp.float32),
            jax.ShapeDtypeStruct((1, LANES), jnp.float32),
        ),
        [((3, blocks, LANES), jnp.float32)],
        2**26,
        back,
        picks,
        modes,
    )


def splat(got, copies):
    groups = got.shape[0] // 4
    size = min(SPLAT_CHUNK, groups * LANES // 2)
    return call(
        splat_kernel,
        "splat",
        jax.ShapeDtypeStruct((copies, EDGE, PLANE), jnp.float32),
        [
            ((4, groups, LANES), jnp.float32),
            ((2, EDGE, size), jnp.float32),
            ((2, EDGE, size), jnp.bfloat16),
            ((2, PLANE, size), jnp.bfloat16),
            ((PLANE, EDGE), jnp.float32),
        ],
        2**29,
        got,
    )


def pull(got, parts, target):
    groups = got.shape[0] // 4
    size = min(PULL_CHUNK, groups * LANES // 2)
    return call(
        pull_kernel,
        "pull",
        jax.ShapeDtypeStruct((8 * groups, LANES), jnp.float32),
        [
            ((4, groups, LANES), jnp.float32),
            ((2, EDGE, size), jnp.float32),
            ((2, 2, EDGE, size), jnp.float32),
            ((2, PLANE, size), jnp.bfloat16),
            ((11 * EDGE, PLANE), jnp.bfloat16),
            ((2, 3, groups, LANES), jnp.float32),
        ],
        2**32,
        got,
        parts,
        target,
    )


TILE_AXES = ("y", "z", "core")


def exchange(values, axes):
    return lax.all_to_all(values, axes, split_axis=0, concat_axis=0, tiled=True)


def on_device(coords, weights, mode_vectors, amplitudes, density_map, block_tiles, block_offsets):
    a_dev = coords.shape[1]
    n_tile = lax.axis_size(TILE_AXES)
    n_seg = lax.axis_size("seg")
    modes = jnp.transpose(mode_vectors, (1, 0, 2))
    send, picks = pack(
        coords,
        weights.reshape(a_dev // LANES, LANES),
        modes,
        amplitudes.reshape(1, -1),
        block_tiles.T,
        jnp.transpose(block_offsets, (2, 1, 0)),
        n_tile,
    )
    got = exchange(send.reshape(n_tile, 2, LANES), TILE_AXES).reshape(2 * n_tile, LANES)
    target = jnp.transpose(density_map.reshape(PLANE, EDGE))
    parts = exchange(splat(got, n_seg), "seg")
    pulled = pull(got, parts, target)
    back = exchange(pulled.reshape(n_tile, 4, LANES), TILE_AXES).reshape(4 * n_tile, LANES)
    near, far = ("core", "seg"), ("y", "z")
    forces, spread, score = finish(
        back, picks, modes, float(n_tile * EDGE**3), a_dev * n_tile * n_seg, lax.axis_size(near)
    )
    near_sum = jnp.sum(exchange(spread.reshape(-1, 2, LANES), near), axis=0)
    copies = jnp.broadcast_to(near_sum[None], (lax.axis_size(far), 2, LANES))
    mode_grad = jnp.sum(exchange(copies, far), axis=0).reshape(-1)
    return (forces, mode_grad, score[0, 0])


def solution(mesh):
    split = Mesh(mesh.devices.reshape(8, 8, 2, 4), TILE_AXES + ("seg",))
    every = TILE_AXES + ("seg",)
    return jax.shard_map(
        on_device,
        mesh=split,
        in_specs=(
            P(None, every),
            P(every),
            P(None, None, every),
            P(),
            P(TILE_AXES, None),
            P(every, None),
            P(every, None, None),
        ),
        out_specs=(P(None, every), P(), P()),
        check_vma=False,
    )
```

```python
import math

import jax
import jax.numpy as jnp
from jax import lax
from jax.experimental import pallas as pl
from jax.experimental.pallas import tpu as pltpu
from jax.sharding import Mesh
from jax.sharding import PartitionSpec as P

EDGE = 32
ATOM_BLOCK = 32
PLANE = EDGE * EDGE
LANES = 128
SPLAT_CHUNK = 512
PULL_CHUNK = 512
WIDTH = 256

inverse_var = 1.0 / 2.25
half_log = -0.5 * inverse_var / math.log(2.0)


def factors(places):
    centers = lax.broadcasted_iota(jnp.int32, (EDGE, places.shape[1]), 0).astype(jnp.float32) + 0.5
    distance = centers - places
    profile = jnp.exp2(half_log * (distance * distance))
    return profile, inverse_var * distance * profile


def exact_parts(values):
    high = values.astype(jnp.bfloat16)
    rest = values - high.astype(jnp.float32)
    middle = rest.astype(jnp.bfloat16)
    return high, middle, (rest - middle.astype(jnp.float32)).astype(jnp.bfloat16)


def against_rows(left, right):
    return lax.dot_general(
        left, right, (((1,), (1,)), ((), ())), preferred_element_type=jnp.float32
    )


def quarter_of(shape):
    return lax.broadcasted_iota(jnp.int32, shape, 1) // ATOM_BLOCK


def regroup(rows, target):
    quarter = quarter_of(rows[0].shape)
    result = jnp.zeros_like(rows[0])
    for i in range(4):
        moved = pltpu.roll(rows[i], ((i - target) % 4) * ATOM_BLOCK, 1) if i != target else rows[i]
        result = jnp.where(quarter == i, moved, result)
    return result


def pack_kernel(*refs):
    sources, (send_ref, pick_ref), (cell_ref, block_ref) = refs[:6], refs[6:8], refs[8:10]
    local, sems = refs[10:16], refs[16]
    copies = [
        pltpu.make_async_copy(source, place, sems.at[i])
        for i, (source, place) in enumerate(zip(sources, local))
    ]
    for copy in copies:
        copy.start()
    tiles_ref, offsets_ref, amps_ref, coords_ref, weights_ref, modes_ref = local
    n_tile = send_ref.shape[0] // 2
    blocks = block_ref.shape[0]
    cells = cell_ref.shape[1]
    for copy in copies[:2]:
        copy.wait()
    shape = (n_tile, blocks)
    tile_of_row = lax.broadcasted_iota(jnp.int32, shape, 0)
    row = lax.broadcasted_iota(jnp.int32, (blocks, blocks), 0)
    column = lax.broadcasted_iota(jnp.int32, (blocks, blocks), 1)
    before = jnp.where(row < column, 1.0, 0.0).astype(jnp.bfloat16)
    same = jnp.where(row == column, 1.0, 0.0).astype(jnp.bfloat16)
    ones = jnp.ones((blocks, blocks), jnp.bfloat16)
    seen = jnp.zeros(shape, jnp.float32)
    picks = [jnp.zeros(shape, jnp.float32) for _ in range(2)]
    shifts = [jnp.zeros((n_tile, LANES), jnp.float32) for _ in range(2)]
    for k in range(tiles_ref.shape[0]):
        named = jnp.where(tiles_ref[pl.ds(k, 1), :] == tile_of_row, 1.0, 0.0)
        flags = named.astype(jnp.bfloat16)
        rank = seen + jnp.dot(flags, before, preferred_element_type=jnp.float32)
        seen = seen + jnp.dot(flags, ones, preferred_element_type=jnp.float32)
        offsets = [
            jnp.broadcast_to(offsets_ref[c, pl.ds(k, 1), :].astype(jnp.float32), (ATOM_BLOCK, blocks))
            for c in range(3)
        ]
        offsets = jnp.concatenate(offsets + [jnp.zeros((ATOM_BLOCK, blocks), jnp.float32)], axis=0)
        for slot in range(2):
            mine = jnp.where(rank == float(slot), named, 0.0)
            picks[slot] = picks[slot] + mine
            shifts[slot] = shifts[slot] + against_rows(
                mine.astype(jnp.bfloat16), offsets.astype(jnp.bfloat16)
            )
    for copy in copies[2:]:
        copy.wait()
    amps = jnp.broadcast_to(amps_ref[...], (16, amps_ref.shape[1])).astype(jnp.bfloat16)
    for component in range(3):
        moved = jnp.dot(amps, modes_ref[component], preferred_element_type=jnp.float32)
        places = coords_ref[pl.ds(component, 1), :] + moved[0:1]
        for cell in range(cells):
            cell_ref[component, pl.ds(cell, 1), :] = places[:, cell * LANES : (cell + 1) * LANES]
    cell_ref[3] = weights_ref[...]
    for i in range(4):
        block_ref[pl.ds(i, cells, stride=4), :] = regroup([cell_ref[c] for c in range(4)], i)
    parts = exact_parts(block_ref[...])
    for slot in range(2):
        pick = picks[slot].astype(jnp.bfloat16)
        high, middle, low = [jnp.dot(pick, part, preferred_element_type=jnp.float32) for part in parts]
        send_ref[pl.ds(slot, n_tile, stride=2), :] = ((high + middle) + low) + shifts[slot]
        pick_ref[slot] = against_rows(same, pick).astype(jnp.bfloat16)


def finish_kernel(voxels, atoms, back_ref, pick_ref, modes_ref, forces_ref, spread_ref, score_ref, block_ref):
    n_tile = pick_ref.shape[2]
    lane = lax.broadcasted_iota(jnp.int32, (1, LANES), 1)
    totals = jnp.sum(back_ref[pl.ds(3, n_tile, stride=4), :], axis=0, keepdims=True)
    srm, srr, smm = [
        jnp.sum(jnp.where(lane == i, totals, 0.0), axis=1, keepdims=True) for i in range(3)
    ]
    root = jnp.sqrt(srr * smm)
    score = srm / root
    score_ref[...] = jnp.broadcast_to(score, score_ref.shape)
    map_scale = voxels / root
    model_scale = voxels * (score / srr)
    cells = forces_ref.shape[1] // LANES
    modes = jnp.zeros((1, modes_ref.shape[1]), jnp.float32)
    for component in range(3):
        pulled = back_ref[pl.ds(component, n_tile, stride=4), :]
        pulled = pulled * map_scale - pltpu.roll(pulled, LANES // 2, 1) * model_scale
        parts = exact_parts(pulled)
        first, second = [
            sum([jnp.dot(pick_ref[slot], part, preferred_element_type=jnp.float32) for part in parts[::-1]])
            for slot in range(2)
        ]
        block_ref[component] = first + pltpu.roll(second, LANES - ATOM_BLOCK, 1)
        rows = regroup([block_ref[component, pl.ds(i, cells, stride=4), :] for i in range(4)], 0)
        for cell in range(cells):
            forces_ref[pl.ds(component, 1), cell * LANES : (cell + 1) * LANES] = rows[cell : cell + 1]
        force = jnp.broadcast_to(forces_ref[pl.ds(component, 1), :], (16, forces_ref.shape[1]))
        modes = modes + against_rows(force.astype(jnp.bfloat16), modes_ref[component])[0:1]
    modes = modes / jnp.sqrt(jnp.float32(atoms))
    half = spread_ref.shape[0] // 2
    for part in range(2):
        spread_ref[pl.ds(part, half, stride=2), :] = jnp.broadcast_to(
            modes[:, part * LANES : (part + 1) * LANES], (half, LANES)
        )


def unpack_rows(got_ref, place_ref):
    groups = got_ref.shape[0] // 4
    rows = [got_ref[pl.ds(i, groups, stride=4), :] for i in range(4)]
    for component in range(4):
        place_ref[component] = regroup(rows, component)


def chunk_row(place_ref, component, chunk, size):
    rows = size // LANES
    return jnp.concatenate(
        [place_ref[component, pl.ds(chunk * rows + i, 1), :] for i in range(rows)], axis=1
    )


def pipeline(chunks, build, use):
    build(0, 0)

    @pl.loop(0, chunks // 2)
    def _(step):
        build(1, 2 * step + 1)
        use(0, 2 * step)
        build(0, jnp.minimum(2 * step + 2, chunks - 2))
        use(1, 2 * step + 1)


def build_plane(place_ref, line_ref, plane_ref, slot, chunk, size):
    along_x = factors(chunk_row(place_ref, 0, chunk, size))[0].astype(jnp.bfloat16)
    along_z = factors(chunk_row(place_ref, 2, chunk, size))[0].astype(jnp.bfloat16)
    line_ref[slot] = along_z.astype(jnp.float32)
    for z in range(EDGE):
        line = jnp.broadcast_to(line_ref[slot, pl.ds(z, 1), :], (EDGE, size))
        plane_ref[pl.ds(z * EDGE, EDGE), :] = line.astype(jnp.bfloat16) * along_x


def splat_kernel(got_ref, out_ref, place_ref, line_ref, weight_ref, plane_ref, sum_ref):
    size = plane_ref.shape[2]
    unpack_rows(got_ref, place_ref)
    sum_ref[...] = jnp.zeros_like(sum_ref)

    def build(slot, chunk):
        build_plane(place_ref, line_ref, plane_ref.at[slot], slot, chunk, size)
        along_y = factors(chunk_row(place_ref, 1, chunk, size))[0]
        weight_ref[slot] = (chunk_row(place_ref, 3, chunk, size) * along_y).astype(jnp.bfloat16)

    def use(slot, chunk):
        for half in range(2):
            rows = pl.ds(half * PLANE // 2, PLANE // 2)
            sum_ref[rows, :] += against_rows(plane_ref[slot, rows, :], weight_ref[slot])

    pipeline(place_ref.shape[1] * LANES // size, build, use)
    total = sum_ref[...].T
    for copy in range(out_ref.shape[0]):
        out_ref[copy] = total


middle = EDGE / 2


def voxel_centers():
    voxel = lax.broadcasted_iota(jnp.int32, (EDGE, PLANE), 1)
    return [part.astype(jnp.float32) + (0.5 - middle) for part in (voxel % EDGE, voxel // EDGE)]


def store_rows(row_ref, arrays):
    place = 0
    for values in arrays:
        terms = (values,) if values.dtype == jnp.bfloat16 else exact_parts(values)[:2]
        for term in terms:
            row_ref[place : place + EDGE] = term
            place += EDGE


def take_forces(sum_ref, chunk, sums, weights, places):
    plain, by_x, by_z = sums
    along_y, slope_y = [weight.astype(jnp.float32) for weight in weights]
    whole, force_y, moment_x, moment_z = [
        jnp.sum(values * weight, axis=0, keepdims=True)
        for values, weight in ((plain, along_y), (plain, slope_y), (by_x, along_y), (by_z, along_y))
    ]
    force_x = inverse_var * (moment_x - (places[0] - middle) * whole)
    force_z = inverse_var * (moment_z - (places[1] - middle) * whole)
    rows = whole.shape[1] // LANES
    for component, force in enumerate((force_x, force_y, force_z)):
        for i in range(rows):
            sum_ref[component, pl.ds(chunk * rows + i, 1), :] = force[:, i * LANES : (i + 1) * LANES]


def shape_kernel(got_ref, target_ref, even_ref, odd_ref, weight_ref, place_ref, sum_ref, line_ref, row_ref):
    planes = (even_ref, odd_ref)
    size = even_ref.shape[2]
    width = min(WIDTH, size)
    unpack_rows(got_ref, place_ref)
    wide = target_ref[...].astype(jnp.float32)
    center_x, center_z = voxel_centers()
    store_rows(row_ref, (target_ref[...], wide * center_x, wide * center_z))

    def build(slot, chunk):
        build_plane(place_ref, line_ref, planes[slot].at[chunk // 2], slot, chunk, size)
        profile_y, slope_y = factors(chunk_row(place_ref, 1, chunk, size))
        masses = chunk_row(place_ref, 3, chunk, size)
        weight_ref[slot, chunk // 2, 0] = (masses * profile_y).astype(jnp.bfloat16)
        weight_ref[slot, chunk // 2, 1] = (masses * slope_y).astype(jnp.bfloat16)

    def use(slot, chunk):
        for part in range(size // width):
            atoms = pl.ds(part * width, width)
            small = chunk * (size // width) + part
            pulled = jnp.dot(
                row_ref[...], planes[slot][chunk // 2, :, atoms], preferred_element_type=jnp.float32
            )
            block = [pulled[i * EDGE : (i + 1) * EDGE] for i in range(5)]
            take_forces(
                sum_ref,
                small,
                (block[0], block[1] + block[2], block[3] + block[4]),
                [weight_ref[slot, chunk // 2, i, :, atoms] for i in range(2)],
                [chunk_row(place_ref, i, small, width) for i in (0, 2)],
            )

    pipeline(place_ref.shape[1] * LANES // size, build, use)


def pull_kernel(parts_ref, target_ref, even_ref, odd_ref, weight_ref, place_ref, map_ref, out_ref, row_ref, sum_ref):
    planes = (even_ref, odd_ref)
    size = even_ref.shape[2]
    width = min(WIDTH, size)
    density = (parts_ref[0] + parts_ref[2]) + (parts_ref[1] + parts_ref[3])
    center_x, center_z = voxel_centers()
    store_rows(row_ref, (density, density * center_x, density * center_z))

    @pl.loop(0, even_ref.shape[0])
    def _(step):
        for slot in range(2):
            for part in range(size // width):
                atoms = pl.ds(part * width, width)
                small = (2 * step + slot) * (size // width) + part
                pulled = jnp.dot(
                    row_ref[...], planes[slot][step, :, atoms], preferred_element_type=jnp.float32
                )
                block = [pulled[i * EDGE : (i + 1) * EDGE] for i in range(6)]
                take_forces(
                    sum_ref,
                    small,
                    (block[0] + block[1], block[2] + block[3], block[4] + block[5]),
                    [weight_ref[slot, step, i, :, atoms] for i in range(2)],
                    [chunk_row(place_ref, i, small, width) for i in (0, 2)],
                )

    wide = target_ref[...].astype(jnp.float32)
    pairs = place_ref.shape[1]
    left = lax.broadcasted_iota(jnp.int32, (pairs, LANES), 1) < LANES // 2
    for component in range(3):
        first, second = map_ref[component], sum_ref[component]
        out_ref[pl.ds(component, pairs, stride=8), :] = jnp.where(
            left, first, pltpu.roll(second, LANES // 2, 1)
        )
        out_ref[pl.ds(4 + component, pairs, stride=8), :] = jnp.where(
            left, pltpu.roll(first, LANES // 2, 1), second
        )
    lane = lax.broadcasted_iota(jnp.int32, (2 * pairs, LANES), 1)
    totals = jnp.zeros((2 * pairs, LANES), jnp.float32)
    for place, product in enumerate((density * wide, density * density, wide * wide)):
        totals = jnp.where(lane == place, jnp.sum(product), totals)
    out_ref[pl.ds(3, 2 * pairs, stride=4), :] = totals


def call(kernel, name, out_shape, scratch, flops, *operands, source=pltpu.VMEM, limit=32):
    vmem = pl.BlockSpec(memory_space=pltpu.VMEM)
    return pl.pallas_call(
        kernel,
        out_shape=out_shape,
        in_specs=[pl.BlockSpec(memory_space=source)] * len(operands),
        out_specs=jax.tree.map(lambda _: vmem, out_shape),
        scratch_shapes=[pltpu.VMEM(*entry) if isinstance(entry, tuple) else entry for entry in scratch],
        compiler_params=pltpu.CompilerParams(vmem_limit_bytes=limit * 2**20),
        cost_estimate=pl.CostEstimate(flops=flops, bytes_accessed=2**20, transcendentals=2**20),
        name=name,
    )(*operands)


def pack(coords, weights, modes, amplitudes, tiles, offsets, n_tile):
    blocks = tiles.shape[1]
    operands = (tiles, offsets, amplitudes, coords, weights, modes)
    return call(
        pack_kernel,
        "pack",
        (
            jax.ShapeDtypeStruct((2 * n_tile, LANES), jnp.float32),
            jax.ShapeDtypeStruct((2, blocks, n_tile), jnp.bfloat16),
        ),
        [((4, weights.shape[0], LANES), jnp.float32), ((blocks, LANES), jnp.float32)]
        + [(operand.shape, operand.dtype) for operand in operands]
        + [pltpu.SemaphoreType.DMA((len(operands),))],
        2**26,
        *operands,
        source=pltpu.HBM,
        limit=60,
    )


def finish(back, picks, modes, voxels, atoms, copies):
    blocks = picks.shape[1]
    return call(
        lambda *refs: finish_kernel(voxels, atoms, *refs),
        "finish",
        (
            jax.ShapeDtypeStruct((3, modes.shape[2]), jnp.float32),
            jax.ShapeDtypeStruct((2 * copies, LANES), jnp.float32),
            jax.ShapeDtypeStruct((1, LANES), jnp.float32),
        ),
        [((3, blocks, LANES), jnp.float32)],
        2**26,
        back,
        picks,
        modes,
    )


def splat(got, copies):
    groups = got.shape[0] // 4
    size = min(SPLAT_CHUNK, groups * LANES // 2)
    return call(
        splat_kernel,
        "splat",
        jax.ShapeDtypeStruct((copies, EDGE, PLANE), jnp.float32),
        [
            ((4, groups, LANES), jnp.float32),
            ((2, EDGE, size), jnp.float32),
            ((2, EDGE, size), jnp.bfloat16),
            ((2, PLANE, size), jnp.bfloat16),
            ((PLANE, EDGE), jnp.float32),
        ],
        2**29,
        got,
    )


def shape(got, target):
    groups = got.shape[0] // 4
    atoms = groups * LANES
    size = min(PULL_CHUNK, atoms // 2)
    chunks = atoms // size
    plane = pltpu.VMEM((chunks // 2, PLANE, size), jnp.bfloat16)
    return call(
        shape_kernel,
        "shape",
        (
            plane,
            plane,
            pltpu.VMEM((2, chunks // 2, 2, EDGE, size), jnp.bfloat16),
            pltpu.VMEM((4, groups, LANES), jnp.float32),
            pltpu.VMEM((3, groups, LANES), jnp.float32),
        ),
        [
            ((2, EDGE, size), jnp.float32),
            ((5 * EDGE, PLANE), jnp.bfloat16),
        ],
        2**32,
        got,
        target,
        limit=8,
    )


def pull(parts, target, shapes):
    groups = shapes[3].shape[1]
    return call(
        pull_kernel,
        "pull",
        jax.ShapeDtypeStruct((8 * groups, LANES), jnp.float32),
        [
            ((6 * EDGE, PLANE), jnp.bfloat16),
            ((3, groups, LANES), jnp.float32),
        ],
        2**32,
        parts,
        target,
        *shapes,
        limit=8,
    )


TILE_AXES = ("y", "z", "core")


def exchange(values, axes):
    return lax.all_to_all(values, axes, split_axis=0, concat_axis=0, tiled=True)


def on_device(coords, weights, mode_vectors, amplitudes, density_map, block_tiles, block_offsets):
    a_dev = coords.shape[1]
    n_tile = lax.axis_size(TILE_AXES)
    n_seg = lax.axis_size("seg")
    modes = jnp.transpose(mode_vectors, (1, 0, 2))
    send, picks = pack(
        coords,
        weights.reshape(a_dev // LANES, LANES),
        modes,
        amplitudes.reshape(1, -1),
        block_tiles.T,
        jnp.transpose(block_offsets, (2, 1, 0)),
        n_tile,
    )
    got = exchange(send.reshape(n_tile, 2, LANES), TILE_AXES).reshape(2 * n_tile, LANES)
    target = jnp.transpose(density_map.reshape(PLANE, EDGE))
    parts = exchange(splat(got, n_seg), "seg")
    pulled = pull(parts, target, shape(got, target))
    back = exchange(pulled.reshape(n_tile, 4, LANES), TILE_AXES).reshape(4 * n_tile, LANES)
    near, far = ("z", "core"), ("y", "seg")
    forces, spread, score = finish(
        back, picks, modes, float(n_tile * EDGE**3), a_dev * n_tile * n_seg, lax.axis_size(near)
    )
    near_sum = jnp.sum(exchange(spread.reshape(-1, 2, LANES), near), axis=0)
    copies = jnp.broadcast_to(near_sum[None], (lax.axis_size(far), 2, LANES))
    mode_grad = jnp.sum(exchange(copies, far), axis=0).reshape(-1)
    return (forces, mode_grad, score[0, 0])


def solution(mesh):
    split = Mesh(mesh.devices.reshape(8, 8, 2, 4), TILE_AXES + ("seg",))
    every = TILE_AXES + ("seg",)
    return jax.shard_map(
        on_device,
        mesh=split,
        in_specs=(
            P(None, every),
            P(every),
            P(None, None, every),
            P(),
            P(TILE_AXES, None),
            P(every, None),
            P(every, None, None),
        ),
        out_specs=(P(None, every), P(), P()),
        check_vma=False,
    )
```

```python
import math

import jax
import jax.numpy as jnp
from jax import lax
from jax.experimental import pallas as pl
from jax.experimental.pallas import tpu as pltpu
from jax.sharding import Mesh
from jax.sharding import PartitionSpec as P

EDGE = 32
ATOM_BLOCK = 32
PLANE = EDGE * EDGE
LANES = 128
CHUNK = 512
WIDTH = 256

STEP = 4
HIGHS = EDGE // STEP
MIDDLE = EDGE / 2
FAR = 40.0

inverse_var = 1.0 / 2.25
rate = 0.5 * inverse_var / math.log(2.0)


def row_number(rows, columns):
    return lax.broadcasted_iota(jnp.int32, (rows, columns), 0)


def factors(places, centers):
    distance = centers - places
    profile = jnp.exp2(-rate * (distance * distance))
    return profile, inverse_var * distance * profile


def centers_of(columns):
    return row_number(EDGE, columns).astype(jnp.float32) + 0.5


def exact_parts(values):
    high = values.astype(jnp.bfloat16)
    rest = values - high.astype(jnp.float32)
    middle = rest.astype(jnp.bfloat16)
    return high, middle, (rest - middle.astype(jnp.float32)).astype(jnp.bfloat16)


def against_rows(left, right):
    return lax.dot_general(
        left, right, (((1,), (1,)), ((), ())), preferred_element_type=jnp.float32
    )


def quarter_of(shape):
    return lax.broadcasted_iota(jnp.int32, shape, 1) // ATOM_BLOCK


def regroup(rows, target):
    quarter = quarter_of(rows[0].shape)
    result = jnp.zeros_like(rows[0])
    for i in range(4):
        moved = pltpu.roll(rows[i], ((i - target) % 4) * ATOM_BLOCK, 1) if i != target else rows[i]
        result = jnp.where(quarter == i, moved, result)
    return result


def pack_kernel(*refs):
    sources, (send_ref, pick_ref), (cell_ref, block_ref) = refs[:6], refs[6:8], refs[8:10]
    local, sems = refs[10:16], refs[16]
    copies = [
        pltpu.make_async_copy(source, place, sems.at[i])
        for i, (source, place) in enumerate(zip(sources, local))
    ]
    for copy in copies:
        copy.start()
    tiles_ref, offsets_ref, amps_ref, coords_ref, weights_ref, modes_ref = local
    n_tile = send_ref.shape[0] // 2
    blocks = block_ref.shape[0]
    cells = cell_ref.shape[1]
    for copy in copies[:2]:
        copy.wait()
    shape = (n_tile, blocks)
    tile_of_row = lax.broadcasted_iota(jnp.int32, shape, 0)
    row = lax.broadcasted_iota(jnp.int32, (blocks, blocks), 0)
    column = lax.broadcasted_iota(jnp.int32, (blocks, blocks), 1)
    before = jnp.where(row < column, 1.0, 0.0).astype(jnp.bfloat16)
    same = jnp.where(row == column, 1.0, 0.0).astype(jnp.bfloat16)
    ones = jnp.ones((blocks, blocks), jnp.bfloat16)
    seen = jnp.zeros(shape, jnp.float32)
    picks = [jnp.zeros(shape, jnp.float32) for _ in range(2)]
    shifts = [jnp.zeros((n_tile, LANES), jnp.float32) for _ in range(2)]
    for k in range(tiles_ref.shape[0]):
        named = jnp.where(tiles_ref[pl.ds(k, 1), :] == tile_of_row, 1.0, 0.0)
        flags = named.astype(jnp.bfloat16)
        rank = seen + jnp.dot(flags, before, preferred_element_type=jnp.float32)
        seen = seen + jnp.dot(flags, ones, preferred_element_type=jnp.float32)
        offsets = [
            jnp.broadcast_to(offsets_ref[c, pl.ds(k, 1), :].astype(jnp.float32), (ATOM_BLOCK, blocks))
            for c in range(3)
        ]
        offsets = jnp.concatenate(offsets + [jnp.zeros((ATOM_BLOCK, blocks), jnp.float32)], axis=0)
        for slot in range(2):
            mine = jnp.where(rank == float(slot), named, 0.0)
            picks[slot] = picks[slot] + mine
            shifts[slot] = shifts[slot] + against_rows(
                mine.astype(jnp.bfloat16), offsets.astype(jnp.bfloat16)
            )
    for copy in copies[2:]:
        copy.wait()
    amps = jnp.broadcast_to(amps_ref[...], (16, amps_ref.shape[1])).astype(jnp.bfloat16)
    for component in range(3):
        moved = jnp.dot(amps, modes_ref[component], preferred_element_type=jnp.float32)
        places = coords_ref[pl.ds(component, 1), :] + moved[0:1]
        for cell in range(cells):
            cell_ref[component, pl.ds(cell, 1), :] = places[:, cell * LANES : (cell + 1) * LANES]
    cell_ref[3] = weights_ref[...]
    for i in range(4):
        block_ref[pl.ds(i, cells, stride=4), :] = regroup([cell_ref[c] for c in range(4)], i)
    parts = exact_parts(block_ref[...])
    for slot in range(2):
        pick = picks[slot].astype(jnp.bfloat16)
        high, middle, low = [jnp.dot(pick, part, preferred_element_type=jnp.float32) for part in parts]
        send_ref[pl.ds(slot, n_tile, stride=2), :] = ((high + middle) + low) + shifts[slot]
        pick_ref[slot] = against_rows(same, pick).astype(jnp.bfloat16)


def finish_kernel(voxels, atoms, back_ref, pick_ref, modes_ref, forces_ref, spread_ref, score_ref, block_ref):
    n_tile = pick_ref.shape[2]
    lane = lax.broadcasted_iota(jnp.int32, (1, LANES), 1)
    totals = jnp.sum(back_ref[pl.ds(3, n_tile, stride=4), :], axis=0, keepdims=True)
    srm, srr, smm = [
        jnp.sum(jnp.where(lane == i, totals, 0.0), axis=1, keepdims=True) for i in range(3)
    ]
    root = jnp.sqrt(srr * smm)
    score = srm / root
    score_ref[...] = jnp.broadcast_to(score, score_ref.shape)
    map_scale = voxels / root
    model_scale = voxels * (score / srr)
    cells = forces_ref.shape[1] // LANES
    modes = jnp.zeros((1, modes_ref.shape[1]), jnp.float32)
    for component in range(3):
        pulled = back_ref[pl.ds(component, n_tile, stride=4), :]
        pulled = pulled * map_scale - pltpu.roll(pulled, LANES // 2, 1) * model_scale
        parts = exact_parts(pulled)
        first, second = [
            sum([jnp.dot(pick_ref[slot], part, preferred_element_type=jnp.float32) for part in parts[::-1]])
            for slot in range(2)
        ]
        block_ref[component] = first + pltpu.roll(second, LANES - ATOM_BLOCK, 1)
        rows = regroup([block_ref[component, pl.ds(i, cells, stride=4), :] for i in range(4)], 0)
        for cell in range(cells):
            forces_ref[pl.ds(component, 1), cell * LANES : (cell + 1) * LANES] = rows[cell : cell + 1]
        force = jnp.broadcast_to(forces_ref[pl.ds(component, 1), :], (16, forces_ref.shape[1]))
        modes = modes + against_rows(force.astype(jnp.bfloat16), modes_ref[component])[0:1]
    modes = modes / jnp.sqrt(jnp.float32(atoms))
    half = spread_ref.shape[0] // 2
    for part in range(2):
        spread_ref[pl.ds(part, half, stride=2), :] = jnp.broadcast_to(
            modes[:, part * LANES : (part + 1) * LANES], (half, LANES)
        )


def unpack_rows(got_ref, place_ref):
    groups = got_ref.shape[0] // 4
    rows = [got_ref[pl.ds(i, groups, stride=4), :] for i in range(4)]
    for component in range(4):
        place_ref[component] = regroup(rows, component)


def chunk_row(place_ref, component, chunk, size):
    rows = size // LANES
    return jnp.concatenate(
        [place_ref[component, pl.ds(chunk * rows + i, 1), :] for i in range(rows)], axis=1
    )


def pipeline(chunks, build, use):
    build(0, 0)

    @pl.loop(0, chunks // 2)
    def _(step):
        build(1, 2 * step + 1)
        use(0, 2 * step)
        build(0, jnp.minimum(2 * step + 2, chunks - 2))
        use(1, 2 * step + 1)


def pair_of_lines(line_ref, z, size):
    return jnp.concatenate(
        [jnp.broadcast_to(line_ref[pl.ds(z + i, 1), :], (HIGHS, size)) for i in range(2)], axis=0
    )


def splat_kernel(got_ref, out_ref, place_ref, line_ref, even_ref, odd_ref, even_weight_ref, odd_weight_ref, sum_ref):
    size = even_ref.shape[1]
    planes, weights = (even_ref, odd_ref), (even_weight_ref, odd_weight_ref)
    unpack_rows(got_ref, place_ref)
    sum_ref[...] = jnp.zeros_like(sum_ref)
    lows = [low + 0.5 - STEP / 2 for low in range(STEP)]

    def build(slot, chunk):
        place_x, place_y, place_z, masses = [chunk_row(place_ref, i, chunk, size) for i in range(4)]
        place_x = place_x - MIDDLE
        coarse = STEP * row_number(HIGHS, size).astype(jnp.float32) + (STEP / 2 - MIDDLE)
        along_x = factors(place_x, coarse)[0]
        line_ref[slot] = factors(place_z, centers_of(size))[0]
        for z in range(0, EDGE, 2):
            line = pair_of_lines(line_ref.at[slot], z, size)
            block = line * jnp.concatenate([along_x, along_x], axis=0)
            planes[slot][pl.ds(z * HIGHS, 2 * HIGHS), :] = block.astype(jnp.bfloat16)
        along_y = masses * factors(place_y, centers_of(size))[0]
        near = jnp.clip(place_x, -FAR, FAR)
        for low in range(STEP):
            fine = jnp.exp2((2.0 * rate * lows[low]) * near)
            weights[slot][pl.ds(low * EDGE, EDGE), :] = (along_y * fine).astype(jnp.bfloat16)

    def use(slot, chunk):
        width = min(WIDTH, size)
        for part in range(size // width):
            atoms = pl.ds(part * width, width)
            sum_ref[...] += against_rows(planes[slot][:, atoms], weights[slot][:, atoms])

    pipeline(place_ref.shape[1] * LANES // size, build, use)
    total = sum_ref[...].T
    high = (lax.broadcasted_iota(jnp.int32, (EDGE, EDGE * HIGHS), 1) % HIGHS).astype(jnp.float32)
    coarse = STEP * high + (STEP / 2 - MIDDLE)
    for low in range(STEP):
        scale = jnp.exp2(-rate * (2.0 * lows[low] * coarse + lows[low] ** 2))
        block = total[low * EDGE : (low + 1) * EDGE] * scale
        for copy in range(out_ref.shape[0]):
            out_ref[copy, :, pl.ds(low * EDGE * HIGHS, EDGE * HIGHS)] = block


def build_shape(place_ref, line_ref, plane_ref, weight_ref, chunk, size):
    place_x, place_y, place_z, masses = [chunk_row(place_ref, i, chunk, size) for i in range(4)]
    row = row_number(EDGE, size)
    centers = (STEP * (row % HIGHS) + row // HIGHS).astype(jnp.float32) + 0.5
    along_x = factors(place_x, centers)[0]
    doubled = []
    for low in range(STEP):
        block = along_x[low * HIGHS : (low + 1) * HIGHS]
        doubled.append(jnp.concatenate([block, block], axis=0).astype(jnp.bfloat16))
    line_ref[...] = factors(place_z, centers_of(size))[0].astype(jnp.bfloat16).astype(jnp.float32)
    for z in range(0, EDGE, 2):
        line = pair_of_lines(line_ref, z, size).astype(jnp.bfloat16)
        for low in range(STEP):
            plane_ref[pl.ds(low * EDGE * HIGHS + z * HIGHS, 2 * HIGHS), :] = line * doubled[low]
    profile_y, slope_y = factors(place_y, centers_of(size))
    weight_ref[0] = (masses * profile_y).astype(jnp.bfloat16).astype(jnp.float32)
    weight_ref[1] = (masses * slope_y).astype(jnp.bfloat16).astype(jnp.float32)


def voxel_centers():
    voxel = lax.broadcasted_iota(jnp.int32, (EDGE, PLANE), 1)
    low, z, high = voxel // (EDGE * HIGHS), voxel // HIGHS % EDGE, voxel % HIGHS
    return [part.astype(jnp.float32) + (0.5 - MIDDLE) for part in (STEP * high + low, z)]


def store_rows(row_ref, arrays):
    place = 0
    for values in arrays:
        terms = (values,) if values.dtype == jnp.bfloat16 else exact_parts(values)[:2]
        for term in terms:
            row_ref[place : place + EDGE] = term
            place += EDGE


def take_forces(sum_ref, chunk, sums, weights, places):
    plain, by_x, by_z = sums
    along_y, slope_y = weights
    whole, force_y, moment_x, moment_z = [
        jnp.sum(values * weight, axis=0, keepdims=True)
        for values, weight in ((plain, along_y), (plain, slope_y), (by_x, along_y), (by_z, along_y))
    ]
    force_x = inverse_var * (moment_x - (places[0] - MIDDLE) * whole)
    force_z = inverse_var * (moment_z - (places[1] - MIDDLE) * whole)
    rows = whole.shape[1] // LANES
    for component, force in enumerate((force_x, force_y, force_z)):
        for i in range(rows):
            sum_ref[component, pl.ds(chunk * rows + i, 1), :] = force[:, i * LANES : (i + 1) * LANES]


def pull_rows(single, place_ref, row_ref, sum_ref, line_ref, even_ref, odd_ref, weight_ref):
    planes = (even_ref, odd_ref)
    size = even_ref.shape[1]
    width = min(WIDTH, size)

    def build(slot, chunk):
        build_shape(place_ref, line_ref.at[slot], planes[slot], weight_ref.at[slot], chunk, size)

    def use(slot, chunk):
        for part in range(size // width):
            atoms = pl.ds(part * width, width)
            small = chunk * (size // width) + part
            pulled = jnp.dot(row_ref[...], planes[slot][:, atoms], preferred_element_type=jnp.float32)
            block = [pulled[i : i + EDGE] for i in range(0, pulled.shape[0], EDGE)]
            plain = block[0] if single else block[0] + block[1]
            block = block[1:] if single else block[2:]
            take_forces(
                sum_ref,
                small,
                (plain, block[0] + block[1], block[2] + block[3]),
                [weight_ref[slot, i, :, atoms] for i in range(2)],
                [chunk_row(place_ref, i, small, width) for i in (0, 2)],
            )

    pipeline(place_ref.shape[1] * LANES // size, build, use)


def map_kernel(got_ref, target_ref, sum_ref, place_ref, row_ref, *scratch):
    unpack_rows(got_ref, place_ref)
    wide = target_ref[...].astype(jnp.float32)
    center_x, center_z = voxel_centers()
    store_rows(row_ref, (target_ref[...], wide * center_x, wide * center_z))
    pull_rows(True, place_ref, row_ref, sum_ref, *scratch)


def pull_kernel(got_ref, parts_ref, target_ref, map_ref, out_ref, place_ref, row_ref, sum_ref, *scratch):
    unpack_rows(got_ref, place_ref)
    density = (parts_ref[0] + parts_ref[2]) + (parts_ref[1] + parts_ref[3])
    center_x, center_z = voxel_centers()
    store_rows(row_ref, (density, density * center_x, density * center_z))
    pull_rows(False, place_ref, row_ref, sum_ref, *scratch)
    wide = target_ref[...].astype(jnp.float32)
    pairs = place_ref.shape[1]
    left = lax.broadcasted_iota(jnp.int32, (pairs, LANES), 1) < LANES // 2
    for component in range(3):
        first, second = map_ref[component], sum_ref[component]
        out_ref[pl.ds(component, pairs, stride=8), :] = jnp.where(
            left, first, pltpu.roll(second, LANES // 2, 1)
        )
        out_ref[pl.ds(4 + component, pairs, stride=8), :] = jnp.where(
            left, pltpu.roll(first, LANES // 2, 1), second
        )
    lane = lax.broadcasted_iota(jnp.int32, (2 * pairs, LANES), 1)
    totals = jnp.zeros((2 * pairs, LANES), jnp.float32)
    for place, product in enumerate((density * wide, density * density, wide * wide)):
        totals = jnp.where(lane == place, jnp.sum(product), totals)
    out_ref[pl.ds(3, 2 * pairs, stride=4), :] = totals


def call(kernel, name, out_shape, scratch, flops, *operands, source=pltpu.VMEM, limit=32):
    vmem = pl.BlockSpec(memory_space=pltpu.VMEM)
    return pl.pallas_call(
        kernel,
        out_shape=out_shape,
        in_specs=[pl.BlockSpec(memory_space=source)] * len(operands),
        out_specs=jax.tree.map(lambda _: vmem, out_shape),
        scratch_shapes=[pltpu.VMEM(*entry) if isinstance(entry, tuple) else entry for entry in scratch],
        compiler_params=pltpu.CompilerParams(vmem_limit_bytes=limit * 2**20),
        cost_estimate=pl.CostEstimate(flops=flops, bytes_accessed=2**20, transcendentals=2**20),
        name=name,
    )(*operands)


def pack(coords, weights, modes, amplitudes, tiles, offsets, n_tile):
    blocks = tiles.shape[1]
    operands = (tiles, offsets, amplitudes, coords, weights, modes)
    return call(
        pack_kernel,
        "pack",
        (
            jax.ShapeDtypeStruct((2 * n_tile, LANES), jnp.float32),
            jax.ShapeDtypeStruct((2, blocks, n_tile), jnp.bfloat16),
        ),
        [((4, weights.shape[0], LANES), jnp.float32), ((blocks, LANES), jnp.float32)]
        + [(operand.shape, operand.dtype) for operand in operands]
        + [pltpu.SemaphoreType.DMA((len(operands),))],
        2**26,
        *operands,
        source=pltpu.HBM,
        limit=60,
    )


def finish(back, picks, modes, voxels, atoms, copies):
    blocks = picks.shape[1]
    return call(
        lambda *refs: finish_kernel(voxels, atoms, *refs),
        "finish",
        (
            jax.ShapeDtypeStruct((3, modes.shape[2]), jnp.float32),
            jax.ShapeDtypeStruct((2 * copies, LANES), jnp.float32),
            jax.ShapeDtypeStruct((1, LANES), jnp.float32),
        ),
        [((3, blocks, LANES), jnp.float32)],
        2**26,
        back,
        picks,
        modes,
    )


def splat(got, copies):
    groups = got.shape[0] // 4
    size = min(CHUNK, groups * LANES // 2)
    plane = ((EDGE * HIGHS, size), jnp.bfloat16)
    weight = ((EDGE * STEP, size), jnp.bfloat16)
    return call(
        splat_kernel,
        "splat",
        jax.ShapeDtypeStruct((copies, EDGE, PLANE), jnp.float32),
        [
            ((4, groups, LANES), jnp.float32),
            ((2, EDGE, size), jnp.float32),
            plane,
            plane,
            weight,
            weight,
            ((EDGE * HIGHS, EDGE * STEP), jnp.float32),
        ],
        2**29,
        got,
    )


def shape_scratch(groups):
    size = min(CHUNK, groups * LANES // 2)
    plane = ((PLANE, size), jnp.bfloat16)
    return [((2, EDGE, size), jnp.float32), plane, plane, ((2, 2, EDGE, size), jnp.float32)]


def pull_map(got, target):
    groups = got.shape[0] // 4
    return call(
        map_kernel,
        "pull_map",
        jax.ShapeDtypeStruct((3, groups, LANES), jnp.float32),
        [((4, groups, LANES), jnp.float32), ((5 * EDGE, PLANE), jnp.bfloat16)] + shape_scratch(groups),
        2**32,
        got,
        target,
    )


def pull(got, parts, target, from_map):
    groups = got.shape[0] // 4
    return call(
        pull_kernel,
        "pull",
        jax.ShapeDtypeStruct((8 * groups, LANES), jnp.float32),
        [
            ((4, groups, LANES), jnp.float32),
            ((6 * EDGE, PLANE), jnp.bfloat16),
            ((3, groups, LANES), jnp.float32),
        ]
        + shape_scratch(groups),
        2**32,
        got,
        parts,
        target,
        from_map,
    )


TILE_AXES = ("y", "z", "core")


def exchange(values, axes):
    return lax.all_to_all(values, axes, split_axis=0, concat_axis=0, tiled=True)


def on_device(coords, weights, mode_vectors, amplitudes, density_map, block_tiles, block_offsets):
    a_dev = coords.shape[1]
    n_tile = lax.axis_size(TILE_AXES)
    n_seg = lax.axis_size("seg")
    modes = jnp.transpose(mode_vectors, (1, 0, 2))
    send, picks = pack(
        coords,
        weights.reshape(a_dev // LANES, LANES),
        modes,
        amplitudes.reshape(1, -1),
        block_tiles.T,
        jnp.transpose(block_offsets, (2, 1, 0)),
        n_tile,
    )
    got = exchange(send.reshape(n_tile, 2, LANES), TILE_AXES).reshape(2 * n_tile, LANES)
    target = density_map.reshape(EDGE, HIGHS, STEP, EDGE)
    target = jnp.transpose(target, (3, 2, 0, 1)).reshape(EDGE, PLANE)
    parts = exchange(splat(got, n_seg), "seg")
    pulled = pull(got, parts, target, pull_map(got, target))
    back = exchange(pulled.reshape(n_tile, 4, LANES), TILE_AXES).reshape(4 * n_tile, LANES)
    near, far = ("z", "core"), ("y", "seg")
    forces, spread, score = finish(
        back, picks, modes, float(n_tile * EDGE**3), a_dev * n_tile * n_seg, lax.axis_size(near)
    )
    near_sum = jnp.sum(exchange(spread.reshape(-1, 2, LANES), near), axis=0)
    copies = jnp.broadcast_to(near_sum[None], (lax.axis_size(far), 2, LANES))
    mode_grad = jnp.sum(exchange(copies, far), axis=0).reshape(-1)
    return (forces, mode_grad, score[0, 0])


def solution(mesh):
    split = Mesh(mesh.devices.reshape(8, 8, 2, 4), TILE_AXES + ("seg",))
    every = TILE_AXES + ("seg",)
    return jax.shard_map(
        on_device,
        mesh=split,
        in_specs=(
            P(None, every),
            P(every),
            P(None, None, every),
            P(),
            P(TILE_AXES, None),
            P(every, None),
            P(every, None, None),
        ),
        out_specs=(P(None, every), P(), P()),
        check_vma=False,
    )
```

```python
import math

import jax
import jax.numpy as jnp
from jax import lax
from jax.experimental import pallas as pl
from jax.experimental.pallas import tpu as pltpu
from jax.sharding import Mesh
from jax.sharding import PartitionSpec as P

EDGE = 32
ATOM_BLOCK = 32
PLANE = EDGE * EDGE
LANES = 128
CHUNK = 512
WIDTH = 256

STEP = 4
HIGHS = EDGE // STEP
MIDDLE = EDGE / 2
FAR = 40.0

inverse_var = 1.0 / 2.25
rate = 0.5 * inverse_var / math.log(2.0)


def row_number(rows, columns):
    return lax.broadcasted_iota(jnp.int32, (rows, columns), 0)


def factors(places, centers):
    distance = centers - places
    profile = jnp.exp2(-rate * (distance * distance))
    return profile, inverse_var * distance * profile


def centers_of(columns):
    return row_number(EDGE, columns).astype(jnp.float32) + 0.5


def exact_parts(values):
    high = values.astype(jnp.bfloat16)
    rest = values - high.astype(jnp.float32)
    middle = rest.astype(jnp.bfloat16)
    return high, middle, (rest - middle.astype(jnp.float32)).astype(jnp.bfloat16)


def against_rows(left, right):
    return lax.dot_general(
        left, right, (((1,), (1,)), ((), ())), preferred_element_type=jnp.float32
    )


def quarter_of(shape):
    return lax.broadcasted_iota(jnp.int32, shape, 1) // ATOM_BLOCK


def regroup(rows, target):
    quarter = quarter_of(rows[0].shape)
    result = jnp.zeros_like(rows[0])
    for i in range(4):
        moved = pltpu.roll(rows[i], ((i - target) % 4) * ATOM_BLOCK, 1) if i != target else rows[i]
        result = jnp.where(quarter == i, moved, result)
    return result


def pack_kernel(*refs):
    sources, (send_ref, pick_ref), (cell_ref, block_ref) = refs[:6], refs[6:8], refs[8:10]
    local, sems = refs[10:16], refs[16]
    copies = [
        pltpu.make_async_copy(source, place, sems.at[i])
        for i, (source, place) in enumerate(zip(sources, local))
    ]
    for copy in copies:
        copy.start()
    tiles_ref, offsets_ref, amps_ref, coords_ref, weights_ref, modes_ref = local
    n_tile = send_ref.shape[0] // 2
    blocks = block_ref.shape[0]
    cells = cell_ref.shape[1]
    for copy in copies[:2]:
        copy.wait()
    shape = (n_tile, blocks)
    tile_of_row = lax.broadcasted_iota(jnp.int32, shape, 0)
    row = lax.broadcasted_iota(jnp.int32, (blocks, blocks), 0)
    column = lax.broadcasted_iota(jnp.int32, (blocks, blocks), 1)
    before = jnp.where(row < column, 1.0, 0.0).astype(jnp.bfloat16)
    same = jnp.where(row == column, 1.0, 0.0).astype(jnp.bfloat16)
    ones = jnp.ones((blocks, blocks), jnp.bfloat16)
    seen = jnp.zeros(shape, jnp.float32)
    picks = [jnp.zeros(shape, jnp.float32) for _ in range(2)]
    shifts = [jnp.zeros((n_tile, LANES), jnp.float32) for _ in range(2)]
    for k in range(tiles_ref.shape[0]):
        named = jnp.where(tiles_ref[pl.ds(k, 1), :] == tile_of_row, 1.0, 0.0)
        flags = named.astype(jnp.bfloat16)
        rank = seen + jnp.dot(flags, before, preferred_element_type=jnp.float32)
        seen = seen + jnp.dot(flags, ones, preferred_element_type=jnp.float32)
        offsets = [
            jnp.broadcast_to(offsets_ref[c, pl.ds(k, 1), :].astype(jnp.float32), (ATOM_BLOCK, blocks))
            for c in range(3)
        ]
        offsets = jnp.concatenate(offsets + [jnp.zeros((ATOM_BLOCK, blocks), jnp.float32)], axis=0)
        for slot in range(2):
            mine = jnp.where(rank == float(slot), named, 0.0)
            picks[slot] = picks[slot] + mine
            shifts[slot] = shifts[slot] + against_rows(
                mine.astype(jnp.bfloat16), offsets.astype(jnp.bfloat16)
            )
    for copy in copies[2:]:
        copy.wait()
    amps = jnp.broadcast_to(amps_ref[...], (16, amps_ref.shape[1])).astype(jnp.bfloat16)
    for component in range(3):
        moved = jnp.dot(amps, modes_ref[component], preferred_element_type=jnp.float32)
        places = coords_ref[pl.ds(component, 1), :] + moved[0:1]
        for cell in range(cells):
            cell_ref[component, pl.ds(cell, 1), :] = places[:, cell * LANES : (cell + 1) * LANES]
    cell_ref[3] = weights_ref[...]
    for i in range(4):
        block_ref[pl.ds(i, cells, stride=4), :] = regroup([cell_ref[c] for c in range(4)], i)
    parts = exact_parts(block_ref[...])
    for slot in range(2):
        pick = picks[slot].astype(jnp.bfloat16)
        high, middle, low = [jnp.dot(pick, part, preferred_element_type=jnp.float32) for part in parts]
        send_ref[pl.ds(slot, n_tile, stride=2), :] = ((high + middle) + low) + shifts[slot]
        pick_ref[slot] = against_rows(same, pick).astype(jnp.bfloat16)


def finish_kernel(voxels, atoms, back_ref, pick_ref, modes_ref, forces_ref, spread_ref, score_ref, wide_ref, block_ref):
    n_tile = pick_ref.shape[2]
    wide_ref[...] = back_ref[...].astype(jnp.float32)
    last = wide_ref[pl.ds(3, n_tile, stride=4), :]
    place = lax.broadcasted_iota(jnp.int32, (n_tile, LANES), 1) // 3
    ratio = jnp.sum(jnp.where(place == 3, last, 0.0), axis=1, keepdims=True)
    totals = jnp.sum(last, axis=0, keepdims=True)
    srm, srr, smm = [
        jnp.sum(jnp.where(place[0:1] == i, totals, 0.0), axis=1, keepdims=True) for i in range(3)
    ]
    root = jnp.sqrt(srr * smm)
    score = srm / root
    score_ref[...] = jnp.broadcast_to(score, score_ref.shape)
    map_scale = voxels / root
    model_scale = map_scale * (ratio - srm / srr)
    cells = forces_ref.shape[1] // LANES
    modes = jnp.zeros((1, modes_ref.shape[1]), jnp.float32)
    for component in range(3):
        pulled = wide_ref[pl.ds(component, n_tile, stride=4), :]
        pulled = pulled * map_scale + pltpu.roll(pulled, LANES // 2, 1) * model_scale
        parts = exact_parts(pulled)
        first, second = [
            sum([jnp.dot(pick_ref[slot], part, preferred_element_type=jnp.float32) for part in parts[::-1]])
            for slot in range(2)
        ]
        block_ref[component] = first + pltpu.roll(second, LANES - ATOM_BLOCK, 1)
        rows = regroup([block_ref[component, pl.ds(i, cells, stride=4), :] for i in range(4)], 0)
        for cell in range(cells):
            forces_ref[pl.ds(component, 1), cell * LANES : (cell + 1) * LANES] = rows[cell : cell + 1]
        force = jnp.broadcast_to(forces_ref[pl.ds(component, 1), :], (16, forces_ref.shape[1]))
        modes = modes + against_rows(force.astype(jnp.bfloat16), modes_ref[component])[0:1]
    modes = modes / jnp.sqrt(jnp.float32(atoms))
    half = spread_ref.shape[0] // 2
    for part in range(2):
        spread_ref[pl.ds(part, half, stride=2), :] = jnp.broadcast_to(
            modes[:, part * LANES : (part + 1) * LANES], (half, LANES)
        )


def unpack_rows(got_ref, place_ref):
    groups = got_ref.shape[0] // 4
    rows = [got_ref[pl.ds(i, groups, stride=4), :] for i in range(4)]
    for component in range(4):
        place_ref[component] = regroup(rows, component)


def chunk_row(place_ref, component, chunk, size):
    rows = size // LANES
    return jnp.concatenate(
        [place_ref[component, pl.ds(chunk * rows + i, 1), :] for i in range(rows)], axis=1
    )


def pipeline(chunks, build, use):
    build(0, 0)

    @pl.loop(0, chunks // 2)
    def _(step):
        build(1, 2 * step + 1)
        use(0, 2 * step)
        build(0, jnp.minimum(2 * step + 2, chunks - 2))
        use(1, 2 * step + 1)


def pair_of_lines(line_ref, z, size):
    return jnp.concatenate(
        [jnp.broadcast_to(line_ref[pl.ds(z + i, 1), :], (HIGHS, size)) for i in range(2)], axis=0
    )


def splat_kernel(got_ref, out_ref, place_ref, line_ref, even_ref, odd_ref, even_weight_ref, odd_weight_ref, sum_ref):
    size = even_ref.shape[1]
    planes, weights = (even_ref, odd_ref), (even_weight_ref, odd_weight_ref)
    unpack_rows(got_ref, place_ref)
    sum_ref[...] = jnp.zeros_like(sum_ref)
    lows = [low + 0.5 - STEP / 2 for low in range(STEP)]

    def build(slot, chunk):
        place_x, place_y, place_z, masses = [chunk_row(place_ref, i, chunk, size) for i in range(4)]
        place_x = place_x - MIDDLE
        coarse = STEP * row_number(HIGHS, size).astype(jnp.float32) + (STEP / 2 - MIDDLE)
        along_x = factors(place_x, coarse)[0]
        line_ref[slot] = factors(place_z, centers_of(size))[0]
        for z in range(0, EDGE, 2):
            line = pair_of_lines(line_ref.at[slot], z, size)
            block = line * jnp.concatenate([along_x, along_x], axis=0)
            planes[slot][pl.ds(z * HIGHS, 2 * HIGHS), :] = block.astype(jnp.bfloat16)
        along_y = masses * factors(place_y, centers_of(size))[0]
        near = jnp.clip(place_x, -FAR, FAR)
        for low in range(STEP):
            fine = jnp.exp2((2.0 * rate * lows[low]) * near)
            weights[slot][pl.ds(low * EDGE, EDGE), :] = (along_y * fine).astype(jnp.bfloat16)

    def use(slot, chunk):
        width = min(WIDTH, size)
        for part in range(size // width):
            atoms = pl.ds(part * width, width)
            sum_ref[...] += against_rows(planes[slot][:, atoms], weights[slot][:, atoms])

    pipeline(place_ref.shape[1] * LANES // size, build, use)
    total = sum_ref[...].T
    high = (lax.broadcasted_iota(jnp.int32, (EDGE, EDGE * HIGHS), 1) % HIGHS).astype(jnp.float32)
    coarse = STEP * high + (STEP / 2 - MIDDLE)
    for low in range(STEP):
        scale = jnp.exp2(-rate * (2.0 * lows[low] * coarse + lows[low] ** 2))
        block = total[low * EDGE : (low + 1) * EDGE] * scale
        for copy in range(out_ref.shape[0]):
            out_ref[copy, :, pl.ds(low * EDGE * HIGHS, EDGE * HIGHS)] = block


def build_shape(place_ref, line_ref, plane_ref, weight_ref, chunk, size):
    place_x, place_y, place_z, masses = [chunk_row(place_ref, i, chunk, size) for i in range(4)]
    row = row_number(EDGE, size)
    centers = (STEP * (row % HIGHS) + row // HIGHS).astype(jnp.float32) + 0.5
    along_x = factors(place_x, centers)[0]
    doubled = []
    for low in range(STEP):
        block = along_x[low * HIGHS : (low + 1) * HIGHS]
        doubled.append(jnp.concatenate([block, block], axis=0).astype(jnp.bfloat16))
    line_ref[...] = factors(place_z, centers_of(size))[0].astype(jnp.bfloat16).astype(jnp.float32)
    for z in range(0, EDGE, 2):
        line = pair_of_lines(line_ref, z, size).astype(jnp.bfloat16)
        for low in range(STEP):
            plane_ref[pl.ds(low * EDGE * HIGHS + z * HIGHS, 2 * HIGHS), :] = line * doubled[low]
    profile_y, slope_y = factors(place_y, centers_of(size))
    weight_ref[0] = (masses * profile_y).astype(jnp.bfloat16).astype(jnp.float32)
    weight_ref[1] = (masses * slope_y).astype(jnp.bfloat16).astype(jnp.float32)


def voxel_centers():
    voxel = lax.broadcasted_iota(jnp.int32, (EDGE, PLANE), 1)
    low, z, high = voxel // (EDGE * HIGHS), voxel // HIGHS % EDGE, voxel % HIGHS
    return [part.astype(jnp.float32) + (0.5 - MIDDLE) for part in (STEP * high + low, z)]


def store_rows(row_ref, arrays):
    place = 0
    for values in arrays:
        terms = (values,) if values.dtype == jnp.bfloat16 else exact_parts(values)[:2]
        for term in terms:
            row_ref[place : place + EDGE] = term
            place += EDGE


def take_forces(sum_ref, chunk, sums, weights, places):
    plain, by_x, by_z = sums
    along_y, slope_y = weights
    whole, force_y, moment_x, moment_z = [
        jnp.sum(values * weight, axis=0, keepdims=True)
        for values, weight in ((plain, along_y), (plain, slope_y), (by_x, along_y), (by_z, along_y))
    ]
    force_x = inverse_var * (moment_x - (places[0] - MIDDLE) * whole)
    force_z = inverse_var * (moment_z - (places[1] - MIDDLE) * whole)
    rows = whole.shape[1] // LANES
    for component, force in enumerate((force_x, force_y, force_z)):
        for i in range(rows):
            sum_ref[component, pl.ds(chunk * rows + i, 1), :] = force[:, i * LANES : (i + 1) * LANES]


def pull_rows(single, place_ref, row_ref, sum_ref, line_ref, even_ref, odd_ref, weight_ref):
    planes = (even_ref, odd_ref)
    size = even_ref.shape[1]
    width = min(WIDTH, size)

    def build(slot, chunk):
        build_shape(place_ref, line_ref.at[slot], planes[slot], weight_ref.at[slot], chunk, size)

    def use(slot, chunk):
        for part in range(size // width):
            atoms = pl.ds(part * width, width)
            small = chunk * (size // width) + part
            pulled = jnp.dot(row_ref[...], planes[slot][:, atoms], preferred_element_type=jnp.float32)
            block = [pulled[i : i + EDGE] for i in range(0, pulled.shape[0], EDGE)]
            plain = block[0] if single else block[0] + block[1]
            block = block[1:] if single else block[2:]
            take_forces(
                sum_ref,
                small,
                (plain, block[0] + block[1], block[2] + block[3]),
                [weight_ref[slot, i, :, atoms] for i in range(2)],
                [chunk_row(place_ref, i, small, width) for i in (0, 2)],
            )

    pipeline(place_ref.shape[1] * LANES // size, build, use)


def map_kernel(got_ref, target_ref, sum_ref, place_ref, row_ref, *scratch):
    unpack_rows(got_ref, place_ref)
    wide = target_ref[...].astype(jnp.float32)
    center_x, center_z = voxel_centers()
    store_rows(row_ref, (target_ref[...], wide * center_x, wide * center_z))
    pull_rows(True, place_ref, row_ref, sum_ref, *scratch)


def pull_kernel(got_ref, parts_ref, target_ref, map_ref, out_ref, place_ref, row_ref, sum_ref, stage_ref, *scratch):
    unpack_rows(got_ref, place_ref)
    density = (parts_ref[0] + parts_ref[2]) + (parts_ref[1] + parts_ref[3])
    center_x, center_z = voxel_centers()
    store_rows(row_ref, (density, density * center_x, density * center_z))
    wide = target_ref[...].astype(jnp.float32)
    totals = [
        jnp.sum(jnp.sum(product, axis=0, keepdims=True), axis=1, keepdims=True)
        for product in (density * wide, density * density, wide * wide)
    ]
    ratio = jnp.where(totals[1] > 0.0, totals[0] / totals[1], 0.0)
    pairs = place_ref.shape[1]
    lane = lax.broadcasted_iota(jnp.int32, (8, LANES), 1)
    last = jnp.zeros((8, LANES), jnp.float32)
    for place, value in enumerate(totals + [ratio]):
        for i, term in enumerate(exact_parts(jnp.broadcast_to(value, (8, LANES)))):
            last = jnp.where(lane == 3 * place + i, term.astype(jnp.float32), last)
    stage_ref[pl.ds(3, 2 * pairs, stride=4), :] = jnp.broadcast_to(last[0:1], (2 * pairs, LANES))
    pull_rows(False, place_ref, row_ref, sum_ref, *scratch)
    left = lax.broadcasted_iota(jnp.int32, (pairs, LANES), 1) < LANES // 2
    for component in range(3):
        second = sum_ref[component]
        first = map_ref[component] - ratio * second
        stage_ref[pl.ds(component, pairs, stride=8), :] = jnp.where(
            left, first, pltpu.roll(second, LANES // 2, 1)
        )
        stage_ref[pl.ds(4 + component, pairs, stride=8), :] = jnp.where(
            left, pltpu.roll(first, LANES // 2, 1), second
        )
    out_ref[...] = stage_ref[...].astype(jnp.bfloat16)


def call(kernel, name, out_shape, scratch, flops, *operands, source=pltpu.VMEM, limit=32):
    vmem = pl.BlockSpec(memory_space=pltpu.VMEM)
    return pl.pallas_call(
        kernel,
        out_shape=out_shape,
        in_specs=[pl.BlockSpec(memory_space=source)] * len(operands),
        out_specs=jax.tree.map(lambda _: vmem, out_shape),
        scratch_shapes=[pltpu.VMEM(*entry) if isinstance(entry, tuple) else entry for entry in scratch],
        compiler_params=pltpu.CompilerParams(vmem_limit_bytes=limit * 2**20),
        cost_estimate=pl.CostEstimate(flops=flops, bytes_accessed=2**20, transcendentals=2**20),
        name=name,
    )(*operands)


def pack(coords, weights, modes, amplitudes, tiles, offsets, n_tile):
    blocks = tiles.shape[1]
    operands = (tiles, offsets, amplitudes, coords, weights, modes)
    return call(
        pack_kernel,
        "pack",
        (
            jax.ShapeDtypeStruct((2 * n_tile, LANES), jnp.float32),
            jax.ShapeDtypeStruct((2, blocks, n_tile), jnp.bfloat16),
        ),
        [((4, weights.shape[0], LANES), jnp.float32), ((blocks, LANES), jnp.float32)]
        + [(operand.shape, operand.dtype) for operand in operands]
        + [pltpu.SemaphoreType.DMA((len(operands),))],
        2**26,
        *operands,
        source=pltpu.HBM,
        limit=60,
    )


def finish(back, picks, modes, voxels, atoms, copies):
    blocks = picks.shape[1]
    return call(
        lambda *refs: finish_kernel(voxels, atoms, *refs),
        "finish",
        (
            jax.ShapeDtypeStruct((3, modes.shape[2]), jnp.float32),
            jax.ShapeDtypeStruct((2 * copies, LANES), jnp.float32),
            jax.ShapeDtypeStruct((1, LANES), jnp.float32),
        ),
        [(back.shape, jnp.float32), ((3, blocks, LANES), jnp.float32)],
        2**26,
        back,
        picks,
        modes,
    )


def splat(got, copies):
    groups = got.shape[0] // 4
    size = min(CHUNK, groups * LANES // 2)
    plane = ((EDGE * HIGHS, size), jnp.bfloat16)
    weight = ((EDGE * STEP, size), jnp.bfloat16)
    return call(
        splat_kernel,
        "splat",
        jax.ShapeDtypeStruct((copies, EDGE, PLANE), jnp.float32),
        [
            ((4, groups, LANES), jnp.float32),
            ((2, EDGE, size), jnp.float32),
            plane,
            plane,
            weight,
            weight,
            ((EDGE * HIGHS, EDGE * STEP), jnp.float32),
        ],
        2**29,
        got,
    )


def shape_scratch(groups):
    size = min(CHUNK, groups * LANES // 2)
    plane = ((PLANE, size), jnp.bfloat16)
    return [((2, EDGE, size), jnp.float32), plane, plane, ((2, 2, EDGE, size), jnp.float32)]


def pull_map(got, target):
    groups = got.shape[0] // 4
    return call(
        map_kernel,
        "pull_map",
        jax.ShapeDtypeStruct((3, groups, LANES), jnp.float32),
        [((4, groups, LANES), jnp.float32), ((5 * EDGE, PLANE), jnp.bfloat16)] + shape_scratch(groups),
        2**32,
        got,
        target,
    )


def pull(got, parts, target, from_map):
    groups = got.shape[0] // 4
    return call(
        pull_kernel,
        "pull",
        jax.ShapeDtypeStruct((8 * groups, LANES), jnp.bfloat16),
        [
            ((4, groups, LANES), jnp.float32),
            ((6 * EDGE, PLANE), jnp.bfloat16),
            ((3, groups, LANES), jnp.float32),
            ((8 * groups, LANES), jnp.float32),
        ]
        + shape_scratch(groups),
        2**32,
        got,
        parts,
        target,
        from_map,
    )


TILE_AXES = ("y", "z", "core")


def exchange(values, axes):
    return lax.all_to_all(values, axes, split_axis=0, concat_axis=0, tiled=True)


def on_device(coords, weights, mode_vectors, amplitudes, density_map, block_tiles, block_offsets):
    a_dev = coords.shape[1]
    n_tile = lax.axis_size(TILE_AXES)
    n_seg = lax.axis_size("seg")
    modes = jnp.transpose(mode_vectors, (1, 0, 2))
    send, picks = pack(
        coords,
        weights.reshape(a_dev // LANES, LANES),
        modes,
        amplitudes.reshape(1, -1),
        block_tiles.T,
        jnp.transpose(block_offsets, (2, 1, 0)),
        n_tile,
    )
    got = exchange(send.reshape(n_tile, 2, LANES), TILE_AXES).reshape(2 * n_tile, LANES)
    target = density_map.reshape(EDGE, HIGHS, STEP, EDGE)
    target = jnp.transpose(target, (3, 2, 0, 1)).reshape(EDGE, PLANE)
    parts = exchange(splat(got, n_seg), "seg")
    pulled = pull(got, parts, target, pull_map(got, target))
    back = exchange(pulled.reshape(n_tile, 4, LANES), TILE_AXES).reshape(4 * n_tile, LANES)
    near, far = ("z", "core"), ("y", "seg")
    forces, spread, score = finish(
        back, picks, modes, float(n_tile * EDGE**3), a_dev * n_tile * n_seg, lax.axis_size(near)
    )
    near_sum = jnp.sum(exchange(spread.reshape(-1, 2, LANES), near), axis=0)
    copies = jnp.broadcast_to(near_sum[None], (lax.axis_size(far), 2, LANES))
    mode_grad = jnp.sum(exchange(copies, far), axis=0).reshape(-1)
    return (forces, mode_grad, score[0, 0])


def solution(mesh):
    split = Mesh(mesh.devices.reshape(8, 8, 2, 4), TILE_AXES + ("seg",))
    every = TILE_AXES + ("seg",)
    return jax.shard_map(
        on_device,
        mesh=split,
        in_specs=(
            P(None, every),
            P(every),
            P(None, None, every),
            P(),
            P(TILE_AXES, None),
            P(every, None),
            P(every, None, None),
        ),
        out_specs=(P(None, every), P(), P()),
        check_vma=False,
    )
```

```python
import math

import jax
import jax.numpy as jnp
from jax import lax
from jax.experimental import pallas as pl
from jax.experimental.pallas import tpu as pltpu
from jax.sharding import Mesh
from jax.sharding import PartitionSpec as P

EDGE = 32
ATOM_BLOCK = 32
PLANE = EDGE * EDGE
LANES = 128
CHUNK = 512
WIDTH = 256

STEP = 4
HIGHS = EDGE // STEP
MIDDLE = EDGE / 2

SPAN = 40.0
PLACE_STEPS = 32000.0 / SPAN
MASS_STEPS = 8000.0
DENSITY_STEPS = 16000.0
POWER_ROWS = 16

inverse_var = 1.0 / 2.25
rate = 0.5 * inverse_var / math.log(2.0)


def row_number(rows, columns):
    return lax.broadcasted_iota(jnp.int32, (rows, columns), 0)


def factors(places, centers):
    distance = centers - places
    profile = jnp.exp2(-rate * (distance * distance))
    return profile, inverse_var * distance * profile


def centers_of(columns):
    return row_number(EDGE, columns).astype(jnp.float32) + 0.5


def exact_parts(values):
    high = values.astype(jnp.bfloat16)
    rest = values - high.astype(jnp.float32)
    middle = rest.astype(jnp.bfloat16)
    return high, middle, (rest - middle.astype(jnp.float32)).astype(jnp.bfloat16)


def whole_steps(values):
    return jnp.floor(values + 0.5).astype(jnp.int32).astype(jnp.int16)


def from_steps(steps):
    return steps.astype(jnp.int32).astype(jnp.float32)


def against_rows(left, right):
    return lax.dot_general(
        left, right, (((1,), (1,)), ((), ())), preferred_element_type=jnp.float32
    )


def quarter_of(shape):
    return lax.broadcasted_iota(jnp.int32, shape, 1) // ATOM_BLOCK


def regroup(rows, target):
    quarter = quarter_of(rows[0].shape)
    result = jnp.zeros_like(rows[0])
    for i in range(4):
        moved = pltpu.roll(rows[i], ((i - target) % 4) * ATOM_BLOCK, 1) if i != target else rows[i]
        result = jnp.where(quarter == i, moved, result)
    return result


def pack_kernel(*refs):
    sources, (send_ref, pick_ref), (cell_ref, block_ref, wide_ref) = refs[:6], refs[6:8], refs[8:11]
    local, sems = refs[11:17], refs[17]
    copies = [
        pltpu.make_async_copy(source, place, sems.at[i])
        for i, (source, place) in enumerate(zip(sources, local))
    ]
    for copy in copies:
        copy.start()
    tiles_ref, offsets_ref, amps_ref, coords_ref, weights_ref, modes_ref = local
    n_tile = send_ref.shape[0] // 2
    blocks = block_ref.shape[0]
    cells = cell_ref.shape[1]
    for copy in copies[:2]:
        copy.wait()
    shape = (n_tile, blocks)
    tile_of_row = lax.broadcasted_iota(jnp.int32, shape, 0)
    row = lax.broadcasted_iota(jnp.int32, (blocks, blocks), 0)
    column = lax.broadcasted_iota(jnp.int32, (blocks, blocks), 1)
    before = jnp.where(row < column, 1.0, 0.0).astype(jnp.bfloat16)
    same = jnp.where(row == column, 1.0, 0.0).astype(jnp.bfloat16)
    ones = jnp.ones((blocks, blocks), jnp.bfloat16)
    seen = jnp.zeros(shape, jnp.float32)
    picks = [jnp.zeros(shape, jnp.float32) for _ in range(2)]
    shifts = [jnp.zeros((n_tile, LANES), jnp.float32) for _ in range(2)]
    for k in range(tiles_ref.shape[0]):
        named = jnp.where(tiles_ref[pl.ds(k, 1), :] == tile_of_row, 1.0, 0.0)
        flags = named.astype(jnp.bfloat16)
        rank = seen + jnp.dot(flags, before, preferred_element_type=jnp.float32)
        seen = seen + jnp.dot(flags, ones, preferred_element_type=jnp.float32)
        offsets = [
            jnp.broadcast_to(offsets_ref[c, pl.ds(k, 1), :].astype(jnp.float32), (ATOM_BLOCK, blocks))
            for c in range(3)
        ]
        offsets = jnp.concatenate(offsets + [jnp.zeros((ATOM_BLOCK, blocks), jnp.float32)], axis=0)
        for slot in range(2):
            mine = jnp.where(rank == float(slot), named, 0.0)
            picks[slot] = picks[slot] + mine
            shifts[slot] = shifts[slot] + against_rows(
                mine.astype(jnp.bfloat16), offsets.astype(jnp.bfloat16)
            )
    for copy in copies[2:]:
        copy.wait()
    amps = jnp.broadcast_to(amps_ref[...], (16, amps_ref.shape[1])).astype(jnp.bfloat16)
    for component in range(3):
        moved = jnp.dot(amps, modes_ref[component], preferred_element_type=jnp.float32)
        places = coords_ref[pl.ds(component, 1), :] + moved[0:1]
        for cell in range(cells):
            cell_ref[component, pl.ds(cell, 1), :] = places[:, cell * LANES : (cell + 1) * LANES]
    cell_ref[3] = weights_ref[...]
    for i in range(4):
        block_ref[pl.ds(i, cells, stride=4), :] = regroup([cell_ref[c] for c in range(4)], i)
    parts = exact_parts(block_ref[...])
    for slot in range(2):
        pick = picks[slot].astype(jnp.bfloat16)
        high, middle, low = [jnp.dot(pick, part, preferred_element_type=jnp.float32) for part in parts]
        rows = ((high + middle) + low) + shifts[slot]
        steps = jnp.clip(rows - MIDDLE, -SPAN, SPAN) * PLACE_STEPS
        wide_ref[pl.ds(slot, n_tile, stride=2), :] = jnp.where(
            quarter_of(rows.shape) < 3, steps, rows * MASS_STEPS
        )
        pick_ref[slot] = against_rows(same, pick).astype(jnp.bfloat16)
    send_ref[...] = whole_steps(wide_ref[...])


def finish_kernel(voxels, atoms, back_ref, pick_ref, modes_ref, forces_ref, spread_ref, score_ref, wide_ref, block_ref):
    n_tile = pick_ref.shape[2]
    wide_ref[...] = back_ref[...].astype(jnp.float32)
    last = wide_ref[pl.ds(3, n_tile, stride=4), :]
    place = lax.broadcasted_iota(jnp.int32, (n_tile, LANES), 1) // 3
    ratio = jnp.sum(jnp.where(place == 3, last, 0.0), axis=1, keepdims=True)
    totals = jnp.sum(last, axis=0, keepdims=True)
    srm, srr, smm = [
        jnp.sum(jnp.where(place[0:1] == i, totals, 0.0), axis=1, keepdims=True) for i in range(3)
    ]
    root = jnp.sqrt(srr * smm)
    score = srm / root
    score_ref[...] = jnp.broadcast_to(score, score_ref.shape)
    map_scale = voxels / root
    model_scale = map_scale * (ratio - srm / srr)
    cells = forces_ref.shape[1] // LANES
    modes = jnp.zeros((1, modes_ref.shape[1]), jnp.float32)
    for component in range(3):
        pulled = wide_ref[pl.ds(component, n_tile, stride=4), :]
        pulled = pulled * map_scale + pltpu.roll(pulled, LANES // 2, 1) * model_scale
        parts = exact_parts(pulled)
        first, second = [
            sum([jnp.dot(pick_ref[slot], part, preferred_element_type=jnp.float32) for part in parts[::-1]])
            for slot in range(2)
        ]
        block_ref[component] = first + pltpu.roll(second, LANES - ATOM_BLOCK, 1)
        rows = regroup([block_ref[component, pl.ds(i, cells, stride=4), :] for i in range(4)], 0)
        for cell in range(cells):
            forces_ref[pl.ds(component, 1), cell * LANES : (cell + 1) * LANES] = rows[cell : cell + 1]
        force = jnp.broadcast_to(forces_ref[pl.ds(component, 1), :], (16, forces_ref.shape[1]))
        modes = modes + against_rows(force.astype(jnp.bfloat16), modes_ref[component])[0:1]
    modes = modes / jnp.sqrt(jnp.float32(atoms))
    half = spread_ref.shape[0] // 2
    for part in range(2):
        spread_ref[pl.ds(part, half, stride=2), :] = jnp.broadcast_to(
            modes[:, part * LANES : (part + 1) * LANES], (half, LANES)
        )


def unpack_rows(got_ref, wide_ref, place_ref):
    wide_ref[...] = from_steps(got_ref[...])
    groups = got_ref.shape[0] // 4
    rows = [wide_ref[pl.ds(i, groups, stride=4), :] for i in range(4)]
    for component in range(3):
        place_ref[component] = regroup(rows, component) * (1.0 / PLACE_STEPS) + MIDDLE
    place_ref[3] = regroup(rows, 3) * (1.0 / MASS_STEPS)


def chunk_row(place_ref, component, chunk, size):
    rows = size // LANES
    return jnp.concatenate(
        [place_ref[component, pl.ds(chunk * rows + i, 1), :] for i in range(rows)], axis=1
    )


def pipeline(chunks, build, use):
    build(0, 0)

    @pl.loop(0, chunks // 2)
    def _(step):
        build(1, 2 * step + 1)
        use(0, 2 * step)
        build(0, jnp.minimum(2 * step + 2, chunks - 2))
        use(1, 2 * step + 1)


def pair_of_lines(line_ref, z, size):
    return jnp.concatenate(
        [jnp.broadcast_to(line_ref[pl.ds(z + i, 1), :], (HIGHS, size)) for i in range(2)], axis=0
    )


def splat_kernel(got_ref, out_ref, wide_ref, place_ref, line_ref, even_ref, odd_ref, even_weight_ref, odd_weight_ref, sum_ref):
    size = even_ref.shape[1]
    planes, weights = (even_ref, odd_ref), (even_weight_ref, odd_weight_ref)
    unpack_rows(got_ref, wide_ref, place_ref)
    sum_ref[...] = jnp.zeros_like(sum_ref)
    lows = [low + 0.5 - STEP / 2 for low in range(STEP)]

    def build(slot, chunk):
        place_x, place_y, place_z, masses = [chunk_row(place_ref, i, chunk, size) for i in range(4)]
        place_x = place_x - MIDDLE
        coarse = STEP * row_number(HIGHS, size).astype(jnp.float32) + (STEP / 2 - MIDDLE)
        along_x = factors(place_x, coarse)[0]
        line_ref[slot] = factors(place_z, centers_of(size))[0]
        for z in range(0, EDGE, 2):
            line = pair_of_lines(line_ref.at[slot], z, size)
            block = line * jnp.concatenate([along_x, along_x], axis=0)
            planes[slot][pl.ds(z * HIGHS, 2 * HIGHS), :] = block.astype(jnp.bfloat16)
        along_y = masses * factors(place_y, centers_of(size))[0]
        near = jnp.clip(place_x, -SPAN, SPAN)
        for low in range(STEP):
            fine = jnp.exp2((2.0 * rate * lows[low]) * near)
            weights[slot][pl.ds(low * EDGE, EDGE), :] = (along_y * fine).astype(jnp.bfloat16)

    def use(slot, chunk):
        width = min(WIDTH, size)
        for part in range(size // width):
            atoms = pl.ds(part * width, width)
            sum_ref[...] += against_rows(planes[slot][:, atoms], weights[slot][:, atoms])

    pipeline(place_ref.shape[1] * LANES // size, build, use)
    total = sum_ref[...].T
    high = (lax.broadcasted_iota(jnp.int32, (EDGE, EDGE * HIGHS), 1) % HIGHS).astype(jnp.float32)
    coarse = STEP * high + (STEP / 2 - MIDDLE)
    blocks = []
    for low in range(STEP):
        scale = jnp.exp2(-rate * (2.0 * lows[low] * coarse + lows[low] ** 2))
        block = total[low * EDGE : (low + 1) * EDGE] * scale
        blocks += [block[:, i : i + LANES] for i in range(0, block.shape[1], LANES)]
    largest = blocks[0]
    for block in blocks[1:]:
        largest = jnp.maximum(largest, block)
    largest = jnp.max(jnp.max(largest, axis=0, keepdims=True), axis=1, keepdims=True)
    power = jnp.floor(jnp.log(jnp.clip(largest, 1e-30, 1e30)) * (1.0 / math.log(2.0)))
    steps = DENSITY_STEPS * jnp.exp2(-power)
    rows = [whole_steps(block * steps) for block in blocks]
    rows.append(whole_steps(jnp.broadcast_to(power, (POWER_ROWS, LANES))))
    for copy in range(out_ref.shape[0]):
        place = 0
        for block in rows:
            out_ref[copy, pl.ds(place, block.shape[0]), :] = block
            place += block.shape[0]


def density_of(parts_ref, part):
    count = parts_ref.shape[1] - POWER_ROWS
    power = from_steps(parts_ref[part, pl.ds(count, POWER_ROWS), :])[0:1]
    step = jnp.exp2(power) * (1.0 / DENSITY_STEPS)
    blocks = [from_steps(parts_ref[part, pl.ds(i, EDGE), :]) * step for i in range(0, count, EDGE)]
    return jnp.concatenate(blocks, axis=1)


def build_shape(place_ref, line_ref, plane_ref, weight_ref, chunk, size):
    place_x, place_y, place_z, masses = [chunk_row(place_ref, i, chunk, size) for i in range(4)]
    row = row_number(EDGE, size)
    centers = (STEP * (row % HIGHS) + row // HIGHS).astype(jnp.float32) + 0.5
    along_x = factors(place_x, centers)[0]
    doubled = []
    for low in range(STEP):
        block = along_x[low * HIGHS : (low + 1) * HIGHS]
        doubled.append(jnp.concatenate([block, block], axis=0).astype(jnp.bfloat16))
    line_ref[...] = factors(place_z, centers_of(size))[0].astype(jnp.bfloat16).astype(jnp.float32)
    for z in range(0, EDGE, 2):
        line = pair_of_lines(line_ref, z, size).astype(jnp.bfloat16)
        for low in range(STEP):
            plane_ref[pl.ds(low * EDGE * HIGHS + z * HIGHS, 2 * HIGHS), :] = line * doubled[low]
    profile_y, slope_y = factors(place_y, centers_of(size))
    weight_ref[0] = (masses * profile_y).astype(jnp.bfloat16).astype(jnp.float32)
    weight_ref[1] = (masses * slope_y).astype(jnp.bfloat16).astype(jnp.float32)


def voxel_centers():
    voxel = lax.broadcasted_iota(jnp.int32, (EDGE, PLANE), 1)
    low, z, high = voxel // (EDGE * HIGHS), voxel // HIGHS % EDGE, voxel % HIGHS
    return [part.astype(jnp.float32) + (0.5 - MIDDLE) for part in (STEP * high + low, z)]


def store_rows(row_ref, arrays):
    place = 0
    for values in arrays:
        terms = (values,) if values.dtype == jnp.bfloat16 else exact_parts(values)[:2]
        for term in terms:
            row_ref[place : place + EDGE] = term
            place += EDGE


def take_forces(sum_ref, chunk, sums, weights, places):
    plain, by_x, by_z = sums
    along_y, slope_y = weights
    whole, force_y, moment_x, moment_z = [
        jnp.sum(values * weight, axis=0, keepdims=True)
        for values, weight in ((plain, along_y), (plain, slope_y), (by_x, along_y), (by_z, along_y))
    ]
    force_x = inverse_var * (moment_x - (places[0] - MIDDLE) * whole)
    force_z = inverse_var * (moment_z - (places[1] - MIDDLE) * whole)
    rows = whole.shape[1] // LANES
    for component, force in enumerate((force_x, force_y, force_z)):
        for i in range(rows):
            sum_ref[component, pl.ds(chunk * rows + i, 1), :] = force[:, i * LANES : (i + 1) * LANES]


def pull_rows(single, place_ref, row_ref, sum_ref, line_ref, even_ref, odd_ref, weight_ref):
    planes = (even_ref, odd_ref)
    size = even_ref.shape[1]
    width = min(WIDTH, size)

    def build(slot, chunk):
        build_shape(place_ref, line_ref.at[slot], planes[slot], weight_ref.at[slot], chunk, size)

    def use(slot, chunk):
        for part in range(size // width):
            atoms = pl.ds(part * width, width)
            small = chunk * (size // width) + part
            pulled = jnp.dot(row_ref[...], planes[slot][:, atoms], preferred_element_type=jnp.float32)
            block = [pulled[i : i + EDGE] for i in range(0, pulled.shape[0], EDGE)]
            plain = block[0] if single else block[0] + block[1]
            block = block[1:] if single else block[2:]
            take_forces(
                sum_ref,
                small,
                (plain, block[0] + block[1], block[2] + block[3]),
                [weight_ref[slot, i, :, atoms] for i in range(2)],
                [chunk_row(place_ref, i, small, width) for i in (0, 2)],
            )

    pipeline(place_ref.shape[1] * LANES // size, build, use)


def map_kernel(got_ref, target_ref, sum_ref, wide_ref, place_ref, row_ref, *scratch):
    unpack_rows(got_ref, wide_ref, place_ref)
    wide = target_ref[...].astype(jnp.float32)
    center_x, center_z = voxel_centers()
    store_rows(row_ref, (target_ref[...], wide * center_x, wide * center_z))
    pull_rows(True, place_ref, row_ref, sum_ref, *scratch)


def pull_kernel(got_ref, parts_ref, target_ref, map_ref, out_ref, wide_ref, place_ref, row_ref, sum_ref, stage_ref, *scratch):
    unpack_rows(got_ref, wide_ref, place_ref)
    parts = [density_of(parts_ref, i) for i in range(4)]
    density = (parts[0] + parts[2]) + (parts[1] + parts[3])
    center_x, center_z = voxel_centers()
    store_rows(row_ref, (density, density * center_x, density * center_z))
    wide = target_ref[...].astype(jnp.float32)
    totals = [
        jnp.sum(jnp.sum(product, axis=0, keepdims=True), axis=1, keepdims=True)
        for product in (density * wide, density * density, wide * wide)
    ]
    ratio = jnp.where(totals[1] > 0.0, totals[0] / totals[1], 0.0)
    pairs = place_ref.shape[1]
    lane = lax.broadcasted_iota(jnp.int32, (8, LANES), 1)
    last = jnp.zeros((8, LANES), jnp.float32)
    for place, value in enumerate(totals + [ratio]):
        for i, term in enumerate(exact_parts(jnp.broadcast_to(value, (8, LANES)))):
            last = jnp.where(lane == 3 * place + i, term.astype(jnp.float32), last)
    stage_ref[pl.ds(3, 2 * pairs, stride=4), :] = jnp.broadcast_to(last[0:1], (2 * pairs, LANES))
    pull_rows(False, place_ref, row_ref, sum_ref, *scratch)
    left = lax.broadcasted_iota(jnp.int32, (pairs, LANES), 1) < LANES // 2
    for component in range(3):
        second = sum_ref[component]
        first = map_ref[component] - ratio * second
        stage_ref[pl.ds(component, pairs, stride=8), :] = jnp.where(
            left, first, pltpu.roll(second, LANES // 2, 1)
        )
        stage_ref[pl.ds(4 + component, pairs, stride=8), :] = jnp.where(
            left, pltpu.roll(first, LANES // 2, 1), second
        )
    out_ref[...] = stage_ref[...].astype(jnp.bfloat16)


def call(kernel, name, out_shape, scratch, flops, *operands, source=pltpu.VMEM, limit=32):
    vmem = pl.BlockSpec(memory_space=pltpu.VMEM)
    return pl.pallas_call(
        kernel,
        out_shape=out_shape,
        in_specs=[pl.BlockSpec(memory_space=source)] * len(operands),
        out_specs=jax.tree.map(lambda _: vmem, out_shape),
        scratch_shapes=[pltpu.VMEM(*entry) if isinstance(entry, tuple) else entry for entry in scratch],
        compiler_params=pltpu.CompilerParams(vmem_limit_bytes=limit * 2**20),
        cost_estimate=pl.CostEstimate(flops=flops, bytes_accessed=2**20, transcendentals=2**20),
        name=name,
    )(*operands)


def pack(coords, weights, modes, amplitudes, tiles, offsets, n_tile):
    blocks = tiles.shape[1]
    operands = (tiles, offsets, amplitudes, coords, weights, modes)
    return call(
        pack_kernel,
        "pack",
        (
            jax.ShapeDtypeStruct((2 * n_tile, LANES), jnp.int16),
            jax.ShapeDtypeStruct((2, blocks, n_tile), jnp.bfloat16),
        ),
        [
            ((4, weights.shape[0], LANES), jnp.float32),
            ((blocks, LANES), jnp.float32),
            ((2 * n_tile, LANES), jnp.float32),
        ]
        + [(operand.shape, operand.dtype) for operand in operands]
        + [pltpu.SemaphoreType.DMA((len(operands),))],
        2**26,
        *operands,
        source=pltpu.HBM,
        limit=60,
    )


def finish(back, picks, modes, voxels, atoms, copies):
    blocks = picks.shape[1]
    return call(
        lambda *refs: finish_kernel(voxels, atoms, *refs),
        "finish",
        (
            jax.ShapeDtypeStruct((3, modes.shape[2]), jnp.float32),
            jax.ShapeDtypeStruct((2 * copies, LANES), jnp.float32),
            jax.ShapeDtypeStruct((1, LANES), jnp.float32),
        ),
        [(back.shape, jnp.float32), ((3, blocks, LANES), jnp.float32)],
        2**26,
        back,
        picks,
        modes,
    )


def splat(got, copies):
    groups = got.shape[0] // 4
    size = min(CHUNK, groups * LANES // 2)
    plane = ((EDGE * HIGHS, size), jnp.bfloat16)
    weight = ((EDGE * STEP, size), jnp.bfloat16)
    return call(
        splat_kernel,
        "splat",
        jax.ShapeDtypeStruct((copies, EDGE * PLANE // LANES + POWER_ROWS, LANES), jnp.int16),
        [
            ((4 * groups, LANES), jnp.float32), ((4, groups, LANES), jnp.float32),
            ((2, EDGE, size), jnp.float32),
            plane,
            plane,
            weight,
            weight,
            ((EDGE * HIGHS, EDGE * STEP), jnp.float32),
        ],
        2**29,
        got,
    )


def shape_scratch(groups):
    size = min(CHUNK, groups * LANES // 2)
    plane = ((PLANE, size), jnp.bfloat16)
    return [((2, EDGE, size), jnp.float32), plane, plane, ((2, 2, EDGE, size), jnp.float32)]


def pull_map(got, target):
    groups = got.shape[0] // 4
    return call(
        map_kernel,
        "pull_map",
        jax.ShapeDtypeStruct((3, groups, LANES), jnp.float32),
        [((4 * groups, LANES), jnp.float32), ((4, groups, LANES), jnp.float32), ((5 * EDGE, PLANE), jnp.bfloat16)] + shape_scratch(groups),
        2**32,
        got,
        target,
    )


def pull(got, parts, target, from_map):
    groups = got.shape[0] // 4
    return call(
        pull_kernel,
        "pull",
        jax.ShapeDtypeStruct((8 * groups, LANES), jnp.bfloat16),
        [
            ((4 * groups, LANES), jnp.float32), ((4, groups, LANES), jnp.float32),
            ((6 * EDGE, PLANE), jnp.bfloat16),
            ((3, groups, LANES), jnp.float32),
            ((8 * groups, LANES), jnp.float32),
        ]
        + shape_scratch(groups),
        2**32,
        got,
        parts,
        target,
        from_map,
    )


TILE_AXES = ("y", "z", "core")


def exchange(values, axes):
    return lax.all_to_all(values, axes, split_axis=0, concat_axis=0, tiled=True)


def on_device(coords, weights, mode_vectors, amplitudes, density_map, block_tiles, block_offsets):
    a_dev = coords.shape[1]
    n_tile = lax.axis_size(TILE_AXES)
    n_seg = lax.axis_size("seg")
    modes = jnp.transpose(mode_vectors, (1, 0, 2))
    send, picks = pack(
        coords,
        weights.reshape(a_dev // LANES, LANES),
        modes,
        amplitudes.reshape(1, -1),
        block_tiles.T,
        jnp.transpose(block_offsets, (2, 1, 0)),
        n_tile,
    )
    got = exchange(send.reshape(n_tile, 2, LANES), TILE_AXES).reshape(2 * n_tile, LANES)
    target = density_map.reshape(EDGE, HIGHS, STEP, EDGE)
    target = jnp.transpose(target, (3, 2, 0, 1)).reshape(EDGE, PLANE)
    parts = exchange(splat(got, n_seg), "seg")
    pulled = pull(got, parts, target, pull_map(got, target))
    back = exchange(pulled.reshape(n_tile, 4, LANES), TILE_AXES).reshape(4 * n_tile, LANES)
    near, far = ("z", "core"), ("y", "seg")
    forces, spread, score = finish(
        back, picks, modes, float(n_tile * EDGE**3), a_dev * n_tile * n_seg, lax.axis_size(near)
    )
    near_sum = jnp.sum(exchange(spread.reshape(-1, 2, LANES), near), axis=0)
    copies = jnp.broadcast_to(near_sum[None], (lax.axis_size(far), 2, LANES))
    mode_grad = jnp.sum(exchange(copies, far), axis=0).reshape(-1)
    return (forces, mode_grad, score[0, 0])


def solution(mesh):
    split = Mesh(mesh.devices.reshape(8, 8, 2, 4), TILE_AXES + ("seg",))
    every = TILE_AXES + ("seg",)
    return jax.shard_map(
        on_device,
        mesh=split,
        in_specs=(
            P(None, every),
            P(every),
            P(None, None, every),
            P(),
            P(TILE_AXES, None),
            P(every, None),
            P(every, None, None),
        ),
        out_specs=(P(None, every), P(), P()),
        check_vma=False,
    )
```

```python
import math

import jax
import jax.numpy as jnp
from jax import lax
from jax.experimental import pallas as pl
from jax.experimental.pallas import tpu as pltpu
from jax.sharding import Mesh
from jax.sharding import PartitionSpec as P

EDGE = 32
ATOM_BLOCK = 32
PLANE = EDGE * EDGE
LANES = 128
CHUNK = 512
WIDTH = 256

STEP = 4
HIGHS = EDGE // STEP
MIDDLE = EDGE / 2

SPAN = 40.0
PLACE_STEPS = 32000.0 / SPAN
MASS_STEPS = 8000.0
DENSITY_STEPS = 16000.0
POWER_ROWS = 16

inverse_var = 1.0 / 2.25
rate = 0.5 * inverse_var / math.log(2.0)


def row_number(rows, columns):
    return lax.broadcasted_iota(jnp.int32, (rows, columns), 0)


def factors(places, centers):
    distance = centers - places
    profile = jnp.exp2(-rate * (distance * distance))
    return profile, inverse_var * distance * profile


def centers_of(columns):
    return row_number(EDGE, columns).astype(jnp.float32) + 0.5


def exact_parts(values):
    high = values.astype(jnp.bfloat16)
    rest = values - high.astype(jnp.float32)
    middle = rest.astype(jnp.bfloat16)
    return high, middle, (rest - middle.astype(jnp.float32)).astype(jnp.bfloat16)


def whole_steps(values):
    return jnp.floor(values + 0.5).astype(jnp.int32).astype(jnp.int16)


def from_steps(steps):
    return steps.astype(jnp.int32).astype(jnp.float32)


def against_rows(left, right):
    return lax.dot_general(
        left, right, (((1,), (1,)), ((), ())), preferred_element_type=jnp.float32
    )


def quarter_of(shape):
    return lax.broadcasted_iota(jnp.int32, shape, 1) // ATOM_BLOCK


def regroup(rows, target):
    quarter = quarter_of(rows[0].shape)
    result = jnp.zeros_like(rows[0])
    for i in range(4):
        moved = pltpu.roll(rows[i], ((i - target) % 4) * ATOM_BLOCK, 1) if i != target else rows[i]
        result = jnp.where(quarter == i, moved, result)
    return result


def pack_kernel(*refs):
    sources, (send_ref, pick_ref), (cell_ref, block_ref, wide_ref) = refs[:6], refs[6:8], refs[8:11]
    local, sems = refs[11:17], refs[17]
    copies = [
        pltpu.make_async_copy(source, place, sems.at[i])
        for i, (source, place) in enumerate(zip(sources, local))
    ]
    for copy in copies:
        copy.start()
    tiles_ref, offsets_ref, amps_ref, coords_ref, weights_ref, modes_ref = local
    n_tile = send_ref.shape[0] // 2
    blocks = block_ref.shape[0]
    cells = cell_ref.shape[1]
    for copy in copies[:2]:
        copy.wait()
    shape = (n_tile, blocks)
    tile_of_row = lax.broadcasted_iota(jnp.int32, shape, 0)
    row = lax.broadcasted_iota(jnp.int32, (blocks, blocks), 0)
    column = lax.broadcasted_iota(jnp.int32, (blocks, blocks), 1)
    before = jnp.where(row < column, 1.0, 0.0).astype(jnp.bfloat16)
    same = jnp.where(row == column, 1.0, 0.0).astype(jnp.bfloat16)
    ones = jnp.ones((blocks, blocks), jnp.bfloat16)
    seen = jnp.zeros(shape, jnp.float32)
    picks = [jnp.zeros(shape, jnp.float32) for _ in range(2)]
    shifts = [jnp.zeros((n_tile, LANES), jnp.float32) for _ in range(2)]
    for k in range(tiles_ref.shape[0]):
        named = jnp.where(tiles_ref[pl.ds(k, 1), :] == tile_of_row, 1.0, 0.0)
        flags = named.astype(jnp.bfloat16)
        rank = seen + jnp.dot(flags, before, preferred_element_type=jnp.float32)
        seen = seen + jnp.dot(flags, ones, preferred_element_type=jnp.float32)
        offsets = [
            jnp.broadcast_to(offsets_ref[c, pl.ds(k, 1), :].astype(jnp.float32), (ATOM_BLOCK, blocks))
            for c in range(3)
        ]
        offsets = jnp.concatenate(offsets + [jnp.zeros((ATOM_BLOCK, blocks), jnp.float32)], axis=0)
        for slot in range(2):
            mine = jnp.where(rank == float(slot), named, 0.0)
            picks[slot] = picks[slot] + mine
            shifts[slot] = shifts[slot] + against_rows(
                mine.astype(jnp.bfloat16), offsets.astype(jnp.bfloat16)
            )
    for copy in copies[2:]:
        copy.wait()
    amps = jnp.broadcast_to(amps_ref[...], (16, amps_ref.shape[1])).astype(jnp.bfloat16)
    for component in range(3):
        moved = jnp.dot(amps, modes_ref[component], preferred_element_type=jnp.float32)
        places = coords_ref[pl.ds(component, 1), :] + moved[0:1]
        for cell in range(cells):
            cell_ref[component, pl.ds(cell, 1), :] = places[:, cell * LANES : (cell + 1) * LANES]
    cell_ref[3] = weights_ref[...]
    for i in range(4):
        block_ref[pl.ds(i, cells, stride=4), :] = regroup([cell_ref[c] for c in range(4)], i)
    parts = exact_parts(block_ref[...])
    for slot in range(2):
        pick = picks[slot].astype(jnp.bfloat16)
        high, middle, low = [jnp.dot(pick, part, preferred_element_type=jnp.float32) for part in parts]
        rows = ((high + middle) + low) + shifts[slot]
        steps = jnp.clip(rows - MIDDLE, -SPAN, SPAN) * PLACE_STEPS
        wide_ref[pl.ds(slot, n_tile, stride=2), :] = jnp.where(
            quarter_of(rows.shape) < 3, steps, rows * MASS_STEPS
        )
        pick_ref[slot] = against_rows(same, pick).astype(jnp.bfloat16)
    send_ref[...] = whole_steps(wide_ref[...])


def finish_kernel(voxels, atoms, back_ref, pick_ref, modes_ref, forces_ref, spread_ref, score_ref, wide_ref, block_ref):
    n_tile = pick_ref.shape[2]
    wide_ref[...] = back_ref[...].astype(jnp.float32)
    last = wide_ref[pl.ds(3, n_tile, stride=4), :]
    place = lax.broadcasted_iota(jnp.int32, (n_tile, LANES), 1) // 3
    ratio = jnp.sum(jnp.where(place == 3, last, 0.0), axis=1, keepdims=True)
    totals = jnp.sum(last, axis=0, keepdims=True)
    srm, srr, smm = [
        jnp.sum(jnp.where(place[0:1] == i, totals, 0.0), axis=1, keepdims=True) for i in range(3)
    ]
    root = jnp.sqrt(srr * smm)
    score = srm / root
    score_ref[...] = jnp.broadcast_to(score, score_ref.shape)
    map_scale = voxels / root
    model_scale = map_scale * (ratio - srm / srr)
    cells = forces_ref.shape[1] // LANES
    modes = jnp.zeros((1, modes_ref.shape[1]), jnp.float32)
    for component in range(3):
        pulled = wide_ref[pl.ds(component, n_tile, stride=4), :]
        pulled = pulled * map_scale + pltpu.roll(pulled, LANES // 2, 1) * model_scale
        parts = exact_parts(pulled)
        first, second = [
            sum([jnp.dot(pick_ref[slot], part, preferred_element_type=jnp.float32) for part in parts[::-1]])
            for slot in range(2)
        ]
        block_ref[component] = first + pltpu.roll(second, LANES - ATOM_BLOCK, 1)
        rows = regroup([block_ref[component, pl.ds(i, cells, stride=4), :] for i in range(4)], 0)
        for cell in range(cells):
            forces_ref[pl.ds(component, 1), cell * LANES : (cell + 1) * LANES] = rows[cell : cell + 1]
        force = jnp.broadcast_to(forces_ref[pl.ds(component, 1), :], (16, forces_ref.shape[1]))
        modes = modes + against_rows(force.astype(jnp.bfloat16), modes_ref[component])[0:1]
    modes = modes / jnp.sqrt(jnp.float32(atoms))
    half = spread_ref.shape[0] // 2
    for part in range(2):
        spread_ref[pl.ds(part, half, stride=2), :] = jnp.broadcast_to(
            modes[:, part * LANES : (part + 1) * LANES], (half, LANES)
        )


def unpack_rows(got_ref, wide_ref, place_ref):
    wide_ref[...] = from_steps(got_ref[...])
    groups = got_ref.shape[0] // 4
    rows = [wide_ref[pl.ds(i, groups, stride=4), :] for i in range(4)]
    for component in range(3):
        place_ref[component] = regroup(rows, component) * (1.0 / PLACE_STEPS) + MIDDLE
    place_ref[3] = regroup(rows, 3) * (1.0 / MASS_STEPS)


def chunk_row(place_ref, component, chunk, size):
    rows = size // LANES
    return jnp.concatenate(
        [place_ref[component, pl.ds(chunk * rows + i, 1), :] for i in range(rows)], axis=1
    )


def pipeline(chunks, build, use):
    build(0, 0)

    @pl.loop(0, chunks // 2)
    def _(step):
        build(1, 2 * step + 1)
        use(0, 2 * step)
        build(0, jnp.minimum(2 * step + 2, chunks - 2))
        use(1, 2 * step + 1)


def pair_of_lines(line_ref, z, size):
    return jnp.concatenate(
        [jnp.broadcast_to(line_ref[pl.ds(z + i, 1), :], (HIGHS, size)) for i in range(2)], axis=0
    )


LOWS = [low + 0.5 - STEP / 2 for low in range(STEP)]


def coarse_of(high):
    return STEP * high.astype(jnp.float32) + (STEP / 2 - MIDDLE)


def own_factor(low, width):
    coarse = coarse_of(lax.broadcasted_iota(jnp.int32, (EDGE, width), 1) % HIGHS)
    return jnp.exp2(-rate * (2.0 * LOWS[low] * coarse + LOWS[low] ** 2))


def splat_kernel(got_ref, out_ref, wide_ref, place_ref, line_ref, even_ref, odd_ref, even_weight_ref, odd_weight_ref, sum_ref):
    size = even_ref.shape[1]
    planes, weights = (even_ref, odd_ref), (even_weight_ref, odd_weight_ref)
    unpack_rows(got_ref, wide_ref, place_ref)
    sum_ref[...] = jnp.zeros_like(sum_ref)

    def build(slot, chunk):
        place_x, place_y, place_z, masses = [chunk_row(place_ref, i, chunk, size) for i in range(4)]
        place_x = place_x - MIDDLE
        along_x = factors(place_x, coarse_of(row_number(HIGHS, size)))[0]
        line_ref[slot] = factors(place_z, centers_of(size))[0]
        for z in range(0, EDGE, 2):
            line = pair_of_lines(line_ref.at[slot], z, size)
            block = line * jnp.concatenate([along_x, along_x], axis=0)
            planes[slot][pl.ds(z * HIGHS, 2 * HIGHS), :] = block.astype(jnp.bfloat16)
        along_y = masses * factors(place_y, centers_of(size))[0]
        near = jnp.clip(place_x, -SPAN, SPAN)
        for low in range(STEP):
            fine = jnp.exp2((2.0 * rate * LOWS[low]) * near)
            weights[slot][pl.ds(low * EDGE, EDGE), :] = (along_y * fine).astype(jnp.bfloat16)

    def use(slot, chunk):
        width = min(WIDTH, size)
        for part in range(size // width):
            atoms = pl.ds(part * width, width)
            sum_ref[...] += against_rows(planes[slot][:, atoms], weights[slot][:, atoms])

    pipeline(place_ref.shape[1] * LANES // size, build, use)
    total = sum_ref[...].T
    blocks = []
    for low in range(STEP):
        block = total[low * EDGE : (low + 1) * EDGE] * own_factor(low, EDGE * HIGHS)
        blocks += [block[:, i : i + LANES] for i in range(0, block.shape[1], LANES)]
    largest = blocks[0]
    for block in blocks[1:]:
        largest = jnp.maximum(largest, block)
    largest = jnp.max(jnp.max(largest, axis=0, keepdims=True), axis=1, keepdims=True)
    power = jnp.floor(jnp.log(jnp.clip(largest, 1e-30, 1e30)) * (1.0 / math.log(2.0)))
    steps = DENSITY_STEPS * jnp.exp2(-power)
    rows = [whole_steps(block * steps) for block in blocks]
    rows.append(whole_steps(jnp.broadcast_to(power, (POWER_ROWS, LANES))))
    for copy in range(out_ref.shape[0]):
        place = 0
        for block in rows:
            out_ref[copy, pl.ds(place, block.shape[0]), :] = block
            place += block.shape[0]


def density_of(parts_ref, part):
    count = parts_ref.shape[1] - POWER_ROWS
    power = from_steps(parts_ref[part, pl.ds(count, POWER_ROWS), :])[0:1]
    step = jnp.exp2(power) * (1.0 / DENSITY_STEPS)
    blocks = [from_steps(parts_ref[part, pl.ds(i, EDGE), :]) * step for i in range(0, count, EDGE)]
    return jnp.concatenate(blocks, axis=1)


def field_rows(row_ref, field):
    width = EDGE * HIGHS
    for low in range(STEP):
        rows = field[:, low * width : (low + 1) * width] * own_factor(low, width)
        row_ref[low * EDGE : (low + 1) * EDGE] = rows.astype(jnp.bfloat16)


def pull_rows(place_ref, row_ref, sum_ref, line_ref, even_ref, odd_ref, weight_ref, fine_ref):
    planes = (even_ref, odd_ref)
    size = even_ref.shape[2]
    width = min(WIDTH, size)

    def build(slot, chunk):
        place_x, place_y, place_z, masses = [chunk_row(place_ref, i, chunk, size) for i in range(4)]
        place_x = place_x - MIDDLE
        distance = coarse_of(row_number(HIGHS, size)) - place_x
        along_x = jnp.exp2(-rate * (distance * distance))
        near = jnp.clip(place_x, -SPAN, SPAN)
        for low in range(STEP):
            fine_ref[slot, pl.ds(low, 1), :] = jnp.exp2((2.0 * rate * LOWS[low]) * near)
        for i, values in enumerate(factors(place_z, centers_of(size))):
            line_ref[slot, i] = values.astype(jnp.bfloat16).astype(jnp.float32)
        for i, values in enumerate(factors(place_y, centers_of(size))):
            weight_ref[slot, i] = (masses * values).astype(jnp.bfloat16).astype(jnp.float32)
        plain = jnp.concatenate([along_x, along_x], axis=0)
        sloped = plain * jnp.concatenate([distance, distance], axis=0)
        for z in range(0, EDGE, 2):
            line = pair_of_lines(line_ref.at[slot, 0], z, size)
            slope_line = pair_of_lines(line_ref.at[slot, 1], z, size)
            place = pl.ds(z * HIGHS, 2 * HIGHS)
            planes[slot][0, place, :] = (line * plain).astype(jnp.bfloat16)
            planes[slot][1, place, :] = (line * sloped).astype(jnp.bfloat16)
            planes[slot][2, place, :] = (slope_line * plain).astype(jnp.bfloat16)

    def use(slot, chunk):
        for part in range(size // width):
            atoms = pl.ds(part * width, width)
            pulled = [
                jnp.dot(row_ref[...], planes[slot][i, :, atoms], preferred_element_type=jnp.float32)
                for i in range(3)
            ]
            sums = [jnp.zeros((EDGE, width), jnp.float32) for _ in range(3)]
            for low in range(STEP):
                fine = fine_ref[slot, pl.ds(low, 1), atoms]
                plain, by_x, by_z = [values[low * EDGE : (low + 1) * EDGE] for values in pulled]
                sums[0] = sums[0] + (by_x + LOWS[low] * plain) * fine
                sums[1] = sums[1] + plain * fine
                sums[2] = sums[2] + by_z * fine
            along_y, slope_y = [weight_ref[slot, i, :, atoms] for i in range(2)]
            rows = width // LANES
            for component, weight in enumerate((inverse_var * along_y, slope_y, along_y)):
                force = jnp.sum(sums[component] * weight, axis=0, keepdims=True)
                for i in range(rows):
                    row = (chunk * (size // width) + part) * rows + i
                    sum_ref[component, pl.ds(row, 1), :] = force[:, i * LANES : (i + 1) * LANES]

    pipeline(place_ref.shape[1] * LANES // size, build, use)


def map_kernel(got_ref, target_ref, sum_ref, wide_ref, place_ref, row_ref, *scratch):
    unpack_rows(got_ref, wide_ref, place_ref)
    field_rows(row_ref, target_ref[...].astype(jnp.float32))
    pull_rows(place_ref, row_ref, sum_ref, *scratch)


def pull_kernel(got_ref, parts_ref, target_ref, map_ref, out_ref, wide_ref, place_ref, row_ref, sum_ref, stage_ref, *scratch):
    unpack_rows(got_ref, wide_ref, place_ref)
    parts = [density_of(parts_ref, i) for i in range(4)]
    density = (parts[0] + parts[2]) + (parts[1] + parts[3])
    wide = target_ref[...].astype(jnp.float32)
    totals = [
        jnp.sum(jnp.sum(product, axis=0, keepdims=True), axis=1, keepdims=True)
        for product in (density * wide, density * density, wide * wide)
    ]
    ratio = jnp.where(totals[0] > 0.0, totals[0] / jnp.maximum(totals[1], 1e-30), 1.0)
    field_rows(row_ref, wide - ratio * density)
    pairs = place_ref.shape[1]
    lane = lax.broadcasted_iota(jnp.int32, (8, LANES), 1)
    last = jnp.zeros((8, LANES), jnp.float32)
    for place, value in enumerate(totals + [ratio]):
        for i, term in enumerate(exact_parts(jnp.broadcast_to(value, (8, LANES)))):
            last = jnp.where(lane == 3 * place + i, term.astype(jnp.float32), last)
    stage_ref[pl.ds(3, 2 * pairs, stride=4), :] = jnp.broadcast_to(last[0:1], (2 * pairs, LANES))
    pull_rows(place_ref, row_ref, sum_ref, *scratch)
    left = lax.broadcasted_iota(jnp.int32, (pairs, LANES), 1) < LANES // 2
    for component in range(3):
        first = sum_ref[component]
        second = (map_ref[component] - first) / ratio
        stage_ref[pl.ds(component, pairs, stride=8), :] = jnp.where(
            left, first, pltpu.roll(second, LANES // 2, 1)
        )
        stage_ref[pl.ds(4 + component, pairs, stride=8), :] = jnp.where(
            left, pltpu.roll(first, LANES // 2, 1), second
        )
    out_ref[...] = stage_ref[...].astype(jnp.bfloat16)


def call(kernel, name, out_shape, scratch, flops, *operands, source=pltpu.VMEM, limit=32):
    vmem = pl.BlockSpec(memory_space=pltpu.VMEM)
    return pl.pallas_call(
        kernel,
        out_shape=out_shape,
        in_specs=[pl.BlockSpec(memory_space=source)] * len(operands),
        out_specs=jax.tree.map(lambda _: vmem, out_shape),
        scratch_shapes=[pltpu.VMEM(*entry) if isinstance(entry, tuple) else entry for entry in scratch],
        compiler_params=pltpu.CompilerParams(vmem_limit_bytes=limit * 2**20),
        cost_estimate=pl.CostEstimate(flops=flops, bytes_accessed=2**20, transcendentals=2**20),
        name=name,
    )(*operands)


def pack(coords, weights, modes, amplitudes, tiles, offsets, n_tile):
    blocks = tiles.shape[1]
    operands = (tiles, offsets, amplitudes, coords, weights, modes)
    return call(
        pack_kernel,
        "pack",
        (
            jax.ShapeDtypeStruct((2 * n_tile, LANES), jnp.int16),
            jax.ShapeDtypeStruct((2, blocks, n_tile), jnp.bfloat16),
        ),
        [
            ((4, weights.shape[0], LANES), jnp.float32),
            ((blocks, LANES), jnp.float32),
            ((2 * n_tile, LANES), jnp.float32),
        ]
        + [(operand.shape, operand.dtype) for operand in operands]
        + [pltpu.SemaphoreType.DMA((len(operands),))],
        2**26,
        *operands,
        source=pltpu.HBM,
        limit=60,
    )


def finish(back, picks, modes, voxels, atoms, copies):
    blocks = picks.shape[1]
    return call(
        lambda *refs: finish_kernel(voxels, atoms, *refs),
        "finish",
        (
            jax.ShapeDtypeStruct((3, modes.shape[2]), jnp.float32),
            jax.ShapeDtypeStruct((2 * copies, LANES), jnp.float32),
            jax.ShapeDtypeStruct((1, LANES), jnp.float32),
        ),
        [(back.shape, jnp.float32), ((3, blocks, LANES), jnp.float32)],
        2**26,
        back,
        picks,
        modes,
    )


def splat(got, copies):
    groups = got.shape[0] // 4
    size = min(CHUNK, groups * LANES // 2)
    plane = ((EDGE * HIGHS, size), jnp.bfloat16)
    weight = ((EDGE * STEP, size), jnp.bfloat16)
    return call(
        splat_kernel,
        "splat",
        jax.ShapeDtypeStruct((copies, EDGE * PLANE // LANES + POWER_ROWS, LANES), jnp.int16),
        [
            ((4 * groups, LANES), jnp.float32), ((4, groups, LANES), jnp.float32),
            ((2, EDGE, size), jnp.float32),
            plane,
            plane,
            weight,
            weight,
            ((EDGE * HIGHS, EDGE * STEP), jnp.float32),
        ],
        2**29,
        got,
    )


def pull_scratch(groups):
    size = min(CHUNK, groups * LANES // 2)
    plane = ((3, EDGE * HIGHS, size), jnp.bfloat16)
    lines = ((2, 2, EDGE, size), jnp.float32)
    return [lines, plane, plane, lines, ((2, STEP, size), jnp.float32)]


def pull_map(got, target):
    groups = got.shape[0] // 4
    return call(
        map_kernel,
        "pull_map",
        jax.ShapeDtypeStruct((3, groups, LANES), jnp.float32),
        [((4 * groups, LANES), jnp.float32), ((4, groups, LANES), jnp.float32), ((STEP * EDGE, EDGE * HIGHS), jnp.bfloat16)] + pull_scratch(groups),
        2**32,
        got,
        target,
    )


def pull(got, parts, target, from_map):
    groups = got.shape[0] // 4
    return call(
        pull_kernel,
        "pull",
        jax.ShapeDtypeStruct((8 * groups, LANES), jnp.bfloat16),
        [
            ((4 * groups, LANES), jnp.float32), ((4, groups, LANES), jnp.float32),
            ((STEP * EDGE, EDGE * HIGHS), jnp.bfloat16),
            ((3, groups, LANES), jnp.float32),
            ((8 * groups, LANES), jnp.float32),
        ]
        + pull_scratch(groups),
        2**32,
        got,
        parts,
        target,
        from_map,
    )


TILE_AXES = ("y", "z", "core")


def exchange(values, axes):
    return lax.all_to_all(values, axes, split_axis=0, concat_axis=0, tiled=True)


def on_device(coords, weights, mode_vectors, amplitudes, density_map, block_tiles, block_offsets):
    a_dev = coords.shape[1]
    n_tile = lax.axis_size(TILE_AXES)
    n_seg = lax.axis_size("seg")
    modes = jnp.transpose(mode_vectors, (1, 0, 2))
    send, picks = pack(
        coords,
        weights.reshape(a_dev // LANES, LANES),
        modes,
        amplitudes.reshape(1, -1),
        block_tiles.T,
        jnp.transpose(block_offsets, (2, 1, 0)),
        n_tile,
    )
    got = exchange(send.reshape(n_tile, 2, LANES), TILE_AXES).reshape(2 * n_tile, LANES)
    target = density_map.reshape(EDGE, HIGHS, STEP, EDGE)
    target = jnp.transpose(target, (3, 2, 0, 1)).reshape(EDGE, PLANE)
    parts = exchange(splat(got, n_seg), "seg")
    pulled = pull(got, parts, target, pull_map(got, target))
    back = exchange(pulled.reshape(n_tile, 4, LANES), TILE_AXES).reshape(4 * n_tile, LANES)
    near, far = ("z", "core"), ("y", "seg")
    forces, spread, score = finish(
        back, picks, modes, float(n_tile * EDGE**3), a_dev * n_tile * n_seg, lax.axis_size(near)
    )
    near_sum = jnp.sum(exchange(spread.reshape(-1, 2, LANES), near), axis=0)
    copies = jnp.broadcast_to(near_sum[None], (lax.axis_size(far), 2, LANES))
    mode_grad = jnp.sum(exchange(copies, far), axis=0).reshape(-1)
    return (forces, mode_grad, score[0, 0])


def solution(mesh):
    split = Mesh(mesh.devices.reshape(8, 8, 2, 4), TILE_AXES + ("seg",))
    every = TILE_AXES + ("seg",)
    return jax.shard_map(
        on_device,
        mesh=split,
        in_specs=(
            P(None, every),
            P(every),
            P(None, None, every),
            P(),
            P(TILE_AXES, None),
            P(every, None),
            P(every, None, None),
        ),
        out_specs=(P(None, every), P(), P()),
        check_vma=False,
    )
```

```python
import math

import jax
import jax.numpy as jnp
from jax import lax
from jax.experimental import pallas as pl
from jax.experimental.pallas import tpu as pltpu
from jax.sharding import Mesh
from jax.sharding import PartitionSpec as P

EDGE = 32
ATOM_BLOCK = 32
PLANE = EDGE * EDGE
LANES = 128
CHUNK = 512
WIDTH = 256

STEP = 4
HIGHS = EDGE // STEP
MIDDLE = EDGE / 2

SPAN = 40.0
PLACE_STEPS = 32000.0 / SPAN
MASS_STEPS = 8000.0
DENSITY_STEPS = 16000.0
POWER_ROWS = 16

inverse_var = 1.0 / 2.25
rate = 0.5 * inverse_var / math.log(2.0)


def row_number(rows, columns):
    return lax.broadcasted_iota(jnp.int32, (rows, columns), 0)


def factors(places, centers):
    distance = centers - places
    profile = jnp.exp2(-rate * (distance * distance))
    return profile, inverse_var * distance * profile


def centers_of(columns):
    return row_number(EDGE, columns).astype(jnp.float32) + 0.5


def exact_parts(values):
    high = values.astype(jnp.bfloat16)
    rest = values - high.astype(jnp.float32)
    middle = rest.astype(jnp.bfloat16)
    return high, middle, (rest - middle.astype(jnp.float32)).astype(jnp.bfloat16)


def whole_steps(values):
    return jnp.floor(values + 0.5).astype(jnp.int32).astype(jnp.int16)


def from_steps(steps):
    return steps.astype(jnp.int32).astype(jnp.float32)


def against_rows(left, right):
    return lax.dot_general(
        left, right, (((1,), (1,)), ((), ())), preferred_element_type=jnp.float32
    )


def quarter_of(shape):
    return lax.broadcasted_iota(jnp.int32, shape, 1) // ATOM_BLOCK


def regroup(rows, target):
    quarter = quarter_of(rows[0].shape)
    result = jnp.zeros_like(rows[0])
    for i in range(4):
        moved = pltpu.roll(rows[i], ((i - target) % 4) * ATOM_BLOCK, 1) if i != target else rows[i]
        result = jnp.where(quarter == i, moved, result)
    return result


def pack_kernel(*refs):
    sources, (send_ref, pick_ref), (cell_ref, block_ref, wide_ref) = refs[:6], refs[6:8], refs[8:11]
    local, sems = refs[11:17], refs[17]
    pairs = list(zip(sources[:5], local[:5]))
    pairs += [(sources[5].at[i], local[5].at[i]) for i in range(3)]
    copies = [
        pltpu.make_async_copy(source, place, sems.at[i]) for i, (source, place) in enumerate(pairs)
    ]
    for copy in copies:
        copy.start()
    tiles_ref, offsets_ref, amps_ref, coords_ref, weights_ref, modes_ref = local
    n_tile = send_ref.shape[0] // 2
    blocks = block_ref.shape[0]
    cells = cell_ref.shape[1]
    for copy in copies[:2]:
        copy.wait()
    shape = (n_tile, blocks)
    tile_of_row = lax.broadcasted_iota(jnp.int32, shape, 0)
    row = lax.broadcasted_iota(jnp.int32, (blocks, blocks), 0)
    column = lax.broadcasted_iota(jnp.int32, (blocks, blocks), 1)
    before = jnp.where(row < column, 1.0, 0.0).astype(jnp.bfloat16)
    same = jnp.where(row == column, 1.0, 0.0).astype(jnp.bfloat16)
    ones = jnp.ones((blocks, blocks), jnp.bfloat16)
    seen = jnp.zeros(shape, jnp.float32)
    picks = [jnp.zeros(shape, jnp.float32) for _ in range(2)]
    shifts = [jnp.zeros((n_tile, LANES), jnp.float32) for _ in range(2)]
    for k in range(tiles_ref.shape[0]):
        named = jnp.where(tiles_ref[pl.ds(k, 1), :] == tile_of_row, 1.0, 0.0)
        flags = named.astype(jnp.bfloat16)
        rank = seen + jnp.dot(flags, before, preferred_element_type=jnp.float32)
        seen = seen + jnp.dot(flags, ones, preferred_element_type=jnp.float32)
        offsets = [
            jnp.broadcast_to(offsets_ref[c, pl.ds(k, 1), :].astype(jnp.float32), (ATOM_BLOCK, blocks))
            for c in range(3)
        ]
        offsets = jnp.concatenate(offsets + [jnp.zeros((ATOM_BLOCK, blocks), jnp.float32)], axis=0)
        for slot in range(2):
            mine = jnp.where(rank == float(slot), named, 0.0)
            picks[slot] = picks[slot] + mine
            shifts[slot] = shifts[slot] + against_rows(
                mine.astype(jnp.bfloat16), offsets.astype(jnp.bfloat16)
            )
    for copy in copies[2:5]:
        copy.wait()
    amps = jnp.broadcast_to(amps_ref[...], (16, amps_ref.shape[1])).astype(jnp.bfloat16)
    for component in range(3):
        copies[5 + component].wait()
        moved = jnp.dot(amps, modes_ref[component], preferred_element_type=jnp.float32)
        places = coords_ref[pl.ds(component, 1), :] + moved[0:1]
        for cell in range(cells):
            cell_ref[component, pl.ds(cell, 1), :] = places[:, cell * LANES : (cell + 1) * LANES]
    cell_ref[3] = weights_ref[...]
    for i in range(4):
        block_ref[pl.ds(i, cells, stride=4), :] = regroup([cell_ref[c] for c in range(4)], i)
    parts = exact_parts(block_ref[...])
    picks = [pick.astype(jnp.bfloat16) for pick in picks]
    both = jnp.concatenate(picks, axis=0)
    high, middle, low = [jnp.dot(both, part, preferred_element_type=jnp.float32) for part in parts]
    places = (high + middle) + low
    for slot in range(2):
        rows = places[slot * n_tile : (slot + 1) * n_tile] + shifts[slot]
        steps = jnp.clip(rows - MIDDLE, -SPAN, SPAN) * PLACE_STEPS
        wide_ref[pl.ds(slot, n_tile, stride=2), :] = jnp.where(
            quarter_of(rows.shape) < 3, steps, rows * MASS_STEPS
        )
        pick_ref[slot] = against_rows(same, picks[slot]).astype(jnp.bfloat16)
    send_ref[...] = whole_steps(wide_ref[...])


def finish_kernel(voxels, atoms, back_ref, pick_ref, modes_ref, forces_ref, spread_ref, score_ref, wide_ref, block_ref):
    blocks, n_tile = pick_ref.shape[1:]
    picks = pick_ref[...].reshape(2 * blocks, n_tile)
    wide_ref[...] = back_ref[...].astype(jnp.float32)
    last = wide_ref[pl.ds(3, n_tile, stride=4), :]
    place = lax.broadcasted_iota(jnp.int32, (n_tile, LANES), 1) // 3
    ratio = jnp.sum(jnp.where(place == 3, last, 0.0), axis=1, keepdims=True)
    totals = jnp.sum(last, axis=0, keepdims=True)
    srm, srr, smm = [
        jnp.sum(jnp.where(place[0:1] == i, totals, 0.0), axis=1, keepdims=True) for i in range(3)
    ]
    root = jnp.sqrt(srr * smm)
    score = srm / root
    score_ref[...] = jnp.broadcast_to(score, score_ref.shape)
    map_scale = voxels / root
    model_scale = map_scale * (ratio - srm / srr)
    cells = forces_ref.shape[1] // LANES
    modes = jnp.zeros((1, modes_ref.shape[1]), jnp.float32)
    for component in range(3):
        pulled = wide_ref[pl.ds(component, n_tile, stride=4), :]
        pulled = pulled * map_scale + pltpu.roll(pulled, LANES // 2, 1) * model_scale
        high, low, _ = exact_parts(pulled)
        sums = jnp.dot(picks, low, preferred_element_type=jnp.float32)
        sums = sums + jnp.dot(picks, high, preferred_element_type=jnp.float32)
        block_ref[component] = sums[:blocks] + pltpu.roll(sums[blocks:], LANES - ATOM_BLOCK, 1)
        rows = regroup([block_ref[component, pl.ds(i, cells, stride=4), :] for i in range(4)], 0)
        for cell in range(cells):
            forces_ref[pl.ds(component, 1), cell * LANES : (cell + 1) * LANES] = rows[cell : cell + 1]
        force = jnp.broadcast_to(forces_ref[pl.ds(component, 1), :], (16, forces_ref.shape[1]))
        modes = modes + against_rows(force.astype(jnp.bfloat16), modes_ref[component])[0:1]
    modes = modes / jnp.sqrt(jnp.float32(atoms))
    half = spread_ref.shape[0] // 2
    for part in range(2):
        spread_ref[pl.ds(part, half, stride=2), :] = jnp.broadcast_to(
            modes[:, part * LANES : (part + 1) * LANES], (half, LANES)
        )


def unpack_rows(got_ref, wide_ref, place_ref):
    wide_ref[...] = from_steps(got_ref[...])
    groups = got_ref.shape[0] // 4
    rows = [wide_ref[pl.ds(i, groups, stride=4), :] for i in range(4)]
    for component in range(3):
        place_ref[component] = regroup(rows, component) * (1.0 / PLACE_STEPS) + MIDDLE
    place_ref[3] = regroup(rows, 3) * (1.0 / MASS_STEPS)


def chunk_row(place_ref, component, chunk, size):
    rows = size // LANES
    return jnp.concatenate(
        [place_ref[component, pl.ds(chunk * rows + i, 1), :] for i in range(rows)], axis=1
    )


def pipeline(chunks, build, use):
    build(0, 0)

    @pl.loop(0, chunks // 2)
    def _(step):
        build(1, 2 * step + 1)
        use(0, 2 * step)
        build(0, jnp.minimum(2 * step + 2, chunks - 2))
        use(1, 2 * step + 1)


def pair_of_lines(line_ref, z, size):
    return jnp.concatenate(
        [jnp.broadcast_to(line_ref[pl.ds(z + i, 1), :], (HIGHS, size)) for i in range(2)], axis=0
    )


LOWS = [low + 0.5 - STEP / 2 for low in range(STEP)]


def coarse_of(high):
    return STEP * high.astype(jnp.float32) + (STEP / 2 - MIDDLE)


def own_factor(low, width):
    coarse = coarse_of(lax.broadcasted_iota(jnp.int32, (EDGE, width), 1) % HIGHS)
    return jnp.exp2(-rate * (2.0 * LOWS[low] * coarse + LOWS[low] ** 2))


def splat_kernel(got_ref, out_ref, wide_ref, place_ref, line_ref, even_ref, odd_ref, even_weight_ref, odd_weight_ref, sum_ref):
    size = even_ref.shape[1]
    planes, weights = (even_ref, odd_ref), (even_weight_ref, odd_weight_ref)
    unpack_rows(got_ref, wide_ref, place_ref)
    sum_ref[...] = jnp.zeros_like(sum_ref)

    def build(slot, chunk):
        place_x, place_y, place_z, masses = [chunk_row(place_ref, i, chunk, size) for i in range(4)]
        place_x = place_x - MIDDLE
        along_x = factors(place_x, coarse_of(row_number(HIGHS, size)))[0]
        line_ref[slot] = factors(place_z, centers_of(size))[0]
        for z in range(0, EDGE, 2):
            line = pair_of_lines(line_ref.at[slot], z, size)
            block = line * jnp.concatenate([along_x, along_x], axis=0)
            planes[slot][pl.ds(z * HIGHS, 2 * HIGHS), :] = block.astype(jnp.bfloat16)
        along_y = masses * factors(place_y, centers_of(size))[0]
        near = jnp.clip(place_x, -SPAN, SPAN)
        for low in range(STEP):
            fine = jnp.exp2((2.0 * rate * LOWS[low]) * near)
            weights[slot][pl.ds(low * EDGE, EDGE), :] = (along_y * fine).astype(jnp.bfloat16)

    def use(slot, chunk):
        width = min(WIDTH, size)
        for part in range(size // width):
            atoms = pl.ds(part * width, width)
            sum_ref[...] += against_rows(planes[slot][:, atoms], weights[slot][:, atoms])

    pipeline(place_ref.shape[1] * LANES // size, build, use)
    total = sum_ref[...].T
    blocks = []
    for low in range(STEP):
        block = total[low * EDGE : (low + 1) * EDGE] * own_factor(low, EDGE * HIGHS)
        blocks += [block[:, i : i + LANES] for i in range(0, block.shape[1], LANES)]
    largest = blocks[0]
    for block in blocks[1:]:
        largest = jnp.maximum(largest, block)
    largest = jnp.max(jnp.max(largest, axis=0, keepdims=True), axis=1, keepdims=True)
    power = jnp.floor(jnp.log(jnp.clip(largest, 1e-30, 1e30)) * (1.0 / math.log(2.0)))
    steps = DENSITY_STEPS * jnp.exp2(-power)
    rows = [whole_steps(block * steps) for block in blocks]
    rows.append(whole_steps(jnp.broadcast_to(power, (POWER_ROWS, LANES))))
    for copy in range(out_ref.shape[0]):
        place = 0
        for block in rows:
            out_ref[copy, pl.ds(place, block.shape[0]), :] = block
            place += block.shape[0]


def density_of(parts_ref, part):
    count = parts_ref.shape[1] - POWER_ROWS
    power = from_steps(parts_ref[part, pl.ds(count, POWER_ROWS), :])[0:1]
    step = jnp.exp2(power) * (1.0 / DENSITY_STEPS)
    blocks = [from_steps(parts_ref[part, pl.ds(i, EDGE), :]) * step for i in range(0, count, EDGE)]
    return jnp.concatenate(blocks, axis=1)


def field_rows(row_ref, field):
    width = EDGE * HIGHS
    for low in range(STEP):
        rows = field[:, low * width : (low + 1) * width] * own_factor(low, width)
        row_ref[low * EDGE : (low + 1) * EDGE] = rows.astype(jnp.bfloat16)


def pull_rows(place_ref, row_ref, sum_ref, line_ref, even_ref, odd_ref, weight_ref, fine_ref):
    planes = (even_ref, odd_ref)
    size = even_ref.shape[2]
    width = min(WIDTH, size)

    def build(slot, chunk):
        place_x, place_y, place_z, masses = [chunk_row(place_ref, i, chunk, size) for i in range(4)]
        place_x = place_x - MIDDLE
        distance = coarse_of(row_number(HIGHS, size)) - place_x
        along_x = jnp.exp2(-rate * (distance * distance))
        near = jnp.clip(place_x, -SPAN, SPAN)
        for low in range(STEP):
            fine_ref[slot, pl.ds(low, 1), :] = jnp.exp2((2.0 * rate * LOWS[low]) * near)
        for i, values in enumerate(factors(place_z, centers_of(size))):
            line_ref[slot, i] = values.astype(jnp.bfloat16).astype(jnp.float32)
        for i, values in enumerate(factors(place_y, centers_of(size))):
            weight_ref[slot, i] = (masses * values).astype(jnp.bfloat16).astype(jnp.float32)
        plain, sloped = [
            jnp.concatenate([values, values], axis=0).astype(jnp.bfloat16)
            for values in (along_x, distance * along_x)
        ]
        for z in range(0, EDGE, 2):
            line, slope_line = [
                pair_of_lines(line_ref.at[slot, i], z, size).astype(jnp.bfloat16) for i in range(2)
            ]
            place = pl.ds(z * HIGHS, 2 * HIGHS)
            planes[slot][0, place, :] = line * plain
            planes[slot][1, place, :] = line * sloped
            planes[slot][2, place, :] = slope_line * plain

    def use(slot, chunk):
        for part in range(size // width):
            atoms = pl.ds(part * width, width)
            pulled = [
                jnp.dot(row_ref[...], planes[slot][i, :, atoms], preferred_element_type=jnp.float32)
                for i in range(3)
            ]
            sums = [jnp.zeros((EDGE, width), jnp.float32) for _ in range(3)]
            for low in range(STEP):
                fine = fine_ref[slot, pl.ds(low, 1), atoms]
                plain, by_x, by_z = [values[low * EDGE : (low + 1) * EDGE] for values in pulled]
                sums[0] = sums[0] + (by_x + LOWS[low] * plain) * fine
                sums[1] = sums[1] + plain * fine
                sums[2] = sums[2] + by_z * fine
            along_y, slope_y = [weight_ref[slot, i, :, atoms] for i in range(2)]
            rows = width // LANES
            for component, weight in enumerate((inverse_var * along_y, slope_y, along_y)):
                force = jnp.sum(sums[component] * weight, axis=0, keepdims=True)
                for i in range(rows):
                    row = (chunk * (size // width) + part) * rows + i
                    sum_ref[component, pl.ds(row, 1), :] = force[:, i * LANES : (i + 1) * LANES]

    pipeline(place_ref.shape[1] * LANES // size, build, use)


def map_kernel(got_ref, target_ref, sum_ref, wide_ref, place_ref, row_ref, *scratch):
    unpack_rows(got_ref, wide_ref, place_ref)
    field_rows(row_ref, target_ref[...].astype(jnp.float32))
    pull_rows(place_ref, row_ref, sum_ref, *scratch)


def pull_kernel(got_ref, parts_ref, target_ref, map_ref, out_ref, wide_ref, place_ref, row_ref, sum_ref, stage_ref, *scratch):
    unpack_rows(got_ref, wide_ref, place_ref)
    parts = [density_of(parts_ref, i) for i in range(4)]
    density = (parts[0] + parts[2]) + (parts[1] + parts[3])
    wide = target_ref[...].astype(jnp.float32)
    totals = [
        jnp.sum(jnp.sum(product, axis=0, keepdims=True), axis=1, keepdims=True)
        for product in (density * wide, density * density, wide * wide)
    ]
    ratio = jnp.where(totals[0] > 0.0, totals[0] / jnp.maximum(totals[1], 1e-30), 1.0)
    field_rows(row_ref, wide - ratio * density)
    pairs = place_ref.shape[1]
    lane = lax.broadcasted_iota(jnp.int32, (8, LANES), 1)
    last = jnp.zeros((8, LANES), jnp.float32)
    for place, value in enumerate(totals + [ratio]):
        for i, term in enumerate(exact_parts(jnp.broadcast_to(value, (8, LANES)))):
            last = jnp.where(lane == 3 * place + i, term.astype(jnp.float32), last)
    stage_ref[pl.ds(3, 2 * pairs, stride=4), :] = jnp.broadcast_to(last[0:1], (2 * pairs, LANES))
    pull_rows(place_ref, row_ref, sum_ref, *scratch)
    left = lax.broadcasted_iota(jnp.int32, (pairs, LANES), 1) < LANES // 2
    for component in range(3):
        first = sum_ref[component]
        second = (map_ref[component] - first) / ratio
        stage_ref[pl.ds(component, pairs, stride=8), :] = jnp.where(
            left, first, pltpu.roll(second, LANES // 2, 1)
        )
        stage_ref[pl.ds(4 + component, pairs, stride=8), :] = jnp.where(
            left, pltpu.roll(first, LANES // 2, 1), second
        )
    out_ref[...] = stage_ref[...].astype(jnp.bfloat16)


def call(kernel, name, out_shape, scratch, flops, *operands, source=pltpu.VMEM, limit=32):
    vmem = pl.BlockSpec(memory_space=pltpu.VMEM)
    return pl.pallas_call(
        kernel,
        out_shape=out_shape,
        in_specs=[pl.BlockSpec(memory_space=source)] * len(operands),
        out_specs=jax.tree.map(lambda _: vmem, out_shape),
        scratch_shapes=[pltpu.VMEM(*entry) if isinstance(entry, tuple) else entry for entry in scratch],
        compiler_params=pltpu.CompilerParams(vmem_limit_bytes=limit * 2**20),
        cost_estimate=pl.CostEstimate(flops=flops, bytes_accessed=2**20, transcendentals=2**20),
        name=name,
    )(*operands)


def pack(coords, weights, modes, amplitudes, tiles, offsets, n_tile):
    blocks = tiles.shape[1]
    operands = (tiles, offsets, amplitudes, coords, weights, modes)
    return call(
        pack_kernel,
        "pack",
        (
            jax.ShapeDtypeStruct((2 * n_tile, LANES), jnp.int16),
            jax.ShapeDtypeStruct((2, blocks, n_tile), jnp.bfloat16),
        ),
        [
            ((4, weights.shape[0], LANES), jnp.float32),
            ((blocks, LANES), jnp.float32),
            ((2 * n_tile, LANES), jnp.float32),
        ]
        + [(operand.shape, operand.dtype) for operand in operands]
        + [pltpu.SemaphoreType.DMA((len(operands) + 2,))],
        2**26,
        *operands,
        source=pltpu.HBM,
        limit=60,
    )


def finish(back, picks, modes, voxels, atoms, copies):
    blocks = picks.shape[1]
    return call(
        lambda *refs: finish_kernel(voxels, atoms, *refs),
        "finish",
        (
            jax.ShapeDtypeStruct((3, modes.shape[2]), jnp.float32),
            jax.ShapeDtypeStruct((2 * copies, LANES), jnp.float32),
            jax.ShapeDtypeStruct((1, LANES), jnp.float32),
        ),
        [(back.shape, jnp.float32), ((3, blocks, LANES), jnp.float32)],
        2**26,
        back,
        picks,
        modes,
    )


def splat(got, copies):
    groups = got.shape[0] // 4
    size = min(CHUNK, groups * LANES // 2)
    plane = ((EDGE * HIGHS, size), jnp.bfloat16)
    weight = ((EDGE * STEP, size), jnp.bfloat16)
    return call(
        splat_kernel,
        "splat",
        jax.ShapeDtypeStruct((copies, EDGE * PLANE // LANES + POWER_ROWS, LANES), jnp.int16),
        [
            ((4 * groups, LANES), jnp.float32), ((4, groups, LANES), jnp.float32),
            ((2, EDGE, size), jnp.float32),
            plane,
            plane,
            weight,
            weight,
            ((EDGE * HIGHS, EDGE * STEP), jnp.float32),
        ],
        2**29,
        got,
    )


def pull_scratch(groups):
    size = min(CHUNK, groups * LANES // 2)
    plane = ((3, EDGE * HIGHS, size), jnp.bfloat16)
    lines = ((2, 2, EDGE, size), jnp.float32)
    return [lines, plane, plane, lines, ((2, STEP, size), jnp.float32)]


def pull_map(got, target):
    groups = got.shape[0] // 4
    return call(
        map_kernel,
        "pull_map",
        jax.ShapeDtypeStruct((3, groups, LANES), jnp.float32),
        [((4 * groups, LANES), jnp.float32), ((4, groups, LANES), jnp.float32), ((STEP * EDGE, EDGE * HIGHS), jnp.bfloat16)] + pull_scratch(groups),
        2**32,
        got,
        target,
    )


def pull(got, parts, target, from_map):
    groups = got.shape[0] // 4
    return call(
        pull_kernel,
        "pull",
        jax.ShapeDtypeStruct((8 * groups, LANES), jnp.bfloat16),
        [
            ((4 * groups, LANES), jnp.float32), ((4, groups, LANES), jnp.float32),
            ((STEP * EDGE, EDGE * HIGHS), jnp.bfloat16),
            ((3, groups, LANES), jnp.float32),
            ((8 * groups, LANES), jnp.float32),
        ]
        + pull_scratch(groups),
        2**32,
        got,
        parts,
        target,
        from_map,
    )


TILE_AXES = ("y", "z", "core")


def exchange(values, axes):
    return lax.all_to_all(values, axes, split_axis=0, concat_axis=0, tiled=True)


def on_device(coords, weights, mode_vectors, amplitudes, density_map, block_tiles, block_offsets):
    a_dev = coords.shape[1]
    n_tile = lax.axis_size(TILE_AXES)
    n_seg = lax.axis_size("seg")
    modes = jnp.transpose(mode_vectors, (1, 0, 2))
    send, picks = pack(
        coords,
        weights.reshape(a_dev // LANES, LANES),
        modes,
        amplitudes.reshape(1, -1),
        block_tiles.T,
        jnp.transpose(block_offsets, (2, 1, 0)),
        n_tile,
    )
    got = exchange(send.reshape(n_tile, 2, LANES), TILE_AXES).reshape(2 * n_tile, LANES)
    target = density_map.reshape(EDGE, HIGHS, STEP, EDGE)
    target = jnp.transpose(target, (3, 2, 0, 1)).reshape(EDGE, PLANE)
    parts = exchange(splat(got, n_seg), "seg")
    pulled = pull(got, parts, target, pull_map(got, target))
    back = exchange(pulled.reshape(n_tile, 4, LANES), TILE_AXES).reshape(4 * n_tile, LANES)
    near, far = ("z", "core"), ("y", "seg")
    forces, spread, score = finish(
        back, picks, modes, float(n_tile * EDGE**3), a_dev * n_tile * n_seg, lax.axis_size(near)
    )
    near_sum = jnp.sum(exchange(spread.reshape(-1, 2, LANES), near), axis=0)
    copies = jnp.broadcast_to(near_sum[None], (lax.axis_size(far), 2, LANES))
    mode_grad = jnp.sum(exchange(copies, far), axis=0).reshape(-1)
    return (forces, mode_grad, score[0, 0])


def solution(mesh):
    split = Mesh(mesh.devices.reshape(8, 8, 2, 4), TILE_AXES + ("seg",))
    every = TILE_AXES + ("seg",)
    return jax.shard_map(
        on_device,
        mesh=split,
        in_specs=(
            P(None, every),
            P(every),
            P(None, None, every),
            P(),
            P(TILE_AXES, None),
            P(every, None),
            P(every, None, None),
        ),
        out_specs=(P(None, every), P(), P()),
        check_vma=False,
    )
```

```python
import math

import jax
import jax.numpy as jnp
from jax import lax
from jax.experimental import pallas as pl
from jax.experimental.pallas import tpu as pltpu
from jax.sharding import Mesh
from jax.sharding import PartitionSpec as P

EDGE = 32
ATOM_BLOCK = 32
PLANE = EDGE * EDGE
LANES = 128
CHUNK = 512
WIDTH = 256

STEP = 4
HIGHS = EDGE // STEP
MIDDLE = EDGE / 2

SPAN = 40.0
PLACE_STEPS = 32000.0 / SPAN
MASS_STEPS = 8000.0
DENSITY_STEPS = 16000.0
POWER_ROWS = 16

inverse_var = 1.0 / 2.25
rate = 0.5 * inverse_var / math.log(2.0)


def row_number(rows, columns):
    return lax.broadcasted_iota(jnp.int32, (rows, columns), 0)


def factors(places, centers):
    distance = centers - places
    profile = jnp.exp2(-rate * (distance * distance))
    return profile, inverse_var * distance * profile


def centers_of(columns):
    return row_number(EDGE, columns).astype(jnp.float32) + 0.5


def exact_parts(values):
    high = values.astype(jnp.bfloat16)
    rest = values - high.astype(jnp.float32)
    middle = rest.astype(jnp.bfloat16)
    return high, middle, (rest - middle.astype(jnp.float32)).astype(jnp.bfloat16)


def whole_steps(values):
    return jnp.floor(values + 0.5).astype(jnp.int32).astype(jnp.int16)


def from_steps(steps):
    return steps.astype(jnp.int32).astype(jnp.float32)


def against_rows(left, right):
    return lax.dot_general(
        left, right, (((1,), (1,)), ((), ())), preferred_element_type=jnp.float32
    )


def quarter_of(shape):
    return lax.broadcasted_iota(jnp.int32, shape, 1) // ATOM_BLOCK


def regroup(rows, target):
    quarter = quarter_of(rows[0].shape)
    result = jnp.zeros_like(rows[0])
    for i in range(4):
        moved = pltpu.roll(rows[i], ((i - target) % 4) * ATOM_BLOCK, 1) if i != target else rows[i]
        result = jnp.where(quarter == i, moved, result)
    return result


def pack_kernel(*refs):
    sources, (send_ref, pick_ref), (cell_ref, block_ref, wide_ref) = refs[:6], refs[6:8], refs[8:11]
    local, sems = refs[11:17], refs[17]
    copies = [
        pltpu.make_async_copy(source, place, sems.at[i])
        for i, (source, place) in enumerate(zip(sources, local))
    ]
    for copy in copies:
        copy.start()
    tiles_ref, offsets_ref, amps_ref, coords_ref, weights_ref, modes_ref = local
    n_tile = send_ref.shape[0] // 2
    blocks = block_ref.shape[0]
    cells = cell_ref.shape[1]
    for copy in copies[:2]:
        copy.wait()
    shape = (n_tile, blocks)
    tile_of_row = lax.broadcasted_iota(jnp.int32, shape, 0)
    row = lax.broadcasted_iota(jnp.int32, (blocks, blocks), 0)
    column = lax.broadcasted_iota(jnp.int32, (blocks, blocks), 1)
    before = jnp.where(row < column, 1.0, 0.0).astype(jnp.bfloat16)
    same = jnp.where(row == column, 1.0, 0.0).astype(jnp.bfloat16)
    ones = jnp.ones((blocks, blocks), jnp.bfloat16)
    seen = jnp.zeros(shape, jnp.float32)
    picks = [jnp.zeros(shape, jnp.float32) for _ in range(2)]
    shifts = [jnp.zeros((n_tile, LANES), jnp.float32) for _ in range(2)]
    for k in range(tiles_ref.shape[0]):
        named = jnp.where(tiles_ref[pl.ds(k, 1), :] == tile_of_row, 1.0, 0.0)
        flags = named.astype(jnp.bfloat16)
        rank = seen + jnp.dot(flags, before, preferred_element_type=jnp.float32)
        seen = seen + jnp.dot(flags, ones, preferred_element_type=jnp.float32)
        offsets = [
            jnp.broadcast_to(offsets_ref[c, pl.ds(k, 1), :].astype(jnp.float32), (ATOM_BLOCK, blocks))
            for c in range(3)
        ]
        offsets = jnp.concatenate(offsets + [jnp.zeros((ATOM_BLOCK, blocks), jnp.float32)], axis=0)
        for slot in range(2):
            mine = jnp.where(rank == float(slot), named, 0.0)
            picks[slot] = picks[slot] + mine
            shifts[slot] = shifts[slot] + against_rows(
                mine.astype(jnp.bfloat16), offsets.astype(jnp.bfloat16)
            )
    for copy in copies[2:]:
        copy.wait()
    amps = jnp.broadcast_to(amps_ref[...], (16, amps_ref.shape[1])).astype(jnp.bfloat16)
    for component in range(3):
        moved = jnp.dot(amps, modes_ref[component], preferred_element_type=jnp.float32)
        places = coords_ref[pl.ds(component, 1), :] + moved[0:1]
        for cell in range(cells):
            cell_ref[component, pl.ds(cell, 1), :] = places[:, cell * LANES : (cell + 1) * LANES]
    cell_ref[3] = weights_ref[...]
    for i in range(4):
        block_ref[pl.ds(i, cells, stride=4), :] = regroup([cell_ref[c] for c in range(4)], i)
    parts = exact_parts(block_ref[...])
    picks = [pick.astype(jnp.bfloat16) for pick in picks]
    both = jnp.concatenate(picks, axis=0)
    high, middle, low = [jnp.dot(both, part, preferred_element_type=jnp.float32) for part in parts]
    places = (high + middle) + low
    for slot in range(2):
        rows = places[slot * n_tile : (slot + 1) * n_tile] + shifts[slot]
        steps = jnp.clip(rows - MIDDLE, -SPAN, SPAN) * PLACE_STEPS
        wide_ref[pl.ds(slot, n_tile, stride=2), :] = jnp.where(
            quarter_of(rows.shape) < 3, steps, rows * MASS_STEPS
        )
        pick_ref[slot] = against_rows(same, picks[slot]).astype(jnp.bfloat16)
    send_ref[...] = whole_steps(wide_ref[...])


def finish_kernel(voxels, atoms, back_ref, pick_ref, modes_ref, forces_ref, spread_ref, score_ref, wide_ref, block_ref):
    blocks, n_tile = pick_ref.shape[1:]
    picks = pick_ref[...].reshape(2 * blocks, n_tile)
    wide_ref[...] = back_ref[...].astype(jnp.float32)
    last = wide_ref[pl.ds(3, n_tile, stride=4), :]
    place = lax.broadcasted_iota(jnp.int32, (n_tile, LANES), 1) // 3
    ratio = jnp.sum(jnp.where(place == 3, last, 0.0), axis=1, keepdims=True)
    totals = jnp.sum(last, axis=0, keepdims=True)
    srm, srr, smm = [
        jnp.sum(jnp.where(place[0:1] == i, totals, 0.0), axis=1, keepdims=True) for i in range(3)
    ]
    root = jnp.sqrt(srr * smm)
    score = srm / root
    score_ref[...] = jnp.broadcast_to(score, score_ref.shape)
    map_scale = voxels / root
    model_scale = map_scale * (ratio - srm / srr)
    cells = forces_ref.shape[1] // LANES
    modes = jnp.zeros((1, modes_ref.shape[1]), jnp.float32)
    for component in range(3):
        pulled = wide_ref[pl.ds(component, n_tile, stride=4), :]
        pulled = pulled * map_scale + pltpu.roll(pulled, LANES // 2, 1) * model_scale
        high, low, _ = exact_parts(pulled)
        sums = jnp.dot(picks, low, preferred_element_type=jnp.float32)
        sums = sums + jnp.dot(picks, high, preferred_element_type=jnp.float32)
        block_ref[component] = sums[:blocks] + pltpu.roll(sums[blocks:], LANES - ATOM_BLOCK, 1)
        rows = regroup([block_ref[component, pl.ds(i, cells, stride=4), :] for i in range(4)], 0)
        for cell in range(cells):
            forces_ref[pl.ds(component, 1), cell * LANES : (cell + 1) * LANES] = rows[cell : cell + 1]
        force = jnp.broadcast_to(forces_ref[pl.ds(component, 1), :], (16, forces_ref.shape[1]))
        modes = modes + against_rows(force.astype(jnp.bfloat16), modes_ref[component])[0:1]
    modes = modes / jnp.sqrt(jnp.float32(atoms))
    half = spread_ref.shape[0] // 2
    for part in range(2):
        spread_ref[pl.ds(part, half, stride=2), :] = jnp.broadcast_to(
            modes[:, part * LANES : (part + 1) * LANES], (half, LANES)
        )


def unpack_rows(got_ref, wide_ref, place_ref):
    wide_ref[...] = from_steps(got_ref[...])
    groups = got_ref.shape[0] // 4
    rows = [wide_ref[pl.ds(i, groups, stride=4), :] for i in range(4)]
    for component in range(3):
        place_ref[component] = regroup(rows, component) * (1.0 / PLACE_STEPS) + MIDDLE
    place_ref[3] = regroup(rows, 3) * (1.0 / MASS_STEPS)


def chunk_row(place_ref, component, chunk, size):
    rows = size // LANES
    return jnp.concatenate(
        [place_ref[component, pl.ds(chunk * rows + i, 1), :] for i in range(rows)], axis=1
    )


def pipeline(chunks, build, use):
    build(0, 0)

    @pl.loop(0, chunks // 2)
    def _(step):
        build(1, 2 * step + 1)
        use(0, 2 * step)
        build(0, jnp.minimum(2 * step + 2, chunks - 2))
        use(1, 2 * step + 1)


def pair_of_lines(line_ref, z, size):
    return jnp.concatenate(
        [jnp.broadcast_to(line_ref[pl.ds(z + i, 1), :], (HIGHS, size)) for i in range(2)], axis=0
    )


LOWS = [low + 0.5 - STEP / 2 for low in range(STEP)]


def coarse_of(high):
    return STEP * high.astype(jnp.float32) + (STEP / 2 - MIDDLE)


def own_factor(low, width):
    coarse = coarse_of(lax.broadcasted_iota(jnp.int32, (EDGE, width), 1) % HIGHS)
    return jnp.exp2(-rate * (2.0 * LOWS[low] * coarse + LOWS[low] ** 2))


def splat_kernel(got_ref, out_ref, wide_ref, place_ref, line_ref, even_ref, odd_ref, even_weight_ref, odd_weight_ref, sum_ref):
    size = even_ref.shape[1]
    planes, weights = (even_ref, odd_ref), (even_weight_ref, odd_weight_ref)
    unpack_rows(got_ref, wide_ref, place_ref)
    sum_ref[...] = jnp.zeros_like(sum_ref)

    def build(slot, chunk):
        place_x, place_y, place_z, masses = [chunk_row(place_ref, i, chunk, size) for i in range(4)]
        place_x = place_x - MIDDLE
        along_x = factors(place_x, coarse_of(row_number(HIGHS, size)))[0]
        line_ref[slot] = factors(place_z, centers_of(size))[0]
        for z in range(0, EDGE, 2):
            line = pair_of_lines(line_ref.at[slot], z, size)
            block = line * jnp.concatenate([along_x, along_x], axis=0)
            planes[slot][pl.ds(z * HIGHS, 2 * HIGHS), :] = block.astype(jnp.bfloat16)
        along_y = masses * factors(place_y, centers_of(size))[0]
        near = jnp.clip(place_x, -SPAN, SPAN)
        for low in range(STEP):
            fine = jnp.exp2((2.0 * rate * LOWS[low]) * near)
            weights[slot][pl.ds(low * EDGE, EDGE), :] = (along_y * fine).astype(jnp.bfloat16)

    def use(slot, chunk):
        width = min(WIDTH, size)
        for part in range(size // width):
            atoms = pl.ds(part * width, width)
            sum_ref[...] += against_rows(planes[slot][:, atoms], weights[slot][:, atoms])

    pipeline(place_ref.shape[1] * LANES // size, build, use)
    total = sum_ref[...].T
    blocks = []
    for low in range(STEP):
        block = total[low * EDGE : (low + 1) * EDGE] * own_factor(low, EDGE * HIGHS)
        blocks += [block[:, i : i + LANES] for i in range(0, block.shape[1], LANES)]
    largest = blocks[0]
    for block in blocks[1:]:
        largest = jnp.maximum(largest, block)
    largest = jnp.max(jnp.max(largest, axis=0, keepdims=True), axis=1, keepdims=True)
    power = jnp.floor(jnp.log(jnp.clip(largest, 1e-30, 1e30)) * (1.0 / math.log(2.0)))
    steps = DENSITY_STEPS * jnp.exp2(-power)
    rows = [whole_steps(block * steps) for block in blocks]
    rows.append(whole_steps(jnp.broadcast_to(power, (POWER_ROWS, LANES))))
    for copy in range(out_ref.shape[0]):
        place = 0
        for block in rows:
            out_ref[copy, pl.ds(place, block.shape[0]), :] = block
            place += block.shape[0]


def density_of(parts_ref, part):
    count = parts_ref.shape[1] - POWER_ROWS
    power = from_steps(parts_ref[part, pl.ds(count, POWER_ROWS), :])[0:1]
    step = jnp.exp2(power) * (1.0 / DENSITY_STEPS)
    blocks = [from_steps(parts_ref[part, pl.ds(i, EDGE), :]) * step for i in range(0, count, EDGE)]
    return jnp.concatenate(blocks, axis=1)


def field_rows(row_ref, field):
    width = EDGE * HIGHS
    for low in range(STEP):
        rows = field[:, low * width : (low + 1) * width] * own_factor(low, width)
        row_ref[low * EDGE : (low + 1) * EDGE] = rows.astype(jnp.bfloat16)


def pull_rows(place_ref, row_ref, sum_ref, line_ref, even_ref, odd_ref, weight_ref, fine_ref):
    planes = (even_ref, odd_ref)
    size = even_ref.shape[2]
    width = min(WIDTH, size)

    def build(slot, chunk):
        place_x, place_y, place_z, masses = [chunk_row(place_ref, i, chunk, size) for i in range(4)]
        place_x = place_x - MIDDLE
        distance = coarse_of(row_number(HIGHS, size)) - place_x
        along_x = jnp.exp2(-rate * (distance * distance))
        near = jnp.clip(place_x, -SPAN, SPAN)
        for low in range(STEP):
            fine_ref[slot, pl.ds(low, 1), :] = jnp.exp2((2.0 * rate * LOWS[low]) * near)
        for i, values in enumerate(factors(place_z, centers_of(size))):
            line_ref[slot, i] = values.astype(jnp.bfloat16).astype(jnp.float32)
        for i, values in enumerate(factors(place_y, centers_of(size))):
            weight_ref[slot, i] = (masses * values).astype(jnp.bfloat16).astype(jnp.float32)
        plain = jnp.concatenate([along_x, along_x], axis=0)
        sloped = plain * jnp.concatenate([distance, distance], axis=0)
        for z in range(0, EDGE, 2):
            line = pair_of_lines(line_ref.at[slot, 0], z, size)
            slope_line = pair_of_lines(line_ref.at[slot, 1], z, size)
            place = pl.ds(z * HIGHS, 2 * HIGHS)
            planes[slot][0, place, :] = (line * plain).astype(jnp.bfloat16)
            planes[slot][1, place, :] = (line * sloped).astype(jnp.bfloat16)
            planes[slot][2, place, :] = (slope_line * plain).astype(jnp.bfloat16)

    def use(slot, chunk):
        for part in range(size // width):
            atoms = pl.ds(part * width, width)
            pulled = [
                jnp.dot(row_ref[...], planes[slot][i, :, atoms], preferred_element_type=jnp.float32)
                for i in range(3)
            ]
            fine = [fine_ref[slot, pl.ds(low, 1), atoms] for low in range(STEP)]
            plain, by_x, by_z = [
                [values[low * EDGE : (low + 1) * EDGE] * fine[low] for low in range(STEP)]
                for values in pulled
            ]
            by_low = 1.5 * (plain[3] - plain[0]) + 0.5 * (plain[2] - plain[1])
            sums = [(values[0] + values[1]) + (values[2] + values[3]) for values in (by_x, plain, by_z)]
            sums[0] = sums[0] + by_low
            along_y, slope_y = [weight_ref[slot, i, :, atoms] for i in range(2)]
            rows = width // LANES
            for component, weight in enumerate((inverse_var * along_y, slope_y, along_y)):
                force = jnp.sum(sums[component] * weight, axis=0, keepdims=True)
                for i in range(rows):
                    row = (chunk * (size // width) + part) * rows + i
                    sum_ref[component, pl.ds(row, 1), :] = force[:, i * LANES : (i + 1) * LANES]

    pipeline(place_ref.shape[1] * LANES // size, build, use)


def map_kernel(got_ref, target_ref, sum_ref, wide_ref, place_ref, row_ref, *scratch):
    unpack_rows(got_ref, wide_ref, place_ref)
    field_rows(row_ref, target_ref[...].astype(jnp.float32))
    pull_rows(place_ref, row_ref, sum_ref, *scratch)


def pull_kernel(got_ref, parts_ref, target_ref, map_ref, out_ref, wide_ref, place_ref, row_ref, sum_ref, stage_ref, *scratch):
    unpack_rows(got_ref, wide_ref, place_ref)
    parts = [density_of(parts_ref, i) for i in range(4)]
    density = (parts[0] + parts[2]) + (parts[1] + parts[3])
    wide = target_ref[...].astype(jnp.float32)
    totals = [
        jnp.sum(jnp.sum(product, axis=0, keepdims=True), axis=1, keepdims=True)
        for product in (density * wide, density * density, wide * wide)
    ]
    ratio = jnp.where(totals[0] > 0.0, totals[0] / jnp.maximum(totals[1], 1e-30), 1.0)
    field_rows(row_ref, wide - ratio * density)
    pairs = place_ref.shape[1]
    lane = lax.broadcasted_iota(jnp.int32, (8, LANES), 1)
    last = jnp.zeros((8, LANES), jnp.float32)
    for place, value in enumerate(totals + [ratio]):
        for i, term in enumerate(exact_parts(jnp.broadcast_to(value, (8, LANES)))):
            last = jnp.where(lane == 3 * place + i, term.astype(jnp.float32), last)
    stage_ref[pl.ds(3, 2 * pairs, stride=4), :] = jnp.broadcast_to(last[0:1], (2 * pairs, LANES))
    pull_rows(place_ref, row_ref, sum_ref, *scratch)
    left = lax.broadcasted_iota(jnp.int32, (pairs, LANES), 1) < LANES // 2
    for component in range(3):
        first = sum_ref[component]
        second = (map_ref[component] - first) / ratio
        stage_ref[pl.ds(component, pairs, stride=8), :] = jnp.where(
            left, first, pltpu.roll(second, LANES // 2, 1)
        )
        stage_ref[pl.ds(4 + component, pairs, stride=8), :] = jnp.where(
            left, pltpu.roll(first, LANES // 2, 1), second
        )
    out_ref[...] = stage_ref[...].astype(jnp.bfloat16)


def call(kernel, name, out_shape, scratch, flops, *operands, source=pltpu.VMEM, limit=32):
    vmem = pl.BlockSpec(memory_space=pltpu.VMEM)
    return pl.pallas_call(
        kernel,
        out_shape=out_shape,
        in_specs=[pl.BlockSpec(memory_space=source)] * len(operands),
        out_specs=jax.tree.map(lambda _: vmem, out_shape),
        scratch_shapes=[pltpu.VMEM(*entry) if isinstance(entry, tuple) else entry for entry in scratch],
        compiler_params=pltpu.CompilerParams(vmem_limit_bytes=limit * 2**20),
        cost_estimate=pl.CostEstimate(flops=flops, bytes_accessed=2**20, transcendentals=2**20),
        name=name,
    )(*operands)


def pack(coords, weights, modes, amplitudes, tiles, offsets, n_tile):
    blocks = tiles.shape[1]
    operands = (tiles, offsets, amplitudes, coords, weights, modes)
    return call(
        pack_kernel,
        "pack",
        (
            pltpu.VMEM((2 * n_tile, LANES), jnp.int16),
            jax.ShapeDtypeStruct((2, blocks, n_tile), jnp.bfloat16),
        ),
        [
            ((4, weights.shape[0], LANES), jnp.float32),
            ((blocks, LANES), jnp.float32),
            ((2 * n_tile, LANES), jnp.float32),
        ]
        + [(operand.shape, operand.dtype) for operand in operands]
        + [pltpu.SemaphoreType.DMA((len(operands),))],
        2**26,
        *operands,
        source=pltpu.HBM,
        limit=56,
    )


def finish(back, picks, modes, voxels, atoms, copies):
    blocks = picks.shape[1]
    return call(
        lambda *refs: finish_kernel(voxels, atoms, *refs),
        "finish",
        (
            jax.ShapeDtypeStruct((3, modes.shape[2]), jnp.float32),
            jax.ShapeDtypeStruct((2 * copies, LANES), jnp.float32),
            jax.ShapeDtypeStruct((1, LANES), jnp.float32),
        ),
        [(back.shape, jnp.float32), ((3, blocks, LANES), jnp.float32)],
        2**26,
        back,
        picks,
        modes,
    )


def splat(got, copies):
    groups = got.shape[0] // 4
    size = min(CHUNK, groups * LANES // 2)
    plane = ((EDGE * HIGHS, size), jnp.bfloat16)
    weight = ((EDGE * STEP, size), jnp.bfloat16)
    return call(
        splat_kernel,
        "splat",
        pltpu.VMEM((copies, EDGE * PLANE // LANES + POWER_ROWS, LANES), jnp.int16),
        [
            ((4 * groups, LANES), jnp.float32), ((4, groups, LANES), jnp.float32),
            ((2, EDGE, size), jnp.float32),
            plane,
            plane,
            weight,
            weight,
            ((EDGE * HIGHS, EDGE * STEP), jnp.float32),
        ],
        2**29,
        got,
    )


def pull_scratch(groups):
    size = min(CHUNK, groups * LANES // 2)
    plane = ((3, EDGE * HIGHS, size), jnp.bfloat16)
    lines = ((2, 2, EDGE, size), jnp.float32)
    return [lines, plane, plane, lines, ((2, STEP, size), jnp.float32)]


def pull_map(got, target):
    groups = got.shape[0] // 4
    return call(
        map_kernel,
        "pull_map",
        jax.ShapeDtypeStruct((3, groups, LANES), jnp.float32),
        [((4 * groups, LANES), jnp.float32), ((4, groups, LANES), jnp.float32), ((STEP * EDGE, EDGE * HIGHS), jnp.bfloat16)] + pull_scratch(groups),
        2**32,
        got,
        target,
    )


def pull(got, parts, target, from_map):
    groups = got.shape[0] // 4
    return call(
        pull_kernel,
        "pull",
        jax.ShapeDtypeStruct((8 * groups, LANES), jnp.bfloat16),
        [
            ((4 * groups, LANES), jnp.float32), ((4, groups, LANES), jnp.float32),
            ((STEP * EDGE, EDGE * HIGHS), jnp.bfloat16),
            ((3, groups, LANES), jnp.float32),
            ((8 * groups, LANES), jnp.float32),
        ]
        + pull_scratch(groups),
        2**32,
        got,
        parts,
        target,
        from_map,
    )


TILE_AXES = ("y", "z", "core")


def exchange(values, axes):
    return lax.all_to_all(values, axes, split_axis=0, concat_axis=0, tiled=True)


def on_device(coords, weights, mode_vectors, amplitudes, density_map, block_tiles, block_offsets):
    a_dev = coords.shape[1]
    n_tile = lax.axis_size(TILE_AXES)
    n_seg = lax.axis_size("seg")
    modes = jnp.transpose(mode_vectors, (1, 0, 2))
    send, picks = pack(
        coords,
        weights.reshape(a_dev // LANES, LANES),
        modes,
        amplitudes.reshape(1, -1),
        block_tiles.T,
        jnp.transpose(block_offsets, (2, 1, 0)),
        n_tile,
    )
    got = exchange(send.reshape(n_tile, 2, LANES), TILE_AXES).reshape(2 * n_tile, LANES)
    target = density_map.reshape(EDGE, HIGHS, STEP, EDGE)
    target = jnp.transpose(target, (3, 2, 0, 1)).reshape(EDGE, PLANE)
    parts = exchange(splat(got, n_seg), "seg")
    pulled = pull(got, parts, target, pull_map(got, target))
    back = exchange(pulled.reshape(n_tile, 4, LANES), TILE_AXES).reshape(4 * n_tile, LANES)
    near, far = ("z", "core"), ("y", "seg")
    forces, spread, score = finish(
        back, picks, modes, float(n_tile * EDGE**3), a_dev * n_tile * n_seg, lax.axis_size(near)
    )
    near_sum = jnp.sum(exchange(spread.reshape(-1, 2, LANES), near), axis=0)
    copies = jnp.broadcast_to(near_sum[None], (lax.axis_size(far), 2, LANES))
    mode_grad = jnp.sum(exchange(copies, far), axis=0).reshape(-1)
    return (forces, mode_grad, score[0, 0])


def solution(mesh):
    split = Mesh(mesh.devices.reshape(8, 8, 2, 4), TILE_AXES + ("seg",))
    every = TILE_AXES + ("seg",)
    return jax.shard_map(
        on_device,
        mesh=split,
        in_specs=(
            P(None, every),
            P(every),
            P(None, None, every),
            P(),
            P(TILE_AXES, None),
            P(every, None),
            P(every, None, None),
        ),
        out_specs=(P(None, every), P(), P()),
        check_vma=False,
    )
```

```python
import math

import jax
import jax.numpy as jnp
from jax import lax
from jax.experimental import pallas as pl
from jax.experimental.pallas import tpu as pltpu
from jax.sharding import Mesh
from jax.sharding import PartitionSpec as P

EDGE = 32
ATOM_BLOCK = 32
PLANE = EDGE * EDGE
LANES = 128
CHUNK = 512
WIDTH = 256

STEP = 4
HIGHS = EDGE // STEP
MIDDLE = EDGE / 2

SPAN = 40.0
PLACE_STEPS = 32000.0 / SPAN
MASS_STEPS = 8000.0
DENSITY_STEPS = 16000.0
POWER_ROWS = 16

inverse_var = 1.0 / 2.25
rate = 0.5 * inverse_var / math.log(2.0)


def row_number(rows, columns):
    return lax.broadcasted_iota(jnp.int32, (rows, columns), 0)


def factors(places, centers):
    distance = centers - places
    profile = jnp.exp2(-rate * (distance * distance))
    return profile, inverse_var * distance * profile


def centers_of(columns):
    return row_number(EDGE, columns).astype(jnp.float32) + 0.5


def exact_parts(values):
    high = values.astype(jnp.bfloat16)
    rest = values - high.astype(jnp.float32)
    middle = rest.astype(jnp.bfloat16)
    return high, middle, (rest - middle.astype(jnp.float32)).astype(jnp.bfloat16)


def whole_steps(values):
    return jnp.floor(values + 0.5).astype(jnp.int32).astype(jnp.int16)


def from_steps(steps):
    return steps.astype(jnp.int32).astype(jnp.float32)


def against_rows(left, right):
    return lax.dot_general(
        left, right, (((1,), (1,)), ((), ())), preferred_element_type=jnp.float32
    )


def quarter_of(shape):
    return lax.broadcasted_iota(jnp.int32, shape, 1) // ATOM_BLOCK


def regroup(rows, target):
    quarter = quarter_of(rows[0].shape)
    result = jnp.zeros_like(rows[0])
    for i in range(4):
        moved = pltpu.roll(rows[i], ((i - target) % 4) * ATOM_BLOCK, 1) if i != target else rows[i]
        result = jnp.where(quarter == i, moved, result)
    return result


def pack_kernel(*refs):
    sources, (send_ref, pick_ref), (cell_ref, block_ref, wide_ref) = refs[:6], refs[6:8], refs[8:11]
    local, sems = refs[11:17], refs[17]
    copies = [
        pltpu.make_async_copy(source, place, sems.at[i])
        for i, (source, place) in enumerate(zip(sources, local))
    ]
    for copy in copies:
        copy.start()
    tiles_ref, offsets_ref, amps_ref, coords_ref, weights_ref, modes_ref = local
    n_tile = send_ref.shape[0] // 2
    blocks = block_ref.shape[0]
    cells = cell_ref.shape[1]
    for copy in copies[:2]:
        copy.wait()
    shape = (n_tile, blocks)
    tile_of_row = lax.broadcasted_iota(jnp.int32, shape, 0)
    row = lax.broadcasted_iota(jnp.int32, (blocks, blocks), 0)
    column = lax.broadcasted_iota(jnp.int32, (blocks, blocks), 1)
    before = jnp.where(row < column, 1.0, 0.0).astype(jnp.bfloat16)
    same = jnp.where(row == column, 1.0, 0.0).astype(jnp.bfloat16)
    ones = jnp.ones((blocks, blocks), jnp.bfloat16)
    seen = jnp.zeros(shape, jnp.float32)
    picks = [jnp.zeros(shape, jnp.float32) for _ in range(2)]
    shifts = [jnp.zeros((n_tile, LANES), jnp.float32) for _ in range(2)]
    for k in range(tiles_ref.shape[0]):
        named = jnp.where(tiles_ref[pl.ds(k, 1), :] == tile_of_row, 1.0, 0.0)
        flags = named.astype(jnp.bfloat16)
        rank = seen + jnp.dot(flags, before, preferred_element_type=jnp.float32)
        seen = seen + jnp.dot(flags, ones, preferred_element_type=jnp.float32)
        offsets = [
            jnp.broadcast_to(offsets_ref[c, pl.ds(k, 1), :].astype(jnp.float32), (ATOM_BLOCK, blocks))
            for c in range(3)
        ]
        offsets = jnp.concatenate(offsets + [jnp.zeros((ATOM_BLOCK, blocks), jnp.float32)], axis=0)
        for slot in range(2):
            mine = jnp.where(rank == float(slot), named, 0.0)
            picks[slot] = picks[slot] + mine
            shifts[slot] = shifts[slot] + against_rows(
                mine.astype(jnp.bfloat16), offsets.astype(jnp.bfloat16)
            )
    for copy in copies[2:]:
        copy.wait()
    amps = jnp.broadcast_to(amps_ref[...], (16, amps_ref.shape[1])).astype(jnp.bfloat16)
    for component in range(3):
        moved = jnp.dot(amps, modes_ref[component], preferred_element_type=jnp.float32)
        places = coords_ref[pl.ds(component, 1), :] + moved[0:1]
        for cell in range(cells):
            cell_ref[component, pl.ds(cell, 1), :] = places[:, cell * LANES : (cell + 1) * LANES]
    cell_ref[3] = weights_ref[...]
    for i in range(4):
        block_ref[pl.ds(i, cells, stride=4), :] = regroup([cell_ref[c] for c in range(4)], i)
    parts = exact_parts(block_ref[...])
    picks = [pick.astype(jnp.bfloat16) for pick in picks]
    both = jnp.concatenate(picks, axis=0)
    high, middle, low = [jnp.dot(both, part, preferred_element_type=jnp.float32) for part in parts]
    places = (high + middle) + low
    for slot in range(2):
        rows = places[slot * n_tile : (slot + 1) * n_tile] + shifts[slot]
        steps = jnp.clip(rows - MIDDLE, -SPAN, SPAN) * PLACE_STEPS
        wide_ref[pl.ds(slot, n_tile, stride=2), :] = jnp.where(
            quarter_of(rows.shape) < 3, steps, rows * MASS_STEPS
        )
        pick_ref[slot] = against_rows(same, picks[slot]).astype(jnp.bfloat16)
    send_ref[...] = whole_steps(wide_ref[...])


def finish_kernel(voxels, atoms, back_ref, pick_ref, modes_ref, forces_ref, spread_ref, score_ref, wide_ref, block_ref):
    blocks, n_tile = pick_ref.shape[1:]
    picks = pick_ref[...].reshape(2 * blocks, n_tile)
    wide_ref[...] = back_ref[...].astype(jnp.float32)
    last = wide_ref[pl.ds(3, n_tile, stride=4), :]
    place = lax.broadcasted_iota(jnp.int32, (n_tile, LANES), 1) // 3
    ratio = jnp.sum(jnp.where(place == 3, last, 0.0), axis=1, keepdims=True)
    totals = jnp.sum(last, axis=0, keepdims=True)
    srm, srr, smm = [
        jnp.sum(jnp.where(place[0:1] == i, totals, 0.0), axis=1, keepdims=True) for i in range(3)
    ]
    root = jnp.sqrt(srr * smm)
    score = srm / root
    score_ref[...] = jnp.broadcast_to(score, score_ref.shape)
    map_scale = voxels / root
    model_scale = map_scale * (ratio - srm / srr)
    cells = forces_ref.shape[1] // LANES
    modes = jnp.zeros((1, modes_ref.shape[1]), jnp.float32)
    for component in range(3):
        pulled = wide_ref[pl.ds(component, n_tile, stride=4), :]
        pulled = pulled * map_scale + pltpu.roll(pulled, LANES // 2, 1) * model_scale
        high, low, _ = exact_parts(pulled)
        sums = jnp.dot(picks, low, preferred_element_type=jnp.float32)
        sums = sums + jnp.dot(picks, high, preferred_element_type=jnp.float32)
        block_ref[component] = sums[:blocks] + pltpu.roll(sums[blocks:], LANES - ATOM_BLOCK, 1)
        rows = regroup([block_ref[component, pl.ds(i, cells, stride=4), :] for i in range(4)], 0)
        for cell in range(cells):
            forces_ref[pl.ds(component, 1), cell * LANES : (cell + 1) * LANES] = rows[cell : cell + 1]
        force = jnp.broadcast_to(forces_ref[pl.ds(component, 1), :], (16, forces_ref.shape[1]))
        modes = modes + against_rows(force.astype(jnp.bfloat16), modes_ref[component])[0:1]
    modes = modes / jnp.sqrt(jnp.float32(atoms))
    half = spread_ref.shape[0] // 2
    for part in range(2):
        spread_ref[pl.ds(part, half, stride=2), :] = jnp.broadcast_to(
            modes[:, part * LANES : (part + 1) * LANES], (half, LANES)
        )


def unpack_rows(got_ref, wide_ref, place_ref):
    wide_ref[...] = from_steps(got_ref[...])
    groups = got_ref.shape[0] // 4
    rows = [wide_ref[pl.ds(i, groups, stride=4), :] for i in range(4)]
    for component in range(3):
        place_ref[component] = regroup(rows, component) * (1.0 / PLACE_STEPS) + MIDDLE
    place_ref[3] = regroup(rows, 3) * (1.0 / MASS_STEPS)


def chunk_row(place_ref, component, chunk, size):
    rows = size // LANES
    return jnp.concatenate(
        [place_ref[component, pl.ds(chunk * rows + i, 1), :] for i in range(rows)], axis=1
    )


def pipeline(chunks, build, use):
    build(0, 0)

    @pl.loop(0, chunks // 2 - 1)
    def _(step):
        build(1, 2 * step + 1)
        use(0, 2 * step)
        build(0, 2 * step + 2)
        use(1, 2 * step + 1)

    build(1, chunks - 1)
    use(0, chunks - 2)
    use(1, chunks - 1)


def pair_of_lines(line_ref, z, size):
    return jnp.concatenate(
        [jnp.broadcast_to(line_ref[pl.ds(z + i, 1), :], (HIGHS, size)) for i in range(2)], axis=0
    )


LOWS = [low + 0.5 - STEP / 2 for low in range(STEP)]


def coarse_of(high):
    return STEP * high.astype(jnp.float32) + (STEP / 2 - MIDDLE)


def own_factor(low, width):
    coarse = coarse_of(lax.broadcasted_iota(jnp.int32, (EDGE, width), 1) % HIGHS)
    return jnp.exp2(-rate * (2.0 * LOWS[low] * coarse + LOWS[low] ** 2))


def splat_kernel(got_ref, out_ref, wide_ref, place_ref, line_ref, even_ref, odd_ref, even_weight_ref, odd_weight_ref, sum_ref):
    size = even_ref.shape[1]
    planes, weights = (even_ref, odd_ref), (even_weight_ref, odd_weight_ref)
    unpack_rows(got_ref, wide_ref, place_ref)
    sum_ref[...] = jnp.zeros_like(sum_ref)

    def build(slot, chunk):
        place_x, place_y, place_z, masses = [chunk_row(place_ref, i, chunk, size) for i in range(4)]
        place_x = place_x - MIDDLE
        along_x = factors(place_x, coarse_of(row_number(HIGHS, size)))[0]
        line_ref[slot] = factors(place_z, centers_of(size))[0]
        for z in range(0, EDGE, 2):
            line = pair_of_lines(line_ref.at[slot], z, size)
            block = line * jnp.concatenate([along_x, along_x], axis=0)
            planes[slot][pl.ds(z * HIGHS, 2 * HIGHS), :] = block.astype(jnp.bfloat16)
        along_y = masses * factors(place_y, centers_of(size))[0]
        near = jnp.clip(place_x, -SPAN, SPAN)
        for low in range(STEP):
            fine = jnp.exp2((2.0 * rate * LOWS[low]) * near)
            weights[slot][pl.ds(low * EDGE, EDGE), :] = (along_y * fine).astype(jnp.bfloat16)

    def use(slot, chunk):
        width = min(WIDTH, size)
        for part in range(size // width):
            atoms = pl.ds(part * width, width)
            sum_ref[...] += against_rows(planes[slot][:, atoms], weights[slot][:, atoms])

    pipeline(place_ref.shape[1] * LANES // size, build, use)
    total = sum_ref[...].T
    blocks = []
    for low in range(STEP):
        block = total[low * EDGE : (low + 1) * EDGE] * own_factor(low, EDGE * HIGHS)
        blocks += [block[:, i : i + LANES] for i in range(0, block.shape[1], LANES)]
    largest = blocks[0]
    for block in blocks[1:]:
        largest = jnp.maximum(largest, block)
    largest = jnp.max(jnp.max(largest, axis=0, keepdims=True), axis=1, keepdims=True)
    power = jnp.floor(jnp.log(jnp.clip(largest, 1e-30, 1e30)) * (1.0 / math.log(2.0)))
    steps = DENSITY_STEPS * jnp.exp2(-power)
    rows = [whole_steps(block * steps) for block in blocks]
    rows.append(whole_steps(jnp.broadcast_to(power, (POWER_ROWS, LANES))))
    for copy in range(out_ref.shape[0]):
        place = 0
        for block in rows:
            out_ref[copy, pl.ds(place, block.shape[0]), :] = block
            place += block.shape[0]


def density_of(parts_ref, part):
    count = parts_ref.shape[1] - POWER_ROWS
    power = from_steps(parts_ref[part, pl.ds(count, POWER_ROWS), :])[0:1]
    step = jnp.exp2(power) * (1.0 / DENSITY_STEPS)
    blocks = [from_steps(parts_ref[part, pl.ds(i, EDGE), :]) * step for i in range(0, count, EDGE)]
    return jnp.concatenate(blocks, axis=1)


def field_rows(row_ref, field):
    width = EDGE * HIGHS
    for low in range(STEP):
        rows = field[:, low * width : (low + 1) * width] * own_factor(low, width)
        row_ref[low * EDGE : (low + 1) * EDGE] = rows.astype(jnp.bfloat16)


def pull_rows(keep, shape_ref, place_ref, row_ref, sum_ref, line_ref, even_ref, odd_ref, fine_ref):
    planes = (even_ref, odd_ref)
    size = even_ref.shape[2]
    width = min(WIDTH, size)

    def build(slot, chunk):
        place_x, place_y, place_z, masses = [chunk_row(place_ref, i, chunk, size) for i in range(4)]
        place_x = place_x - MIDDLE
        distance = coarse_of(row_number(HIGHS, size)) - place_x
        along_x = jnp.exp2(-rate * (distance * distance))
        near = jnp.clip(place_x, -SPAN, SPAN)
        lows = row_number(STEP, size).astype(jnp.float32) + LOWS[0]
        fine_ref[slot] = jnp.exp2((2.0 * rate) * lows * near)
        if keep:
            for i, values in enumerate(factors(place_z, centers_of(size))):
                shape_ref[chunk, i] = values.astype(jnp.bfloat16)
            for i, values in enumerate(factors(place_y, centers_of(size))):
                shape_ref[chunk, 2 + i] = (masses * values).astype(jnp.bfloat16)
        for i in range(2):
            line_ref[slot, i] = shape_ref[chunk, i].astype(jnp.float32)
        plain = jnp.concatenate([along_x, along_x], axis=0)
        sloped = plain * jnp.concatenate([distance, distance], axis=0)
        for z in range(0, EDGE, 2):
            line = pair_of_lines(line_ref.at[slot, 0], z, size)
            slope_line = pair_of_lines(line_ref.at[slot, 1], z, size)
            place = pl.ds(z * HIGHS, 2 * HIGHS)
            planes[slot][0, place, :] = (line * plain).astype(jnp.bfloat16)
            planes[slot][1, place, :] = (line * sloped).astype(jnp.bfloat16)
            planes[slot][2, place, :] = (slope_line * plain).astype(jnp.bfloat16)

    def use(slot, chunk):
        for part in range(size // width):
            atoms = pl.ds(part * width, width)
            pulled = [
                jnp.dot(row_ref[...], planes[slot][i, :, atoms], preferred_element_type=jnp.float32)
                for i in range(3)
            ]
            fine = [fine_ref[slot, pl.ds(low, 1), atoms] for low in range(STEP)]
            plain, by_x, by_z = [
                [values[low * EDGE : (low + 1) * EDGE] * fine[low] for low in range(STEP)]
                for values in pulled
            ]
            by_low = 1.5 * (plain[3] - plain[0]) + 0.5 * (plain[2] - plain[1])
            sums = [(values[0] + values[1]) + (values[2] + values[3]) for values in (by_x, plain, by_z)]
            sums[0] = sums[0] + by_low
            along_y, slope_y = [shape_ref[chunk, 2 + i, :, atoms].astype(jnp.float32) for i in range(2)]
            rows = width // LANES
            for component, weight in enumerate((inverse_var * along_y, slope_y, along_y)):
                force = jnp.sum(sums[component] * weight, axis=0, keepdims=True)
                for i in range(rows):
                    row = (chunk * (size // width) + part) * rows + i
                    sum_ref[component, pl.ds(row, 1), :] = force[:, i * LANES : (i + 1) * LANES]

    pipeline(place_ref.shape[1] * LANES // size, build, use)


def map_kernel(got_ref, target_ref, sum_ref, place_ref, shape_ref, wide_ref, row_ref, *scratch):
    unpack_rows(got_ref, wide_ref, place_ref)
    field_rows(row_ref, target_ref[...].astype(jnp.float32))
    pull_rows(True, shape_ref, place_ref, row_ref, sum_ref, *scratch)


def pull_kernel(parts_ref, target_ref, map_ref, place_ref, shape_ref, out_ref, row_ref, sum_ref, stage_ref, *scratch):
    parts = [density_of(parts_ref, i) for i in range(4)]
    density = (parts[0] + parts[2]) + (parts[1] + parts[3])
    wide = target_ref[...].astype(jnp.float32)
    totals = [
        jnp.sum(jnp.sum(product, axis=0, keepdims=True), axis=1, keepdims=True)
        for product in (density * wide, density * density, wide * wide)
    ]
    ratio = jnp.where(totals[0] > 0.0, totals[0] / jnp.maximum(totals[1], 1e-30), 1.0)
    field_rows(row_ref, wide - ratio * density)
    pairs = place_ref.shape[1]
    lane = lax.broadcasted_iota(jnp.int32, (8, LANES), 1)
    last = jnp.zeros((8, LANES), jnp.float32)
    for place, value in enumerate(totals + [ratio]):
        for i, term in enumerate(exact_parts(jnp.broadcast_to(value, (8, LANES)))):
            last = jnp.where(lane == 3 * place + i, term.astype(jnp.float32), last)
    stage_ref[pl.ds(3, 2 * pairs, stride=4), :] = jnp.broadcast_to(last[0:1], (2 * pairs, LANES))
    pull_rows(False, shape_ref, place_ref, row_ref, sum_ref, *scratch)
    left = lax.broadcasted_iota(jnp.int32, (pairs, LANES), 1) < LANES // 2
    for component in range(3):
        first = sum_ref[component]
        second = (map_ref[component] - first) / ratio
        stage_ref[pl.ds(component, pairs, stride=8), :] = jnp.where(
            left, first, pltpu.roll(second, LANES // 2, 1)
        )
        stage_ref[pl.ds(4 + component, pairs, stride=8), :] = jnp.where(
            left, pltpu.roll(first, LANES // 2, 1), second
        )
    out_ref[...] = stage_ref[...].astype(jnp.bfloat16)


def call(kernel, name, out_shape, scratch, flops, *operands, source=pltpu.VMEM, limit=32):
    vmem = pl.BlockSpec(memory_space=pltpu.VMEM)
    return pl.pallas_call(
        kernel,
        out_shape=out_shape,
        in_specs=[pl.BlockSpec(memory_space=source)] * len(operands),
        out_specs=jax.tree.map(lambda _: vmem, out_shape),
        scratch_shapes=[pltpu.VMEM(*entry) if isinstance(entry, tuple) else entry for entry in scratch],
        compiler_params=pltpu.CompilerParams(vmem_limit_bytes=limit * 2**20),
        cost_estimate=pl.CostEstimate(flops=flops, bytes_accessed=2**20, transcendentals=2**20),
        name=name,
    )(*operands)


def pack(coords, weights, modes, amplitudes, tiles, offsets, n_tile):
    blocks = tiles.shape[1]
    operands = (tiles, offsets, amplitudes, coords, weights, modes)
    return call(
        pack_kernel,
        "pack",
        (
            pltpu.VMEM((2 * n_tile, LANES), jnp.int16),
            jax.ShapeDtypeStruct((2, blocks, n_tile), jnp.bfloat16),
        ),
        [
            ((4, weights.shape[0], LANES), jnp.float32),
            ((blocks, LANES), jnp.float32),
            ((2 * n_tile, LANES), jnp.float32),
        ]
        + [(operand.shape, operand.dtype) for operand in operands]
        + [pltpu.SemaphoreType.DMA((len(operands),))],
        2**26,
        *operands,
        source=pltpu.HBM,
        limit=56,
    )


def finish(back, picks, modes, voxels, atoms, copies):
    blocks = picks.shape[1]
    return call(
        lambda *refs: finish_kernel(voxels, atoms, *refs),
        "finish",
        (
            jax.ShapeDtypeStruct((3, modes.shape[2]), jnp.float32),
            jax.ShapeDtypeStruct((2 * copies, LANES), jnp.float32),
            jax.ShapeDtypeStruct((1, LANES), jnp.float32),
        ),
        [(back.shape, jnp.float32), ((3, blocks, LANES), jnp.float32)],
        2**26,
        back,
        picks,
        modes,
    )


def splat(got, copies):
    groups = got.shape[0] // 4
    size = min(CHUNK, groups * LANES // 2)
    plane = ((EDGE * HIGHS, size), jnp.bfloat16)
    weight = ((EDGE * STEP, size), jnp.bfloat16)
    return call(
        splat_kernel,
        "splat",
        pltpu.VMEM((copies, EDGE * PLANE // LANES + POWER_ROWS, LANES), jnp.int16),
        [
            ((4 * groups, LANES), jnp.float32), ((4, groups, LANES), jnp.float32),
            ((2, EDGE, size), jnp.float32),
            plane,
            plane,
            weight,
            weight,
            ((EDGE * HIGHS, EDGE * STEP), jnp.float32),
        ],
        2**29,
        got,
    )


def pull_scratch(groups):
    size = min(CHUNK, groups * LANES // 2)
    plane = ((3, EDGE * HIGHS, size), jnp.bfloat16)
    return [((2, 2, EDGE, size), jnp.float32), plane, plane, ((2, STEP, size), jnp.float32)]


def pull_map(got, target):
    groups = got.shape[0] // 4
    size = min(CHUNK, groups * LANES // 2)
    return call(
        map_kernel,
        "pull_map",
        (
            pltpu.VMEM((3, groups, LANES), jnp.float32),
            pltpu.VMEM((4, groups, LANES), jnp.float32),
            pltpu.VMEM((groups * LANES // size, 4, EDGE, size), jnp.bfloat16),
        ),
        [((4 * groups, LANES), jnp.float32), ((STEP * EDGE, EDGE * HIGHS), jnp.bfloat16)]
        + pull_scratch(groups),
        2**32,
        got,
        target,
    )


def pull(parts, target, from_map):
    groups = from_map[0].shape[1]
    return call(
        pull_kernel,
        "pull",
        jax.ShapeDtypeStruct((8 * groups, LANES), jnp.bfloat16),
        [
            ((STEP * EDGE, EDGE * HIGHS), jnp.bfloat16),
            ((3, groups, LANES), jnp.float32),
            ((8 * groups, LANES), jnp.float32),
        ]
        + pull_scratch(groups),
        2**32,
        parts,
        target,
        *from_map,
    )


TILE_AXES = ("y", "z", "core")


def exchange(values, axes):
    return lax.all_to_all(values, axes, split_axis=0, concat_axis=0, tiled=True)


def on_device(coords, weights, mode_vectors, amplitudes, density_map, block_tiles, block_offsets):
    a_dev = coords.shape[1]
    n_tile = lax.axis_size(TILE_AXES)
    n_seg = lax.axis_size("seg")
    modes = jnp.transpose(mode_vectors, (1, 0, 2))
    send, picks = pack(
        coords,
        weights.reshape(a_dev // LANES, LANES),
        modes,
        amplitudes.reshape(1, -1),
        block_tiles.T,
        jnp.transpose(block_offsets, (2, 1, 0)),
        n_tile,
    )
    got = exchange(send.reshape(n_tile, 2, LANES), TILE_AXES).reshape(2 * n_tile, LANES)
    target = density_map.reshape(EDGE, HIGHS, STEP, EDGE)
    target = jnp.transpose(target, (3, 2, 0, 1)).reshape(EDGE, PLANE)
    parts = exchange(splat(got, n_seg), "seg")
    pulled = pull(parts, target, pull_map(got, target))
    back = exchange(pulled.reshape(n_tile, 4, LANES), TILE_AXES).reshape(4 * n_tile, LANES)
    near, far = ("z", "core"), ("y", "seg")
    forces, spread, score = finish(
        back, picks, modes, float(n_tile * EDGE**3), a_dev * n_tile * n_seg, lax.axis_size(near)
    )
    near_sum = jnp.sum(exchange(spread.reshape(-1, 2, LANES), near), axis=0)
    copies = jnp.broadcast_to(near_sum[None], (lax.axis_size(far), 2, LANES))
    mode_grad = jnp.sum(exchange(copies, far), axis=0).reshape(-1)
    return (forces, mode_grad, score[0, 0])


def solution(mesh):
    split = Mesh(mesh.devices.reshape(8, 8, 2, 4), TILE_AXES + ("seg",))
    every = TILE_AXES + ("seg",)
    return jax.shard_map(
        on_device,
        mesh=split,
        in_specs=(
            P(None, every),
            P(every),
            P(None, None, every),
            P(),
            P(TILE_AXES, None),
            P(every, None),
            P(every, None, None),
        ),
        out_specs=(P(None, every), P(), P()),
        check_vma=False,
    )
```

```python
import math

import jax
import jax.numpy as jnp
from jax import lax
from jax.experimental import pallas as pl
from jax.experimental.pallas import tpu as pltpu
from jax.sharding import Mesh
from jax.sharding import PartitionSpec as P

EDGE = 32
ATOM_BLOCK = 32
PLANE = EDGE * EDGE
LANES = 128
CHUNK = 512
WIDTH = 256

STEP = 4
HIGHS = EDGE // STEP
MIDDLE = EDGE / 2

SPAN = 40.0
PLACE_STEPS = 32000.0 / SPAN
MASS_STEPS = 8000.0
DENSITY_STEPS = 16000.0
POWER_ROWS = 16

inverse_var = 1.0 / 2.25
rate = 0.5 * inverse_var / math.log(2.0)


def row_number(rows, columns):
    return lax.broadcasted_iota(jnp.int32, (rows, columns), 0)


def factors(places, centers):
    distance = centers - places
    profile = jnp.exp2(-rate * (distance * distance))
    return profile, inverse_var * distance * profile


def centers_of(columns):
    return row_number(EDGE, columns).astype(jnp.float32) + 0.5


def exact_parts(values):
    high = values.astype(jnp.bfloat16)
    rest = values - high.astype(jnp.float32)
    middle = rest.astype(jnp.bfloat16)
    return high, middle, (rest - middle.astype(jnp.float32)).astype(jnp.bfloat16)


def whole_steps(values):
    return jnp.floor(values + 0.5).astype(jnp.int32).astype(jnp.int16)


def from_steps(steps):
    return steps.astype(jnp.int32).astype(jnp.float32)


def against_rows(left, right):
    return lax.dot_general(
        left, right, (((1,), (1,)), ((), ())), preferred_element_type=jnp.float32
    )


def quarter_of(shape):
    return lax.broadcasted_iota(jnp.int32, shape, 1) // ATOM_BLOCK


def regroup(rows, target):
    quarter = quarter_of(rows[0].shape)
    result = jnp.zeros_like(rows[0])
    for i in range(4):
        moved = pltpu.roll(rows[i], ((i - target) % 4) * ATOM_BLOCK, 1) if i != target else rows[i]
        result = jnp.where(quarter == i, moved, result)
    return result


def pack_kernel(*refs):
    sources, (send_ref, pick_ref), (cell_ref, block_ref, wide_ref) = refs[:6], refs[6:8], refs[8:11]
    local, sems = refs[11:17], refs[17]
    copies = [
        pltpu.make_async_copy(source, place, sems.at[i])
        for i, (source, place) in enumerate(zip(sources, local))
    ]
    for copy in copies:
        copy.start()
    tiles_ref, offsets_ref, amps_ref, coords_ref, weights_ref, modes_ref = local
    n_tile = send_ref.shape[0] // 2
    blocks = block_ref.shape[0]
    cells = cell_ref.shape[1]
    for copy in copies[:2]:
        copy.wait()
    shape = (n_tile, blocks)
    tile_of_row = lax.broadcasted_iota(jnp.int32, shape, 0)
    row = lax.broadcasted_iota(jnp.int32, (blocks, blocks), 0)
    column = lax.broadcasted_iota(jnp.int32, (blocks, blocks), 1)
    before = jnp.where(row < column, 1.0, 0.0).astype(jnp.bfloat16)
    same = jnp.where(row == column, 1.0, 0.0).astype(jnp.bfloat16)
    ones = jnp.ones((blocks, blocks), jnp.bfloat16)
    seen = jnp.zeros(shape, jnp.float32)
    picks = [jnp.zeros(shape, jnp.float32) for _ in range(2)]
    shifts = [jnp.zeros((n_tile, LANES), jnp.float32) for _ in range(2)]
    for k in range(tiles_ref.shape[0]):
        named = jnp.where(tiles_ref[pl.ds(k, 1), :] == tile_of_row, 1.0, 0.0)
        flags = named.astype(jnp.bfloat16)
        rank = seen + jnp.dot(flags, before, preferred_element_type=jnp.float32)
        seen = seen + jnp.dot(flags, ones, preferred_element_type=jnp.float32)
        offsets = [
            jnp.broadcast_to(offsets_ref[c, pl.ds(k, 1), :].astype(jnp.float32), (ATOM_BLOCK, blocks))
            for c in range(3)
        ]
        offsets = jnp.concatenate(offsets + [jnp.zeros((ATOM_BLOCK, blocks), jnp.float32)], axis=0)
        for slot in range(2):
            mine = jnp.where(rank == float(slot), named, 0.0)
            picks[slot] = picks[slot] + mine
            shifts[slot] = shifts[slot] + against_rows(
                mine.astype(jnp.bfloat16), offsets.astype(jnp.bfloat16)
            )
    for copy in copies[2:]:
        copy.wait()
    amps = jnp.broadcast_to(amps_ref[...], (16, amps_ref.shape[1])).astype(jnp.bfloat16)
    for component in range(3):
        moved = jnp.dot(amps, modes_ref[component], preferred_element_type=jnp.float32)
        places = coords_ref[pl.ds(component, 1), :] + moved[0:1]
        for cell in range(cells):
            cell_ref[component, pl.ds(cell, 1), :] = places[:, cell * LANES : (cell + 1) * LANES]
    cell_ref[3] = weights_ref[...]
    for i in range(4):
        block_ref[pl.ds(i, cells, stride=4), :] = regroup([cell_ref[c] for c in range(4)], i)
    parts = exact_parts(block_ref[...])
    picks = [pick.astype(jnp.bfloat16) for pick in picks]
    both = jnp.concatenate(picks, axis=0)
    high, middle, low = [jnp.dot(both, part, preferred_element_type=jnp.float32) for part in parts]
    places = (high + middle) + low
    for slot in range(2):
        rows = places[slot * n_tile : (slot + 1) * n_tile] + shifts[slot]
        steps = jnp.clip(rows - MIDDLE, -SPAN, SPAN) * PLACE_STEPS
        wide_ref[pl.ds(slot, n_tile, stride=2), :] = jnp.where(
            quarter_of(rows.shape) < 3, steps, rows * MASS_STEPS
        )
        pick_ref[slot] = against_rows(same, picks[slot]).astype(jnp.bfloat16)
    send_ref[...] = whole_steps(wide_ref[...])


def finish_kernel(voxels, atoms, back_ref, pick_ref, modes_ref, forces_ref, spread_ref, score_ref, wide_ref, block_ref):
    blocks, n_tile = pick_ref.shape[1:]
    picks = pick_ref[...].reshape(2 * blocks, n_tile)
    wide_ref[...] = back_ref[...].astype(jnp.float32)
    last = wide_ref[pl.ds(3, n_tile, stride=4), :]
    place = lax.broadcasted_iota(jnp.int32, (n_tile, LANES), 1) // 3
    ratio = jnp.sum(jnp.where(place == 3, last, 0.0), axis=1, keepdims=True)
    totals = jnp.sum(last, axis=0, keepdims=True)
    srm, srr, smm = [
        jnp.sum(jnp.where(place[0:1] == i, totals, 0.0), axis=1, keepdims=True) for i in range(3)
    ]
    root = jnp.sqrt(srr * smm)
    score = srm / root
    score_ref[...] = jnp.broadcast_to(score, score_ref.shape)
    map_scale = voxels / root
    model_scale = map_scale * (ratio - srm / srr)
    cells = forces_ref.shape[1] // LANES
    modes = jnp.zeros((1, modes_ref.shape[1]), jnp.float32)
    for component in range(3):
        pulled = wide_ref[pl.ds(component, n_tile, stride=4), :]
        pulled = pulled * map_scale + pltpu.roll(pulled, LANES // 2, 1) * model_scale
        high, low, _ = exact_parts(pulled)
        sums = jnp.dot(picks, low, preferred_element_type=jnp.float32)
        sums = sums + jnp.dot(picks, high, preferred_element_type=jnp.float32)
        block_ref[component] = sums[:blocks] + pltpu.roll(sums[blocks:], LANES - ATOM_BLOCK, 1)
        rows = regroup([block_ref[component, pl.ds(i, cells, stride=4), :] for i in range(4)], 0)
        for cell in range(cells):
            forces_ref[pl.ds(component, 1), cell * LANES : (cell + 1) * LANES] = rows[cell : cell + 1]
        force = jnp.broadcast_to(forces_ref[pl.ds(component, 1), :], (16, forces_ref.shape[1]))
        modes = modes + against_rows(force.astype(jnp.bfloat16), modes_ref[component])[0:1]
    modes = modes / jnp.sqrt(jnp.float32(atoms))
    half = spread_ref.shape[0] // 2
    for part in range(2):
        spread_ref[pl.ds(part, half, stride=2), :] = jnp.broadcast_to(
            modes[:, part * LANES : (part + 1) * LANES], (half, LANES)
        )


def unpack_rows(got_ref, wide_ref, place_ref):
    wide_ref[...] = from_steps(got_ref[...])
    groups = got_ref.shape[0] // 4
    rows = [wide_ref[pl.ds(i, groups, stride=4), :] for i in range(4)]
    for component in range(3):
        place_ref[component] = regroup(rows, component) * (1.0 / PLACE_STEPS) + MIDDLE
    place_ref[3] = regroup(rows, 3) * (1.0 / MASS_STEPS)


def chunk_row(place_ref, component, chunk, size):
    rows = size // LANES
    return jnp.concatenate(
        [place_ref[component, pl.ds(chunk * rows + i, 1), :] for i in range(rows)], axis=1
    )


def pipeline(chunks, build, use, last_apart=True):
    build(0, 0)

    @pl.loop(0, chunks // 2 - last_apart)
    def _(step):
        build(1, 2 * step + 1)
        use(0, 2 * step)
        build(0, 2 * step + 2 if last_apart else jnp.minimum(2 * step + 2, chunks - 2))
        use(1, 2 * step + 1)

    if last_apart:
        build(1, chunks - 1)
        use(0, chunks - 2)
        use(1, chunks - 1)


def pair_of_lines(line_ref, z, size):
    return jnp.concatenate(
        [jnp.broadcast_to(line_ref[pl.ds(z + i, 1), :], (HIGHS, size)) for i in range(2)], axis=0
    )


LOWS = [low + 0.5 - STEP / 2 for low in range(STEP)]


def coarse_of(high):
    return STEP * high.astype(jnp.float32) + (STEP / 2 - MIDDLE)


def own_factor(low, width):
    coarse = coarse_of(lax.broadcasted_iota(jnp.int32, (EDGE, width), 1) % HIGHS)
    return jnp.exp2(-rate * (2.0 * LOWS[low] * coarse + LOWS[low] ** 2))


def splat_kernel(got_ref, out_ref, wide_ref, place_ref, line_ref, even_ref, odd_ref, even_weight_ref, odd_weight_ref, fine_ref, sum_ref):
    size = even_ref.shape[1]
    planes, weights = (even_ref, odd_ref), (even_weight_ref, odd_weight_ref)
    unpack_rows(got_ref, wide_ref, place_ref)
    sum_ref[...] = jnp.zeros_like(sum_ref)

    def build(slot, chunk):
        place_x, place_y, place_z, masses = [chunk_row(place_ref, i, chunk, size) for i in range(4)]
        place_x = place_x - MIDDLE
        along_x = factors(place_x, coarse_of(row_number(HIGHS, size)))[0]
        doubled = jnp.concatenate([along_x, along_x], axis=0).astype(jnp.bfloat16)
        along_z = factors(place_z, centers_of(size))[0]
        line_ref[slot] = along_z.astype(jnp.bfloat16).astype(jnp.float32)
        for z in range(0, EDGE, 2):
            line = pair_of_lines(line_ref.at[slot], z, size).astype(jnp.bfloat16)
            planes[slot][pl.ds(z * HIGHS, 2 * HIGHS), :] = line * doubled
        along_y = (masses * factors(place_y, centers_of(size))[0]).astype(jnp.bfloat16)
        near = jnp.clip(place_x, -SPAN, SPAN)
        lows = row_number(STEP, size).astype(jnp.float32) + LOWS[0]
        fine_ref[slot] = jnp.exp2((2.0 * rate) * lows * near)
        for low in range(STEP):
            fine = jnp.broadcast_to(fine_ref[slot, pl.ds(low, 1), :], (EDGE, size))
            weights[slot][pl.ds(low * EDGE, EDGE), :] = along_y * fine.astype(jnp.bfloat16)

    def use(slot, chunk):
        width = min(WIDTH, size)
        for part in range(size // width):
            atoms = pl.ds(part * width, width)
            sum_ref[...] += against_rows(planes[slot][:, atoms], weights[slot][:, atoms])

    pipeline(place_ref.shape[1] * LANES // size, build, use, last_apart=False)
    total = sum_ref[...].T
    blocks = []
    for low in range(STEP):
        block = total[low * EDGE : (low + 1) * EDGE] * own_factor(low, EDGE * HIGHS)
        blocks += [block[:, i : i + LANES] for i in range(0, block.shape[1], LANES)]
    largest = blocks[0]
    for block in blocks[1:]:
        largest = jnp.maximum(largest, block)
    largest = jnp.max(jnp.max(largest, axis=0, keepdims=True), axis=1, keepdims=True)
    power = jnp.floor(jnp.log(jnp.clip(largest, 1e-30, 1e30)) * (1.0 / math.log(2.0)))
    steps = DENSITY_STEPS * jnp.exp2(-power)
    rows = [whole_steps(block * steps) for block in blocks]
    rows.append(whole_steps(jnp.broadcast_to(power, (POWER_ROWS, LANES))))
    for copy in range(out_ref.shape[0]):
        place = 0
        for block in rows:
            out_ref[copy, pl.ds(place, block.shape[0]), :] = block
            place += block.shape[0]


def density_of(parts_ref, part):
    count = parts_ref.shape[1] - POWER_ROWS
    power = from_steps(parts_ref[part, pl.ds(count, POWER_ROWS), :])[0:1]
    step = jnp.exp2(power) * (1.0 / DENSITY_STEPS)
    blocks = [from_steps(parts_ref[part, pl.ds(i, EDGE), :]) * step for i in range(0, count, EDGE)]
    return jnp.concatenate(blocks, axis=1)


def field_rows(row_ref, field):
    width = EDGE * HIGHS
    for low in range(STEP):
        rows = field[:, low * width : (low + 1) * width] * own_factor(low, width)
        row_ref[low * EDGE : (low + 1) * EDGE] = rows.astype(jnp.bfloat16)


def pull_rows(keep, shape_ref, place_ref, row_ref, sum_ref, line_ref, even_ref, odd_ref, fine_ref):
    planes = (even_ref, odd_ref)
    size = even_ref.shape[2]
    width = min(WIDTH, size)

    def build(slot, chunk):
        place_x, place_y, place_z, masses = [chunk_row(place_ref, i, chunk, size) for i in range(4)]
        place_x = place_x - MIDDLE
        distance = coarse_of(row_number(HIGHS, size)) - place_x
        along_x = jnp.exp2(-rate * (distance * distance))
        near = jnp.clip(place_x, -SPAN, SPAN)
        lows = row_number(STEP, size).astype(jnp.float32) + LOWS[0]
        fine_ref[slot] = jnp.exp2((2.0 * rate) * lows * near)
        if keep:
            for i, values in enumerate(factors(place_z, centers_of(size))):
                shape_ref[chunk, i] = values.astype(jnp.bfloat16)
            for i, values in enumerate(factors(place_y, centers_of(size))):
                shape_ref[chunk, 2 + i] = (masses * values).astype(jnp.bfloat16)
        for i in range(2):
            line_ref[slot, i] = shape_ref[chunk, i].astype(jnp.float32)
        plain = jnp.concatenate([along_x, along_x], axis=0)
        sloped = plain * jnp.concatenate([distance, distance], axis=0)
        for z in range(0, EDGE, 2):
            line = pair_of_lines(line_ref.at[slot, 0], z, size)
            slope_line = pair_of_lines(line_ref.at[slot, 1], z, size)
            place = pl.ds(z * HIGHS, 2 * HIGHS)
            planes[slot][0, place, :] = (line * plain).astype(jnp.bfloat16)
            planes[slot][1, place, :] = (line * sloped).astype(jnp.bfloat16)
            planes[slot][2, place, :] = (slope_line * plain).astype(jnp.bfloat16)

    def use(slot, chunk):
        for part in range(size // width):
            atoms = pl.ds(part * width, width)
            pulled = [
                jnp.dot(row_ref[...], planes[slot][i, :, atoms], preferred_element_type=jnp.float32)
                for i in range(3)
            ]
            fine = [fine_ref[slot, pl.ds(low, 1), atoms] for low in range(STEP)]
            plain, by_x, by_z = [
                [values[low * EDGE : (low + 1) * EDGE] * fine[low] for low in range(STEP)]
                for values in pulled
            ]
            by_low = 1.5 * (plain[3] - plain[0]) + 0.5 * (plain[2] - plain[1])
            sums = [(values[0] + values[1]) + (values[2] + values[3]) for values in (by_x, plain, by_z)]
            sums[0] = sums[0] + by_low
            along_y, slope_y = [shape_ref[chunk, 2 + i, :, atoms].astype(jnp.float32) for i in range(2)]
            rows = width // LANES
            for component, weight in enumerate((inverse_var * along_y, slope_y, along_y)):
                force = jnp.sum(sums[component] * weight, axis=0, keepdims=True)
                for i in range(rows):
                    row = (chunk * (size // width) + part) * rows + i
                    sum_ref[component, pl.ds(row, 1), :] = force[:, i * LANES : (i + 1) * LANES]

    pipeline(place_ref.shape[1] * LANES // size, build, use)


def map_kernel(got_ref, target_ref, sum_ref, place_ref, shape_ref, wide_ref, row_ref, *scratch):
    unpack_rows(got_ref, wide_ref, place_ref)
    field_rows(row_ref, target_ref[...].astype(jnp.float32))
    pull_rows(True, shape_ref, place_ref, row_ref, sum_ref, *scratch)


def pull_kernel(parts_ref, target_ref, map_ref, place_ref, shape_ref, out_ref, row_ref, sum_ref, stage_ref, *scratch):
    parts = [density_of(parts_ref, i) for i in range(4)]
    density = (parts[0] + parts[2]) + (parts[1] + parts[3])
    wide = target_ref[...].astype(jnp.float32)
    totals = [
        jnp.sum(jnp.sum(product, axis=0, keepdims=True), axis=1, keepdims=True)
        for product in (density * wide, density * density, wide * wide)
    ]
    ratio = jnp.where(totals[0] > 0.0, totals[0] / jnp.maximum(totals[1], 1e-30), 1.0)
    field_rows(row_ref, wide - ratio * density)
    pairs = place_ref.shape[1]
    lane = lax.broadcasted_iota(jnp.int32, (8, LANES), 1)
    last = jnp.zeros((8, LANES), jnp.float32)
    for place, value in enumerate(totals + [ratio]):
        for i, term in enumerate(exact_parts(jnp.broadcast_to(value, (8, LANES)))):
            last = jnp.where(lane == 3 * place + i, term.astype(jnp.float32), last)
    stage_ref[pl.ds(3, 2 * pairs, stride=4), :] = jnp.broadcast_to(last[0:1], (2 * pairs, LANES))
    pull_rows(False, shape_ref, place_ref, row_ref, sum_ref, *scratch)
    left = lax.broadcasted_iota(jnp.int32, (pairs, LANES), 1) < LANES // 2
    for component in range(3):
        first = sum_ref[component]
        second = (map_ref[component] - first) / ratio
        stage_ref[pl.ds(component, pairs, stride=8), :] = jnp.where(
            left, first, pltpu.roll(second, LANES // 2, 1)
        )
        stage_ref[pl.ds(4 + component, pairs, stride=8), :] = jnp.where(
            left, pltpu.roll(first, LANES // 2, 1), second
        )
    out_ref[...] = stage_ref[...].astype(jnp.bfloat16)


def call(kernel, name, out_shape, scratch, flops, *operands, source=pltpu.VMEM, limit=32):
    vmem = pl.BlockSpec(memory_space=pltpu.VMEM)
    return pl.pallas_call(
        kernel,
        out_shape=out_shape,
        in_specs=[pl.BlockSpec(memory_space=source)] * len(operands),
        out_specs=jax.tree.map(lambda _: vmem, out_shape),
        scratch_shapes=[pltpu.VMEM(*entry) if isinstance(entry, tuple) else entry for entry in scratch],
        compiler_params=pltpu.CompilerParams(vmem_limit_bytes=limit * 2**20),
        cost_estimate=pl.CostEstimate(flops=flops, bytes_accessed=2**20, transcendentals=2**20),
        name=name,
    )(*operands)


def pack(coords, weights, modes, amplitudes, tiles, offsets, n_tile):
    blocks = tiles.shape[1]
    operands = (tiles, offsets, amplitudes, coords, weights, modes)
    return call(
        pack_kernel,
        "pack",
        (
            pltpu.VMEM((2 * n_tile, LANES), jnp.int16),
            jax.ShapeDtypeStruct((2, blocks, n_tile), jnp.bfloat16),
        ),
        [
            ((4, weights.shape[0], LANES), jnp.float32),
            ((blocks, LANES), jnp.float32),
            ((2 * n_tile, LANES), jnp.float32),
        ]
        + [(operand.shape, operand.dtype) for operand in operands]
        + [pltpu.SemaphoreType.DMA((len(operands),))],
        2**26,
        *operands,
        source=pltpu.HBM,
        limit=56,
    )


def finish(back, picks, modes, voxels, atoms, copies):
    blocks = picks.shape[1]
    return call(
        lambda *refs: finish_kernel(voxels, atoms, *refs),
        "finish",
        (
            jax.ShapeDtypeStruct((3, modes.shape[2]), jnp.float32),
            jax.ShapeDtypeStruct((2 * copies, LANES), jnp.float32),
            jax.ShapeDtypeStruct((1, LANES), jnp.float32),
        ),
        [(back.shape, jnp.float32), ((3, blocks, LANES), jnp.float32)],
        2**26,
        back,
        picks,
        modes,
    )


def splat(got, copies):
    groups = got.shape[0] // 4
    size = min(CHUNK, groups * LANES // 2)
    plane = ((EDGE * HIGHS, size), jnp.bfloat16)
    weight = ((EDGE * STEP, size), jnp.bfloat16)
    return call(
        splat_kernel,
        "splat",
        pltpu.VMEM((copies, EDGE * PLANE // LANES + POWER_ROWS, LANES), jnp.int16),
        [
            ((4 * groups, LANES), jnp.float32), ((4, groups, LANES), jnp.float32),
            ((2, EDGE, size), jnp.float32),
            plane,
            plane,
            weight,
            weight,
            ((2, STEP, size), jnp.float32),
            ((EDGE * HIGHS, EDGE * STEP), jnp.float32),
        ],
        2**29,
        got,
    )


def pull_scratch(groups):
    size = min(CHUNK, groups * LANES // 2)
    plane = ((3, EDGE * HIGHS, size), jnp.bfloat16)
    return [((2, 2, EDGE, size), jnp.float32), plane, plane, ((2, STEP, size), jnp.float32)]


def pull_map(got, target):
    groups = got.shape[0] // 4
    size = min(CHUNK, groups * LANES // 2)
    return call(
        map_kernel,
        "pull_map",
        (
            pltpu.VMEM((3, groups, LANES), jnp.float32),
            pltpu.VMEM((4, groups, LANES), jnp.float32),
            pltpu.VMEM((groups * LANES // size, 4, EDGE, size), jnp.bfloat16),
        ),
        [((4 * groups, LANES), jnp.float32), ((STEP * EDGE, EDGE * HIGHS), jnp.bfloat16)]
        + pull_scratch(groups),
        2**32,
        got,
        target,
    )


def pull(parts, target, from_map):
    groups = from_map[0].shape[1]
    return call(
        pull_kernel,
        "pull",
        jax.ShapeDtypeStruct((8 * groups, LANES), jnp.bfloat16),
        [
            ((STEP * EDGE, EDGE * HIGHS), jnp.bfloat16),
            ((3, groups, LANES), jnp.float32),
            ((8 * groups, LANES), jnp.float32),
        ]
        + pull_scratch(groups),
        2**32,
        parts,
        target,
        *from_map,
    )


TILE_AXES = ("y", "z", "core")


def exchange(values, axes):
    return lax.all_to_all(values, axes, split_axis=0, concat_axis=0, tiled=True)


def on_device(coords, weights, mode_vectors, amplitudes, density_map, block_tiles, block_offsets):
    a_dev = coords.shape[1]
    n_tile = lax.axis_size(TILE_AXES)
    n_seg = lax.axis_size("seg")
    modes = jnp.transpose(mode_vectors, (1, 0, 2))
    send, picks = pack(
        coords,
        weights.reshape(a_dev // LANES, LANES),
        modes,
        amplitudes.reshape(1, -1),
        block_tiles.T,
        jnp.transpose(block_offsets, (2, 1, 0)),
        n_tile,
    )
    got = exchange(send.reshape(n_tile, 2, LANES), TILE_AXES).reshape(2 * n_tile, LANES)
    target = density_map.reshape(EDGE, HIGHS, STEP, EDGE)
    target = jnp.transpose(target, (3, 2, 0, 1)).reshape(EDGE, PLANE)
    parts = exchange(splat(got, n_seg), "seg")
    pulled = pull(parts, target, pull_map(got, target))
    back = exchange(pulled.reshape(n_tile, 4, LANES), TILE_AXES).reshape(4 * n_tile, LANES)
    near, far = ("z", "core"), ("y", "seg")
    forces, spread, score = finish(
        back, picks, modes, float(n_tile * EDGE**3), a_dev * n_tile * n_seg, lax.axis_size(near)
    )
    near_sum = jnp.sum(exchange(spread.reshape(-1, 2, LANES), near), axis=0)
    copies = jnp.broadcast_to(near_sum[None], (lax.axis_size(far), 2, LANES))
    mode_grad = jnp.sum(exchange(copies, far), axis=0).reshape(-1)
    return (forces, mode_grad, score[0, 0])


def solution(mesh):
    split = Mesh(mesh.devices.reshape(8, 8, 2, 4), TILE_AXES + ("seg",))
    every = TILE_AXES + ("seg",)
    return jax.shard_map(
        on_device,
        mesh=split,
        in_specs=(
            P(None, every),
            P(every),
            P(None, None, every),
            P(),
            P(TILE_AXES, None),
            P(every, None),
            P(every, None, None),
        ),
        out_specs=(P(None, every), P(), P()),
        check_vma=False,
    )
```

```python
import math

import jax
import jax.numpy as jnp
from jax import lax
from jax.experimental import pallas as pl
from jax.experimental.pallas import tpu as pltpu
from jax.sharding import Mesh
from jax.sharding import PartitionSpec as P

EDGE = 32
ATOM_BLOCK = 32
PLANE = EDGE * EDGE
LANES = 128
CHUNK = 512
WIDTH = 256

STEP = 4
HIGHS = EDGE // STEP
MIDDLE = EDGE / 2

SPAN = 40.0
PLACE_STEPS = 32000.0 / SPAN
MASS_STEPS = 8000.0
DENSITY_STEPS = 16000.0
POWER_ROWS = 16

inverse_var = 1.0 / 2.25
rate = 0.5 * inverse_var / math.log(2.0)


def row_number(rows, columns):
    return lax.broadcasted_iota(jnp.int32, (rows, columns), 0)


def factors(places, centers):
    distance = centers - places
    profile = jnp.exp2(-rate * (distance * distance))
    return profile, inverse_var * distance * profile


def centers_of(columns):
    return row_number(EDGE, columns).astype(jnp.float32) + 0.5


def exact_parts(values):
    high = values.astype(jnp.bfloat16)
    rest = values - high.astype(jnp.float32)
    middle = rest.astype(jnp.bfloat16)
    return high, middle, (rest - middle.astype(jnp.float32)).astype(jnp.bfloat16)


def whole_steps(values):
    return jnp.floor(values + 0.5).astype(jnp.int32).astype(jnp.int16)


def from_steps(steps):
    return steps.astype(jnp.int32).astype(jnp.float32)


def against_rows(left, right):
    return lax.dot_general(
        left, right, (((1,), (1,)), ((), ())), preferred_element_type=jnp.float32
    )


def quarter_of(shape):
    return lax.broadcasted_iota(jnp.int32, shape, 1) // ATOM_BLOCK


def regroup(rows, target):
    quarter = quarter_of(rows[0].shape)
    result = jnp.zeros_like(rows[0])
    for i in range(4):
        moved = pltpu.roll(rows[i], ((i - target) % 4) * ATOM_BLOCK, 1) if i != target else rows[i]
        result = jnp.where(quarter == i, moved, result)
    return result


def pack_kernel(*refs):
    sources, (send_ref, pick_ref), (cell_ref, block_ref, wide_ref) = refs[:6], refs[6:8], refs[8:11]
    local, sems = refs[11:17], refs[17]
    copies = [
        pltpu.make_async_copy(source, place, sems.at[i])
        for i, (source, place) in enumerate(zip(sources, local))
    ]
    for copy in copies:
        copy.start()
    tiles_ref, offsets_ref, amps_ref, coords_ref, weights_ref, modes_ref = local
    n_tile = send_ref.shape[0] // 2
    blocks = block_ref.shape[0]
    cells = cell_ref.shape[1]
    for copy in copies[:2]:
        copy.wait()
    shape = (n_tile, blocks)
    tile_of_row = lax.broadcasted_iota(jnp.int32, shape, 0)
    row = lax.broadcasted_iota(jnp.int32, (blocks, blocks), 0)
    column = lax.broadcasted_iota(jnp.int32, (blocks, blocks), 1)
    before = jnp.where(row < column, 1.0, 0.0).astype(jnp.bfloat16)
    same = jnp.where(row == column, 1.0, 0.0).astype(jnp.bfloat16)
    ones = jnp.ones((blocks, blocks), jnp.bfloat16)
    seen = jnp.zeros(shape, jnp.float32)
    picks = [jnp.zeros(shape, jnp.float32) for _ in range(2)]
    shifts = [jnp.zeros((n_tile, LANES), jnp.float32) for _ in range(2)]
    for k in range(tiles_ref.shape[0]):
        named = jnp.where(tiles_ref[pl.ds(k, 1), :] == tile_of_row, 1.0, 0.0)
        flags = named.astype(jnp.bfloat16)
        rank = seen + jnp.dot(flags, before, preferred_element_type=jnp.float32)
        seen = seen + jnp.dot(flags, ones, preferred_element_type=jnp.float32)
        offsets = [
            jnp.broadcast_to(offsets_ref[c, pl.ds(k, 1), :].astype(jnp.float32), (ATOM_BLOCK, blocks))
            for c in range(3)
        ]
        offsets = jnp.concatenate(offsets + [jnp.zeros((ATOM_BLOCK, blocks), jnp.float32)], axis=0)
        for slot in range(2):
            mine = jnp.where(rank == float(slot), named, 0.0)
            picks[slot] = picks[slot] + mine
            shifts[slot] = shifts[slot] + against_rows(
                mine.astype(jnp.bfloat16), offsets.astype(jnp.bfloat16)
            )
    for copy in copies[2:]:
        copy.wait()
    amps = jnp.broadcast_to(amps_ref[...], (16, amps_ref.shape[1])).astype(jnp.bfloat16)
    for component in range(3):
        moved = jnp.dot(amps, modes_ref[component], preferred_element_type=jnp.float32)
        places = coords_ref[pl.ds(component, 1), :] + moved[0:1]
        for cell in range(cells):
            cell_ref[component, pl.ds(cell, 1), :] = places[:, cell * LANES : (cell + 1) * LANES]
    cell_ref[3] = weights_ref[...]
    for i in range(4):
        block_ref[pl.ds(i, cells, stride=4), :] = regroup([cell_ref[c] for c in range(4)], i)
    parts = exact_parts(block_ref[...])
    picks = [pick.astype(jnp.bfloat16) for pick in picks]
    both = jnp.concatenate(picks, axis=0)
    high, middle, low = [jnp.dot(both, part, preferred_element_type=jnp.float32) for part in parts]
    places = (high + middle) + low
    for slot in range(2):
        rows = places[slot * n_tile : (slot + 1) * n_tile] + shifts[slot]
        steps = jnp.clip(rows - MIDDLE, -SPAN, SPAN) * PLACE_STEPS
        wide_ref[pl.ds(slot, n_tile, stride=2), :] = jnp.where(
            quarter_of(rows.shape) < 3, steps, rows * MASS_STEPS
        )
        pick_ref[slot] = against_rows(same, picks[slot]).astype(jnp.bfloat16)
    send_ref[...] = whole_steps(wide_ref[...])


def finish_kernel(voxels, atoms, back_ref, pick_ref, modes_ref, forces_ref, spread_ref, score_ref, wide_ref, block_ref):
    blocks, n_tile = pick_ref.shape[1:]
    picks = pick_ref[...].reshape(2 * blocks, n_tile)
    wide_ref[...] = back_ref[...].astype(jnp.float32)
    last = wide_ref[pl.ds(3, n_tile, stride=4), :]
    place = lax.broadcasted_iota(jnp.int32, (n_tile, LANES), 1) // 3
    ratio = jnp.sum(jnp.where(place == 3, last, 0.0), axis=1, keepdims=True)
    totals = jnp.sum(last, axis=0, keepdims=True)
    srm, srr, smm = [
        jnp.sum(jnp.where(place[0:1] == i, totals, 0.0), axis=1, keepdims=True) for i in range(3)
    ]
    root = jnp.sqrt(srr * smm)
    score = srm / root
    score_ref[...] = jnp.broadcast_to(score, score_ref.shape)
    map_scale = voxels / root
    model_scale = map_scale * (ratio - srm / srr)
    cells = forces_ref.shape[1] // LANES
    modes = jnp.zeros((1, modes_ref.shape[1]), jnp.float32)
    for component in range(3):
        pulled = wide_ref[pl.ds(component, n_tile, stride=4), :]
        pulled = pulled * map_scale + pltpu.roll(pulled, LANES // 2, 1) * model_scale
        high, low, _ = exact_parts(pulled)
        sums = jnp.dot(picks, low, preferred_element_type=jnp.float32)
        sums = sums + jnp.dot(picks, high, preferred_element_type=jnp.float32)
        block_ref[component] = sums[:blocks] + pltpu.roll(sums[blocks:], LANES - ATOM_BLOCK, 1)
        rows = regroup([block_ref[component, pl.ds(i, cells, stride=4), :] for i in range(4)], 0)
        for cell in range(cells):
            forces_ref[pl.ds(component, 1), cell * LANES : (cell + 1) * LANES] = rows[cell : cell + 1]
        force = jnp.broadcast_to(forces_ref[pl.ds(component, 1), :], (16, forces_ref.shape[1]))
        modes = modes + against_rows(force.astype(jnp.bfloat16), modes_ref[component])[0:1]
    modes = modes / jnp.sqrt(jnp.float32(atoms))
    half = spread_ref.shape[0] // 2
    for part in range(2):
        spread_ref[pl.ds(part, half, stride=2), :] = jnp.broadcast_to(
            modes[:, part * LANES : (part + 1) * LANES], (half, LANES)
        )


def unpack_rows(got_ref, wide_ref, place_ref):
    wide_ref[...] = from_steps(got_ref[...])
    groups = got_ref.shape[0] // 4
    rows = [wide_ref[pl.ds(i, groups, stride=4), :] for i in range(4)]
    for component in range(3):
        place_ref[component] = regroup(rows, component) * (1.0 / PLACE_STEPS) + MIDDLE
    place_ref[3] = regroup(rows, 3) * (1.0 / MASS_STEPS)


def chunk_row(place_ref, component, chunk, size):
    rows = size // LANES
    return jnp.concatenate(
        [place_ref[component, pl.ds(chunk * rows + i, 1), :] for i in range(rows)], axis=1
    )


def pipeline(chunks, build, use, last_apart=True):
    build(0, 0)

    @pl.loop(0, chunks // 2 - last_apart)
    def _(step):
        build(1, 2 * step + 1)
        use(0, 2 * step)
        build(0, 2 * step + 2 if last_apart else jnp.minimum(2 * step + 2, chunks - 2))
        use(1, 2 * step + 1)

    if last_apart:
        build(1, chunks - 1)
        use(0, chunks - 2)
        use(1, chunks - 1)


def pair_of_lines(line_ref, z, size):
    return jnp.concatenate(
        [jnp.broadcast_to(line_ref[pl.ds(z + i, 1), :], (HIGHS, size)) for i in range(2)], axis=0
    )


LOWS = [low + 0.5 - STEP / 2 for low in range(STEP)]


def coarse_of(high):
    return STEP * high.astype(jnp.float32) + (STEP / 2 - MIDDLE)


def own_factor(low, width):
    coarse = coarse_of(lax.broadcasted_iota(jnp.int32, (EDGE, width), 1) % HIGHS)
    return jnp.exp2(-rate * (2.0 * LOWS[low] * coarse + LOWS[low] ** 2))


def splat_kernel(got_ref, out_ref, wide_ref, place_ref, line_ref, even_ref, odd_ref, even_weight_ref, odd_weight_ref, fine_ref, sum_ref):
    size = even_ref.shape[1]
    planes, weights = (even_ref, odd_ref), (even_weight_ref, odd_weight_ref)
    unpack_rows(got_ref, wide_ref, place_ref)
    sum_ref[...] = jnp.zeros_like(sum_ref)

    def build(slot, chunk):
        place_x, place_y, place_z, masses = [chunk_row(place_ref, i, chunk, size) for i in range(4)]
        place_x = place_x - MIDDLE
        along_x = factors(place_x, coarse_of(row_number(HIGHS, size)))[0]
        doubled = jnp.concatenate([along_x, along_x], axis=0).astype(jnp.bfloat16)
        along_z = factors(place_z, centers_of(size))[0]
        line_ref[slot] = along_z.astype(jnp.bfloat16).astype(jnp.float32)
        for z in range(0, EDGE, 2):
            line = pair_of_lines(line_ref.at[slot], z, size).astype(jnp.bfloat16)
            planes[slot][pl.ds(z * HIGHS, 2 * HIGHS), :] = line * doubled
        along_y = (masses * factors(place_y, centers_of(size))[0]).astype(jnp.bfloat16)
        near = jnp.clip(place_x, -SPAN, SPAN)
        lows = row_number(STEP, size).astype(jnp.float32) + LOWS[0]
        fine_ref[slot] = jnp.exp2((2.0 * rate) * lows * near)
        for low in range(STEP):
            fine = jnp.broadcast_to(fine_ref[slot, pl.ds(low, 1), :], (EDGE, size))
            weights[slot][pl.ds(low * EDGE, EDGE), :] = along_y * fine.astype(jnp.bfloat16)

    def use(slot, chunk):
        width = min(WIDTH, size)
        for part in range(size // width):
            atoms = pl.ds(part * width, width)
            sum_ref[part] += against_rows(planes[slot][:, atoms], weights[slot][:, atoms])

    pipeline(place_ref.shape[1] * LANES // size, build, use, last_apart=False)
    total = jnp.sum(sum_ref[...], axis=0).T
    blocks = []
    for low in range(STEP):
        block = total[low * EDGE : (low + 1) * EDGE] * own_factor(low, EDGE * HIGHS)
        blocks += [block[:, i : i + LANES] for i in range(0, block.shape[1], LANES)]
    largest = blocks[0]
    for block in blocks[1:]:
        largest = jnp.maximum(largest, block)
    largest = jnp.max(jnp.max(largest, axis=0, keepdims=True), axis=1, keepdims=True)
    power = jnp.floor(jnp.log(jnp.clip(largest, 1e-30, 1e30)) * (1.0 / math.log(2.0)))
    steps = DENSITY_STEPS * jnp.exp2(-power)
    rows = [whole_steps(block * steps) for block in blocks]
    rows.append(whole_steps(jnp.broadcast_to(power, (POWER_ROWS, LANES))))
    for copy in range(out_ref.shape[0]):
        place = 0
        for block in rows:
            out_ref[copy, pl.ds(place, block.shape[0]), :] = block
            place += block.shape[0]


def density_of(parts_ref, part):
    count = parts_ref.shape[1] - POWER_ROWS
    power = from_steps(parts_ref[part, pl.ds(count, POWER_ROWS), :])[0:1]
    step = jnp.exp2(power) * (1.0 / DENSITY_STEPS)
    blocks = [from_steps(parts_ref[part, pl.ds(i, EDGE), :]) * step for i in range(0, count, EDGE)]
    return jnp.concatenate(blocks, axis=1)


def field_rows(row_ref, field):
    width = EDGE * HIGHS
    for low in range(STEP):
        rows = field[:, low * width : (low + 1) * width] * own_factor(low, width)
        row_ref[low * EDGE : (low + 1) * EDGE] = rows.astype(jnp.bfloat16)


def pull_rows(keep, shape_ref, place_ref, row_ref, sum_ref, line_ref, even_ref, odd_ref, fine_ref):
    planes = (even_ref, odd_ref)
    size = even_ref.shape[2]
    width = min(WIDTH, size)

    def build(slot, chunk):
        place_x, place_y, place_z, masses = [chunk_row(place_ref, i, chunk, size) for i in range(4)]
        place_x = place_x - MIDDLE
        distance = coarse_of(row_number(HIGHS, size)) - place_x
        along_x = jnp.exp2(-rate * (distance * distance))
        near = jnp.clip(place_x, -SPAN, SPAN)
        lows = row_number(STEP, size).astype(jnp.float32) + LOWS[0]
        fine_ref[slot] = jnp.exp2((2.0 * rate) * lows * near)
        if keep:
            for i, values in enumerate(factors(place_z, centers_of(size))):
                shape_ref[chunk, i] = values.astype(jnp.bfloat16)
            for i, values in enumerate(factors(place_y, centers_of(size))):
                shape_ref[chunk, 2 + i] = (masses * values).astype(jnp.bfloat16)
        for i in range(2):
            line_ref[slot, i] = shape_ref[chunk, i].astype(jnp.float32)
        plain = jnp.concatenate([along_x, along_x], axis=0)
        sloped = plain * jnp.concatenate([distance, distance], axis=0)
        for z in range(0, EDGE, 2):
            line = pair_of_lines(line_ref.at[slot, 0], z, size)
            slope_line = pair_of_lines(line_ref.at[slot, 1], z, size)
            place = pl.ds(z * HIGHS, 2 * HIGHS)
            planes[slot][0, place, :] = (line * plain).astype(jnp.bfloat16)
            planes[slot][1, place, :] = (line * sloped).astype(jnp.bfloat16)
            planes[slot][2, place, :] = (slope_line * plain).astype(jnp.bfloat16)

    def use(slot, chunk):
        for part in range(size // width):
            atoms = pl.ds(part * width, width)
            pulled = [
                jnp.dot(row_ref[...], planes[slot][i, :, atoms], preferred_element_type=jnp.float32)
                for i in range(3)
            ]
            fine = [fine_ref[slot, pl.ds(low, 1), atoms] for low in range(STEP)]
            plain, by_x, by_z = [
                [values[low * EDGE : (low + 1) * EDGE] * fine[low] for low in range(STEP)]
                for values in pulled
            ]
            by_low = 1.5 * (plain[3] - plain[0]) + 0.5 * (plain[2] - plain[1])
            sums = [(values[0] + values[1]) + (values[2] + values[3]) for values in (by_x, plain, by_z)]
            sums[0] = sums[0] + by_low
            along_y, slope_y = [shape_ref[chunk, 2 + i, :, atoms].astype(jnp.float32) for i in range(2)]
            rows = width // LANES
            for component, weight in enumerate((inverse_var * along_y, slope_y, along_y)):
                force = jnp.sum(sums[component] * weight, axis=0, keepdims=True)
                for i in range(rows):
                    row = (chunk * (size // width) + part) * rows + i
                    sum_ref[component, pl.ds(row, 1), :] = force[:, i * LANES : (i + 1) * LANES]

    pipeline(place_ref.shape[1] * LANES // size, build, use)


def map_kernel(got_ref, target_ref, sum_ref, place_ref, shape_ref, wide_ref, row_ref, *scratch):
    unpack_rows(got_ref, wide_ref, place_ref)
    field_rows(row_ref, target_ref[...].astype(jnp.float32))
    pull_rows(True, shape_ref, place_ref, row_ref, sum_ref, *scratch)


def pull_kernel(parts_ref, target_ref, map_ref, place_ref, shape_ref, out_ref, row_ref, sum_ref, stage_ref, *scratch):
    parts = [density_of(parts_ref, i) for i in range(4)]
    density = (parts[0] + parts[2]) + (parts[1] + parts[3])
    wide = target_ref[...].astype(jnp.float32)
    totals = [
        jnp.sum(jnp.sum(product, axis=0, keepdims=True), axis=1, keepdims=True)
        for product in (density * wide, density * density, wide * wide)
    ]
    ratio = jnp.where(totals[0] > 0.0, totals[0] / jnp.maximum(totals[1], 1e-30), 1.0)
    field_rows(row_ref, wide - ratio * density)
    pairs = place_ref.shape[1]
    lane = lax.broadcasted_iota(jnp.int32, (8, LANES), 1)
    last = jnp.zeros((8, LANES), jnp.float32)
    for place, value in enumerate(totals + [ratio]):
        for i, term in enumerate(exact_parts(jnp.broadcast_to(value, (8, LANES)))):
            last = jnp.where(lane == 3 * place + i, term.astype(jnp.float32), last)
    stage_ref[pl.ds(3, 2 * pairs, stride=4), :] = jnp.broadcast_to(last[0:1], (2 * pairs, LANES))
    pull_rows(False, shape_ref, place_ref, row_ref, sum_ref, *scratch)
    left = lax.broadcasted_iota(jnp.int32, (pairs, LANES), 1) < LANES // 2
    for component in range(3):
        first = sum_ref[component]
        second = (map_ref[component] - first) / ratio
        stage_ref[pl.ds(component, pairs, stride=8), :] = jnp.where(
            left, first, pltpu.roll(second, LANES // 2, 1)
        )
        stage_ref[pl.ds(4 + component, pairs, stride=8), :] = jnp.where(
            left, pltpu.roll(first, LANES // 2, 1), second
        )
    out_ref[...] = stage_ref[...].astype(jnp.bfloat16)


def call(kernel, name, out_shape, scratch, flops, *operands, source=pltpu.VMEM, limit=32):
    vmem = pl.BlockSpec(memory_space=pltpu.VMEM)
    return pl.pallas_call(
        kernel,
        out_shape=out_shape,
        in_specs=[pl.BlockSpec(memory_space=source)] * len(operands),
        out_specs=jax.tree.map(lambda _: vmem, out_shape),
        scratch_shapes=[pltpu.VMEM(*entry) if isinstance(entry, tuple) else entry for entry in scratch],
        compiler_params=pltpu.CompilerParams(vmem_limit_bytes=limit * 2**20),
        cost_estimate=pl.CostEstimate(flops=flops, bytes_accessed=2**20, transcendentals=2**20),
        name=name,
    )(*operands)


def pack(coords, weights, modes, amplitudes, tiles, offsets, n_tile):
    blocks = tiles.shape[1]
    operands = (tiles, offsets, amplitudes, coords, weights, modes)
    return call(
        pack_kernel,
        "pack",
        (
            pltpu.VMEM((2 * n_tile, LANES), jnp.int16),
            jax.ShapeDtypeStruct((2, blocks, n_tile), jnp.bfloat16),
        ),
        [
            ((4, weights.shape[0], LANES), jnp.float32),
            ((blocks, LANES), jnp.float32),
            ((2 * n_tile, LANES), jnp.float32),
        ]
        + [(operand.shape, operand.dtype) for operand in operands]
        + [pltpu.SemaphoreType.DMA((len(operands),))],
        2**26,
        *operands,
        source=pltpu.HBM,
        limit=56,
    )


def finish(back, picks, modes, voxels, atoms, copies):
    blocks = picks.shape[1]
    return call(
        lambda *refs: finish_kernel(voxels, atoms, *refs),
        "finish",
        (
            jax.ShapeDtypeStruct((3, modes.shape[2]), jnp.float32),
            jax.ShapeDtypeStruct((2 * copies, LANES), jnp.float32),
            jax.ShapeDtypeStruct((1, LANES), jnp.float32),
        ),
        [(back.shape, jnp.float32), ((3, blocks, LANES), jnp.float32)],
        2**26,
        back,
        picks,
        modes,
    )


def splat(got, copies):
    groups = got.shape[0] // 4
    size = min(CHUNK, groups * LANES // 2)
    plane = ((EDGE * HIGHS, size), jnp.bfloat16)
    weight = ((EDGE * STEP, size), jnp.bfloat16)
    return call(
        splat_kernel,
        "splat",
        pltpu.VMEM((copies, EDGE * PLANE // LANES + POWER_ROWS, LANES), jnp.int16),
        [
            ((4 * groups, LANES), jnp.float32), ((4, groups, LANES), jnp.float32),
            ((2, EDGE, size), jnp.float32),
            plane,
            plane,
            weight,
            weight,
            ((2, STEP, size), jnp.float32),
            ((size // min(WIDTH, size), EDGE * HIGHS, EDGE * STEP), jnp.float32),
        ],
        2**29,
        got,
    )


def pull_scratch(groups):
    size = min(CHUNK, groups * LANES // 2)
    plane = ((3, EDGE * HIGHS, size), jnp.bfloat16)
    return [((2, 2, EDGE, size), jnp.float32), plane, plane, ((2, STEP, size), jnp.float32)]


def pull_map(got, target):
    groups = got.shape[0] // 4
    size = min(CHUNK, groups * LANES // 2)
    return call(
        map_kernel,
        "pull_map",
        (
            pltpu.VMEM((3, groups, LANES), jnp.float32),
            pltpu.VMEM((4, groups, LANES), jnp.float32),
            pltpu.VMEM((groups * LANES // size, 4, EDGE, size), jnp.bfloat16),
        ),
        [((4 * groups, LANES), jnp.float32), ((STEP * EDGE, EDGE * HIGHS), jnp.bfloat16)]
        + pull_scratch(groups),
        2**32,
        got,
        target,
    )


def pull(parts, target, from_map):
    groups = from_map[0].shape[1]
    return call(
        pull_kernel,
        "pull",
        jax.ShapeDtypeStruct((8 * groups, LANES), jnp.bfloat16),
        [
            ((STEP * EDGE, EDGE * HIGHS), jnp.bfloat16),
            ((3, groups, LANES), jnp.float32),
            ((8 * groups, LANES), jnp.float32),
        ]
        + pull_scratch(groups),
        2**32,
        parts,
        target,
        *from_map,
    )


TILE_AXES = ("y", "z", "core")


def exchange(values, axes):
    return lax.all_to_all(values, axes, split_axis=0, concat_axis=0, tiled=True)


def on_device(coords, weights, mode_vectors, amplitudes, density_map, block_tiles, block_offsets):
    a_dev = coords.shape[1]
    n_tile = lax.axis_size(TILE_AXES)
    n_seg = lax.axis_size("seg")
    modes = jnp.transpose(mode_vectors, (1, 0, 2))
    send, picks = pack(
        coords,
        weights.reshape(a_dev // LANES, LANES),
        modes,
        amplitudes.reshape(1, -1),
        block_tiles.T,
        jnp.transpose(block_offsets, (2, 1, 0)),
        n_tile,
    )
    got = exchange(send.reshape(n_tile, 2, LANES), TILE_AXES).reshape(2 * n_tile, LANES)
    target = density_map.reshape(EDGE, HIGHS, STEP, EDGE)
    target = jnp.transpose(target, (3, 2, 0, 1)).reshape(EDGE, PLANE)
    parts = exchange(splat(got, n_seg), "seg")
    pulled = pull(parts, target, pull_map(got, target))
    back = exchange(pulled.reshape(n_tile, 4, LANES), TILE_AXES).reshape(4 * n_tile, LANES)
    near, far = ("z", "core"), ("y", "seg")
    forces, spread, score = finish(
        back, picks, modes, float(n_tile * EDGE**3), a_dev * n_tile * n_seg, lax.axis_size(near)
    )
    near_sum = jnp.sum(exchange(spread.reshape(-1, 2, LANES), near), axis=0)
    copies = jnp.broadcast_to(near_sum[None], (lax.axis_size(far), 2, LANES))
    mode_grad = jnp.sum(exchange(copies, far), axis=0).reshape(-1)
    return (forces, mode_grad, score[0, 0])


def solution(mesh):
    split = Mesh(mesh.devices.reshape(8, 8, 2, 4), TILE_AXES + ("seg",))
    every = TILE_AXES + ("seg",)
    return jax.shard_map(
        on_device,
        mesh=split,
        in_specs=(
            P(None, every),
            P(every),
            P(None, None, every),
            P(),
            P(TILE_AXES, None),
            P(every, None),
            P(every, None, None),
        ),
        out_specs=(P(None, every), P(), P()),
        check_vma=False,
    )
```
